32 devices in a mesh: dp: 32 (over z, y, x, core).
Axes of the slice: x: 2, y: 2, z: 4, core: 2. Of those that a mesh axis runs over, the one named last changes fastest.
Arguments:
- embedded: bfloat16 [8192, 768], P('dp'), may hold values from -6 to 6
- doc_ids: int32 [32, 256], P('dp'), may hold values from 0 to 3, never falling along the last dimension, each value on 1 to 170 neighbouring positions
- step_ids: int32 [32, 4], P('dp'), may hold values from 0 to 1023
- step_table: bfloat16 [1024, 768], P('dp'), may hold values from -3 to 3
- qkv_weight: bfloat16 [2, 768, 2304], P(None, 'dp'), may hold values from -0.21875 to 0.21875
- qv_bias: bfloat16 [2, 1536], P(None, 'dp'), may hold values from -3 to 3
- out_weight: bfloat16 [2, 768, 768], P(None, 'dp'), may hold values from -0.625 to 0.625
- out_bias: bfloat16 [2, 768], P(None, 'dp'), may hold values from -2 to 2
- first_gain: bfloat16 [2, 768], P(None, 'dp'), may hold values from 0.5 to 1.5
- first_shift: bfloat16 [2, 768], P(None, 'dp'), may hold values from -2 to 2
- up_weight: bfloat16 [2, 768, 3072], P(None, 'dp'), may hold values from -0.21875 to 0.21875
- up_bias: bfloat16 [2, 3072], P(None, 'dp'), may hold values from -3 to 3
- down_weight: bfloat16 [2, 3072, 768], P(None, 'dp'), may hold values from -0.109375 to 0.109375
- down_bias: bfloat16 [2, 768], P(None, 'dp'), may hold values from -2 to 2
- second_gain: bfloat16 [2, 768], P(None, 'dp'), may hold values from 0.5 to 1.5
- second_shift: bfloat16 [2, 768], P(None, 'dp'), may hold values from -2 to 2
- cotangent: bfloat16 [8192, 768], P('dp'), may hold values from -6 to 6
Outputs:
- block_output: bfloat16 [8192, 768], P('dp')
- input_grad: float32 [8192, 768], P('dp')
- table_grad: float32 [1024, 768], P('dp')
- qkv_weight_grad: float32 [2, 768, 2304], P(None, 'dp')
- qv_bias_grad: float32 [2, 1536], P(None, 'dp')
- out_weight_grad: float32 [2, 768, 768], P(None, 'dp')
- out_bias_grad: float32 [2, 768], P(None, 'dp')
- first_gain_grad: float32 [2, 768], P(None, 'dp')
- first_shift_grad: float32 [2, 768], P(None, 'dp')
- up_weight_grad: float32 [2, 768, 3072], P(None, 'dp')
- up_bias_grad: float32 [2, 3072], P(None, 'dp')
- down_weight_grad: float32 [2, 3072, 768], P(None, 'dp')
- down_bias_grad: float32 [2, 768], P(None, 'dp')
- second_gain_grad: float32 [2, 768], P(None, 'dp')
- second_shift_grad: float32 [2, 768], P(None, 'dp')
The draws below stay inside these ranges and needn't reach their ends.
Inputs may be any that keep to these rules, and one draw needn't show every extreme that they name: `doc_ids`: document numbers never fall along a row of 256 tokens; each of the 4 documents of a row holds 1 to 170 tokens.
All inputs are finite; a program needn't handle non-finite values.
Results may differ from the reference program's by a relative error of at most 0.013.
Values may be sent and summed in bfloat16 or wider, within the bound.
No kernel may reach another device: no remote copies, remote signals or barrier semaphores. Data moves between devices by JAX's collectives and lax.ppermute only.
A program may use at most 256 MiB of HBM per device.

```python
import math
import jax
import jax.numpy as jnp
import numpy as np
from jax import lax

D = 768
HEADS = 12
HEAD_DIM = 64
FF = 3072
LAYERS = 2
TSTEPS = 1024
SEGS = 4
TOK_DEV = 256
DOC_MOST = 170
ROWS = 32
TOKENS = 8192


def plant(entries, own_key, smallest, top_value):
    spot = [jax.random.randint(jax.random.fold_in(own_key, axis), (), 0, length) for axis, length in enumerate(entries.shape)]
    main_axis = entries.shape.index(max(entries.shape))
    next_to = spot[:main_axis] + [(spot[main_axis] + 1) % entries.shape[main_axis]] + spot[main_axis + 1:]
    return entries.at[tuple(spot)].set(smallest).at[tuple(next_to)].set(top_value)


def levels(rng, dims, split, low, high):
    def one(axis_at, parts):
        steps = jax.random.uniform(jax.random.fold_in(jax.random.fold_in(rng, 6), axis_at), (parts,), jnp.float32, low / len(split), high / len(split))
        return jnp.repeat(jnp.exp(steps), dims[axis_at] // parts).reshape((-1,) + (1,) * (len(dims) - axis_at - 1))

    gain = one(*split[0])
    for cut in split[1:]:
        gain = gain * one(*cut)
    return gain


def split_up(number_of, total, bound, skew):
    loads = [(1 << 20) // math.isqrt(rank ** skew) + 1 for rank in range(2, number_of + 1)]
    rest, counts = total - bound - (number_of - 1), [1] * (number_of - 1)
    while rest > 0:
        movable = [i for i in range(number_of - 1) if counts[i] < bound]
        pool, remaining = sum([loads[i] for i in movable]), rest
        for i in movable:
            more = min(bound - counts[i], max(1, remaining * loads[i] // pool), rest)
            counts[i] = counts[i] + more
            rest = rest - more
    return np.array([bound] + counts)


def ragged_sizes(stream_key, count, total, reach, skew):
    if count == 2:
        one = jax.random.randint(stream_key, (), max(1, total - reach), min(reach, total - 1) + 1)
        return jnp.stack([one, total - one])
    sizes = jnp.asarray(split_up(count, total, reach, skew), jnp.int32)
    twos = (count - 1) // 2
    giver, taker = sizes[1:1 + 2 * twos:2], sizes[2:2 + 2 * twos:2]
    margin = jnp.minimum(giver - 1, reach - taker)
    passed = jax.random.randint(jax.random.fold_in(stream_key, 1), (twos,), 0, 1 << 20) % (margin + 1)
    sizes = sizes.at[1:1 + 2 * twos:2].set(giver - passed).at[2:2 + 2 * twos:2].set(taker + passed)
    return sizes[jax.random.permutation(jax.random.fold_in(stream_key, 2), count)]


def normal_values(own_key, dims, deviation, limit, cuts=(), kind=jnp.bfloat16):
    array = deviation * jax.random.normal(own_key, dims, jnp.float32)
    if cuts:
        array = array * levels(own_key, dims, cuts, -0.22, 0.18)
    return jnp.clip(array, -limit, limit).astype(kind)


def setup_inputs(seed: int = 0) -> dict:
    key_list = jax.random.split(jax.random.key(seed), 18)
    return {
        "embedded": normal_values(key_list[0], (TOKENS, D), 1.0, 6.0, ((0, 32),)),
        "doc_ids": jax.vmap(lambda own: jnp.searchsorted(jnp.cumsum(ragged_sizes(own, SEGS, TOK_DEV, DOC_MOST, 0)), jnp.arange(TOK_DEV), side="right"))(jax.random.split(key_list[1], ROWS)).reshape((ROWS, TOK_DEV)).astype(jnp.int32),
        "step_ids": plant(jax.random.randint(key_list[2], (ROWS, SEGS), 0, TSTEPS), jax.random.fold_in(key_list[2], 1), 0, TSTEPS - 1).astype(jnp.int32),
        "step_table": normal_values(key_list[3], (TSTEPS, D), 0.5, 3.0, ((0, 32),)),
        "qkv_weight": normal_values(key_list[4], (LAYERS, D, 3 * D), D ** -0.5, 0.21875, ((1, 32),)),
        "qv_bias": normal_values(key_list[5], (LAYERS, 2 * D), 0.5, 3.0, ((1, 32),)),
        "out_weight": normal_values(key_list[6], (LAYERS, D, D), (D // 8) ** -0.5, 0.625, ((1, 32),)),
        "out_bias": normal_values(key_list[7], (LAYERS, D), 0.3, 2.0, ((1, 32),)),
        "first_gain": jnp.clip(1.0 + 0.1 * jax.random.normal(key_list[8], (LAYERS, D), jnp.float32), 0.5, 1.5).astype(jnp.bfloat16),
        "first_shift": normal_values(key_list[9], (LAYERS, D), 0.3, 2.0, ((1, 32),)),
        "up_weight": normal_values(key_list[10], (LAYERS, D, FF), D ** -0.5, 0.21875, ((1, 32),)),
        "up_bias": normal_values(key_list[11], (LAYERS, FF), 0.5, 3.0, ((1, 32),)),
        "down_weight": normal_values(key_list[12], (LAYERS, FF, D), FF ** -0.5, 0.109375, ((1, 32),)),
        "down_bias": normal_values(key_list[13], (LAYERS, D), 0.3, 2.0, ((1, 32),)),
        "second_gain": jnp.clip(1.0 + 0.1 * jax.random.normal(key_list[14], (LAYERS, D), jnp.float32), 0.5, 1.5).astype(jnp.bfloat16),
        "second_shift": normal_values(key_list[15], (LAYERS, D), 0.3, 2.0, ((1, 32),)),
        "cotangent": normal_values(key_list[16], (TOKENS, D), 1.0, 6.0, ((0, 32),)),
    }


@jax.custom_vjp
def low(v):
    return lax.optimization_barrier(v.astype(jnp.bfloat16)).astype(jnp.float32)

@jax.custom_vjp
def low_back(v):
    return v

def low_keep(v):
    return (low(v), None)

def low_pass(kept, grad):
    return (grad,)

def back_keep(v):
    return (v, None)

def back_low(kept, grad):
    return (low(grad),)
low.defvjp(low_keep, low_pass)
low_back.defvjp(back_keep, back_low)

def norm_rows(hidden, gain_vec, shift_vec):
    average = lax.optimization_barrier(jnp.mean(hidden, axis=-1, keepdims=True))
    centred = hidden - average
    variance = lax.optimization_barrier(jnp.mean(centred * centred, axis=-1, keepdims=True))
    return centred * lax.rsqrt(variance + 1e-05) * gain_vec + shift_vec

def matmul(left, right):
    return jnp.dot(left, right, precision=lax.Precision.HIGHEST)

def attend_row(pair):
    packed, row_docs = pair
    width = packed.shape[1] // 3
    tok_count = packed.shape[0]
    queries = packed[:, :width].reshape(tok_count, HEADS, HEAD_DIM)
    key_rows = packed[:, width:2 * width].reshape(tok_count, HEADS, HEAD_DIM)
    value_rows = packed[:, 2 * width:].reshape(tok_count, HEADS, HEAD_DIM)
    scores = jnp.einsum('qhd,khd->hqk', queries, key_rows, precision=lax.Precision.HIGHEST)
    scores = low_back(scores * (1.0 / math.sqrt(HEAD_DIM)))
    same_doc = row_docs[:, None] == row_docs[None, :]
    masked = jnp.where(same_doc[None], scores, -1e+30)
    top_score = lax.optimization_barrier(jnp.max(masked, axis=-1, keepdims=True))
    expo_rows = jnp.exp(masked - top_score)
    probs = expo_rows / lax.optimization_barrier(jnp.sum(expo_rows, axis=-1, keepdims=True))
    mixed = jnp.einsum('hqk,khd->qhd', low(probs), value_rows, precision=lax.Precision.HIGHEST)
    return low(low_back(mixed.reshape(tok_count, width)))

def forward(embedded, doc_ids, step_ids, step_table, qkv_weight, qv_bias, out_weight, out_bias, first_gain, first_shift, up_weight, up_bias, down_weight, down_bias, second_gain, second_shift):
    row_count = doc_ids.shape[0]
    token_steps = jnp.take_along_axis(step_ids, doc_ids, axis=1).reshape(-1).astype(jnp.int32)
    hidden = embedded + step_table[token_steps]
    width = hidden.shape[1]
    for layer_index in range(LAYERS):
        normed = low(norm_rows(hidden, first_gain[layer_index], first_shift[layer_index]))
        qv_row = qv_bias[layer_index]
        bias_full = jnp.concatenate([qv_row[:width], jnp.zeros((width,), jnp.float32), qv_row[width:]])
        packed = low(low_back(matmul(normed, qkv_weight[layer_index]) + bias_full))
        mixed = lax.map(jax.checkpoint(attend_row), (packed.reshape(row_count, -1, 3 * width), doc_ids))
        branch = low_back(matmul(mixed.reshape(-1, width), out_weight[layer_index]) + out_bias[layer_index])
        hidden = hidden + branch
        normed_b = low(norm_rows(hidden, second_gain[layer_index], second_shift[layer_index]))
        lifted = low_back(matmul(normed_b, up_weight[layer_index]) + up_bias[layer_index])
        activated = low(jax.nn.gelu(lifted, approximate=True))
        branch = low_back(matmul(activated, down_weight[layer_index]) + down_bias[layer_index])
        hidden = hidden + branch
    return hidden

def reference(embedded, doc_ids, step_ids, step_table, qkv_weight, qv_bias, out_weight, out_bias, first_gain, first_shift, up_weight, up_bias, down_weight, down_bias, second_gain, second_shift, cotangent):
    weights = tuple((piece.astype(jnp.float32) for piece in (step_table, qkv_weight, qv_bias, out_weight, out_bias, first_gain, first_shift, up_weight, up_bias, down_weight, down_bias, second_gain, second_shift)))
    group = 1
    while group * 2 <= ROWS and ROWS % (group * 2) == 0 and (group * 2 * TOK_DEV <= 4096):
        group = group * 2
    blocks = ROWS // group
    width = embedded.shape[1]
    emb_groups = embedded.reshape(blocks, group * TOK_DEV, width)
    cot_groups = cotangent.reshape(blocks, group * TOK_DEV, width)
    doc_groups = doc_ids.reshape(blocks, group, TOK_DEV)
    step_groups = step_ids.reshape(blocks, group, step_ids.shape[1])

    def one_group(totals, pieces):
        emb_part, docs_part, steps_part, cot_part = pieces

        def run(emb_float, *params):
            return forward(emb_float, docs_part, steps_part, *params)
        result, pullback = jax.vjp(run, emb_part.astype(jnp.float32), *weights)
        grads = pullback(cot_part.astype(jnp.float32))
        new_totals = jax.tree.map(jnp.add, totals, tuple(grads[1:]))
        return (new_totals, (result.astype(jnp.bfloat16), grads[0]))
    initial = tuple((jnp.zeros_like(piece) for piece in weights))
    totals, (results, in_grads) = lax.scan(one_group, initial, (emb_groups, doc_groups, step_groups, cot_groups))
    block_output = results.reshape(-1, width)
    input_grad = in_grads.reshape(-1, width)
    return (block_output, input_grad, totals[0], totals[1], totals[2], totals[3], totals[4], totals[5], totals[6], totals[7], totals[8], totals[9], totals[10], totals[11], totals[12])
```

```python
import math

import jax
import jax.numpy as jnp
from jax import lax
from jax.experimental import pallas as pl
from jax.experimental.pallas import tpu as pltpu
from jax.sharding import PartitionSpec as P

HEADS = 12
HEAD_DIM = 64
EPSILON = 1e-05
BF = jnp.bfloat16
F32 = jnp.float32

TUNED = 32
CORE, ALONG_X, ALONG_Y, ALONG_Z, MIDDLE = 1, 2, 4, 8, 24
SLAB = 48
HALF = 384
SMALL_SIZES = (48, 24, 24, 24, 96, 24, 24, 24)


def swap(value, stride):
    return lax.ppermute(value, "dp", [(i, i ^ stride) for i in range(TUNED)])


def swap_from(value, stride, zs):
    return lax.ppermute(value, "dp", [(i, i ^ stride) for i in range(TUNED) if i // 8 in zs])


def after(done, waiting):
    return lax.optimization_barrier((done, waiting))


def place():
    index = lax.axis_index("dp")
    return index % 2, index // 2, index // 8


def norm_rows(hidden, gain_vec, shift_vec):
    average = jnp.mean(hidden, axis=-1, keepdims=True)
    centred = hidden - average
    variance = jnp.mean(centred * centred, axis=-1, keepdims=True)
    inverse = lax.rsqrt(variance + EPSILON)
    unit_rows = centred * inverse
    normed = unit_rows * gain_vec.astype(jnp.float32) + shift_vec.astype(jnp.float32)
    return (normed, unit_rows, inverse)


def norm_back(grad_rows, unit_rows, inverse, gain_vec):
    scaled = grad_rows * gain_vec.astype(jnp.float32)
    first_mean = jnp.mean(scaled, axis=-1, keepdims=True)
    second_mean = jnp.mean(scaled * unit_rows, axis=-1, keepdims=True)
    return inverse * (scaled - first_mean - unit_rows * second_mean)


def smooth_gate(lifted):
    return jax.nn.gelu(lifted, approximate=True)


def layer_apply(hidden, params, same_doc):
    qkv_w, qv_b, out_w, out_b, gain_a, shift_a, up_w, up_b, down_w, down_b, gain_b, shift_b = params
    width = out_w.shape[0]
    tok_count = hidden.shape[0]
    scale = 1.0 / math.sqrt(HEAD_DIM)
    normed_a, unit_a, inverse_a = norm_rows(hidden, gain_a, shift_a)
    normed_a = normed_a.astype(jnp.bfloat16)
    qv_float = qv_b.astype(jnp.float32)
    bias_full = jnp.concatenate(
        [qv_float[:width], jnp.zeros((width,), jnp.float32), qv_float[width:]]
    )
    packed = (jnp.dot(normed_a, qkv_w, preferred_element_type=jnp.float32) + bias_full).astype(
        jnp.bfloat16
    )
    queries = packed[:, :width].reshape(tok_count, HEADS, HEAD_DIM)
    key_rows = packed[:, width : 2 * width].reshape(tok_count, HEADS, HEAD_DIM)
    value_rows = packed[:, 2 * width :].reshape(tok_count, HEADS, HEAD_DIM)
    scores = (
        jnp.einsum("qhd,khd->hqk", queries, key_rows, preferred_element_type=jnp.float32) * scale
    )
    masked = jnp.where(same_doc[None], scores, -1e30)
    top_score = jnp.max(masked, axis=-1, keepdims=True)
    expo_rows = jnp.exp(masked - top_score)
    probs = expo_rows / jnp.sum(expo_rows, axis=-1, keepdims=True)
    probs_low = probs.astype(jnp.bfloat16)
    mixed = jnp.einsum("hqk,khd->qhd", probs_low, value_rows, preferred_element_type=jnp.float32)
    mixed = mixed.reshape(tok_count, width).astype(jnp.bfloat16)
    middle = (
        hidden
        + jnp.dot(mixed, out_w, preferred_element_type=jnp.float32)
        + out_b.astype(jnp.float32)
    )
    normed_b, unit_b, inverse_b = norm_rows(middle, gain_b, shift_b)
    normed_b = normed_b.astype(jnp.bfloat16)
    lifted = jnp.dot(normed_b, up_w, preferred_element_type=jnp.float32) + up_b.astype(jnp.float32)
    activated = smooth_gate(lifted).astype(jnp.bfloat16)
    output = (
        middle
        + jnp.dot(activated, down_w, preferred_element_type=jnp.float32)
        + down_b.astype(jnp.float32)
    )
    saved = (
        unit_a,
        inverse_a,
        normed_a,
        queries,
        key_rows,
        value_rows,
        probs,
        probs_low,
        mixed,
        unit_b,
        inverse_b,
        normed_b,
        lifted,
        activated,
    )
    return (output, saved)


def half_sums(rows, grads, core):
    count = grads.shape[1] // 2
    return [
        jnp.einsum(
            "td,te->de",
            rows,
            lax.dynamic_slice_in_dim(grads, side * count, count, 1),
            preferred_element_type=jnp.float32,
        ).astype(BF)
        for side in (core, 1 - core)
    ]


def layer_back(params, saved, grad_top, core):
    qkv_w, qv_b, out_w, out_b, gain_a, shift_a, up_w, up_b, down_w, down_b, gain_b, shift_b = params
    (
        unit_a,
        inverse_a,
        normed_a,
        queries,
        key_rows,
        value_rows,
        probs,
        probs_low,
        mixed,
        unit_b,
        inverse_b,
        normed_b,
        lifted,
        activated,
    ) = saved
    width = out_w.shape[0]
    tok_count = grad_top.shape[0]
    scale = 1.0 / math.sqrt(HEAD_DIM)
    grad_down = grad_top.astype(jnp.bfloat16)
    down_b_grad = jnp.sum(grad_down.astype(jnp.float32), axis=0)
    down_w_grad = [
        part.reshape(16, 4, SLAB, HALF).transpose(0, 2, 1, 3).reshape(width, 4 * HALF)
        for part in half_sums(activated, grad_down, core)
    ]
    grad_act = jnp.einsum("td,fd->tf", grad_down, down_w, preferred_element_type=jnp.float32)
    unused_gate, gate_pull = jax.vjp(smooth_gate, lifted)
    grad_lift = gate_pull(grad_act)[0].astype(jnp.bfloat16)
    up_b_grad = jnp.sum(grad_lift.astype(jnp.float32), axis=0)
    up_w_grad = half_sums(normed_b, grad_lift, core)
    mlp_grads = [jnp.concatenate(pair, axis=1) for pair in zip(up_w_grad, down_w_grad)]
    grad_nb = jnp.einsum("tf,df->td", grad_lift, up_w, preferred_element_type=jnp.float32)
    gain_b_grad = jnp.sum(grad_nb * unit_b, axis=0)
    shift_b_grad = jnp.sum(grad_nb, axis=0)
    grad_mid = grad_top + norm_back(grad_nb, unit_b, inverse_b, gain_b)
    grad_branch = grad_mid.astype(jnp.bfloat16)
    out_b_grad = jnp.sum(grad_branch.astype(jnp.float32), axis=0)
    out_w_grad = half_sums(mixed, grad_branch, core)
    grad_mixed = jnp.einsum("td,ed->te", grad_branch, out_w, preferred_element_type=jnp.float32)
    grad_mixed = grad_mixed.astype(jnp.bfloat16).reshape(tok_count, HEADS, HEAD_DIM)
    grad_probs = jnp.einsum(
        "qhd,khd->hqk", grad_mixed, value_rows, preferred_element_type=jnp.float32
    )
    grad_values = jnp.einsum(
        "hqk,qhd->khd", probs_low, grad_mixed, preferred_element_type=jnp.float32
    )
    grad_scores = probs * (grad_probs - jnp.sum(probs * grad_probs, axis=-1, keepdims=True))
    scores_low = grad_scores.astype(jnp.bfloat16)
    grad_queries = (
        jnp.einsum("hqk,khd->qhd", scores_low, key_rows, preferred_element_type=jnp.float32) * scale
    )
    grad_keys = (
        jnp.einsum("hqk,qhd->khd", scores_low, queries, preferred_element_type=jnp.float32) * scale
    )
    grad_packed = jnp.concatenate(
        [
            grad_queries.reshape(tok_count, width),
            grad_keys.reshape(tok_count, width),
            grad_values.reshape(tok_count, width),
        ],
        axis=1,
    ).astype(jnp.bfloat16)
    packed_sums = jnp.sum(grad_packed.astype(jnp.float32), axis=0)
    qv_b_grad = jnp.concatenate([packed_sums[:width], packed_sums[2 * width :]])
    qkv_w_grad = half_sums(normed_a, grad_packed, core)
    attn_grads = [jnp.concatenate(pair, axis=1) for pair in zip(qkv_w_grad, out_w_grad)]
    grad_na = jnp.einsum("te,de->td", grad_packed, qkv_w, preferred_element_type=jnp.float32)
    gain_a_grad = jnp.sum(grad_na * unit_a, axis=0)
    shift_a_grad = jnp.sum(grad_na, axis=0)
    grad_in = grad_mid + norm_back(grad_na, unit_a, inverse_a, gain_a)
    small_grads = (
        qv_b_grad,
        out_b_grad,
        gain_a_grad,
        shift_a_grad,
        up_b_grad,
        down_b_grad,
        gain_b_grad,
        shift_b_grad,
    )
    return (grad_in, (mlp_grads, attn_grads), small_grads)
def shortened(value):
    return jax.tree.map(lambda a: a.astype(jnp.bfloat16) if a.dtype == jnp.float32 else a, value)


def partner(value, axis, stride):
    return lax.ppermute(value, axis, [(i, i ^ 1 << stride) for i in range(lax.axis_size(axis))])


def halving_sum(members, send_fn):
    levels = lax.axis_size("dp").bit_length() - 1
    position = lax.axis_index("dp")
    current = tuple(members)
    for level in range(levels - 1, -1, -1):
        upper_side = position // (1 << level) % 2 == 1
        kept_list = []
        sent_list = []
        for member in current:
            half = member.shape[0] // 2
            lower_part = member[:half]
            upper_part = member[half:]
            kept_list.append(jnp.where(upper_side, upper_part, lower_part))
            sent_list.append(jnp.where(upper_side, lower_part, upper_part))
        received = send_fn(tuple(sent_list), level)
        current = tuple((kept + came for kept, came in zip(kept_list, received)))
    return current


def plain_back(hidden, params, same_doc, grad_top):
    qkv_w, qv_b, out_w, out_b, gain_a, shift_a, up_w, up_b, down_w, down_b, gain_b, shift_b = params
    unused_output, saved = layer_apply(hidden, params, same_doc)
    (
        unit_a,
        inverse_a,
        normed_a,
        queries,
        key_rows,
        value_rows,
        probs,
        probs_low,
        mixed,
        unit_b,
        inverse_b,
        normed_b,
        lifted,
        activated,
    ) = saved
    width = out_w.shape[0]
    tok_count = hidden.shape[0]
    scale = 1.0 / math.sqrt(HEAD_DIM)
    grad_down = grad_top.astype(jnp.bfloat16)
    down_b_grad = jnp.sum(grad_down.astype(jnp.float32), axis=0)
    down_w_grad = jnp.einsum("tf,td->fd", activated, grad_down, preferred_element_type=jnp.float32)
    grad_act = jnp.einsum("td,fd->tf", grad_down, down_w, preferred_element_type=jnp.float32)
    unused_gate, gate_pull = jax.vjp(smooth_gate, lifted)
    grad_lift = gate_pull(grad_act)[0].astype(jnp.bfloat16)
    up_b_grad = jnp.sum(grad_lift.astype(jnp.float32), axis=0)
    up_w_grad = jnp.einsum("td,tf->df", normed_b, grad_lift, preferred_element_type=jnp.float32)
    grad_nb = jnp.einsum("tf,df->td", grad_lift, up_w, preferred_element_type=jnp.float32)
    gain_b_grad = jnp.sum(grad_nb * unit_b, axis=0)
    shift_b_grad = jnp.sum(grad_nb, axis=0)
    grad_mid = grad_top + norm_back(grad_nb, unit_b, inverse_b, gain_b)
    grad_branch = grad_mid.astype(jnp.bfloat16)
    out_b_grad = jnp.sum(grad_branch.astype(jnp.float32), axis=0)
    out_w_grad = jnp.einsum("te,td->ed", mixed, grad_branch, preferred_element_type=jnp.float32)
    grad_mixed = jnp.einsum("td,ed->te", grad_branch, out_w, preferred_element_type=jnp.float32)
    grad_mixed = grad_mixed.astype(jnp.bfloat16).reshape(tok_count, HEADS, HEAD_DIM)
    grad_probs = jnp.einsum(
        "qhd,khd->hqk", grad_mixed, value_rows, preferred_element_type=jnp.float32
    )
    grad_values = jnp.einsum(
        "hqk,qhd->khd", probs_low, grad_mixed, preferred_element_type=jnp.float32
    )
    grad_scores = probs * (grad_probs - jnp.sum(probs * grad_probs, axis=-1, keepdims=True))
    scores_low = grad_scores.astype(jnp.bfloat16)
    grad_queries = (
        jnp.einsum("hqk,khd->qhd", scores_low, key_rows, preferred_element_type=jnp.float32) * scale
    )
    grad_keys = (
        jnp.einsum("hqk,qhd->khd", scores_low, queries, preferred_element_type=jnp.float32) * scale
    )
    grad_packed = jnp.concatenate(
        [
            grad_queries.reshape(tok_count, width),
            grad_keys.reshape(tok_count, width),
            grad_values.reshape(tok_count, width),
        ],
        axis=1,
    ).astype(jnp.bfloat16)
    packed_sums = jnp.sum(grad_packed.astype(jnp.float32), axis=0)
    qv_b_grad = jnp.concatenate([packed_sums[:width], packed_sums[2 * width :]])
    qkv_w_grad = jnp.einsum("td,te->de", normed_a, grad_packed, preferred_element_type=jnp.float32)
    grad_na = jnp.einsum("te,de->td", grad_packed, qkv_w, preferred_element_type=jnp.float32)
    gain_a_grad = jnp.sum(grad_na * unit_a, axis=0)
    shift_a_grad = jnp.sum(grad_na, axis=0)
    grad_in = grad_mid + norm_back(grad_na, unit_a, inverse_a, gain_a)
    grads = (
        qkv_w_grad,
        qv_b_grad,
        out_w_grad,
        out_b_grad,
        gain_a_grad,
        shift_a_grad,
        up_w_grad,
        up_b_grad,
        down_w_grad,
        down_b_grad,
        gain_b_grad,
        shift_b_grad,
    )
    return (grad_in, grads)


def plain(
    embedded,
    doc_ids,
    step_ids,
    step_table,
    qkv_weight,
    qv_bias,
    out_weight,
    out_bias,
    first_gain,
    first_shift,
    up_weight,
    up_bias,
    down_weight,
    down_bias,
    second_gain,
    second_shift,
    cotangent,
):
    docs_row = doc_ids[0]
    same_doc = docs_row[:, None] == docs_row[None, :]
    doc_count = step_ids.shape[1]
    doc_hot = (docs_row[:, None] == jnp.arange(doc_count, dtype=jnp.int32)[None, :]).astype(
        jnp.float32
    )
    gathered_first = (
        lax.all_gather(qkv_weight[0], "dp", axis=0, tiled=True),
        lax.all_gather(qv_bias[0], "dp", axis=0, tiled=True),
        lax.all_gather(out_weight[0], "dp", axis=0, tiled=True),
        lax.all_gather(out_bias[0], "dp", axis=0, tiled=True),
        lax.all_gather(first_gain[0], "dp", axis=0, tiled=True),
        lax.all_gather(first_shift[0], "dp", axis=0, tiled=True),
        lax.all_gather(up_weight[0], "dp", axis=0, tiled=True),
        lax.all_gather(up_bias[0], "dp", axis=0, tiled=True),
        lax.all_gather(down_weight[0], "dp", axis=0, tiled=True),
        lax.all_gather(down_bias[0], "dp", axis=0, tiled=True),
        lax.all_gather(second_gain[0], "dp", axis=0, tiled=True),
        lax.all_gather(second_shift[0], "dp", axis=0, tiled=True),
        lax.all_gather(step_table, "dp", axis=0, tiled=True),
    )
    params_lower = gathered_first[:12]
    table_whole = gathered_first[12]
    step_hot = step_ids[0][:, None] == jnp.arange(table_whole.shape[0], dtype=jnp.int32)[None, :]
    doc_rows = jnp.dot(
        step_hot.astype(jnp.bfloat16), table_whole, preferred_element_type=jnp.float32
    )
    start = embedded.astype(jnp.float32) + jnp.dot(
        doc_hot, doc_rows, precision=lax.Precision.HIGHEST
    )
    middle_hidden, unused_lower = layer_apply(start, params_lower, same_doc)
    params_upper = (
        lax.all_gather(qkv_weight[1], "dp", axis=0, tiled=True),
        lax.all_gather(qv_bias[1], "dp", axis=0, tiled=True),
        lax.all_gather(out_weight[1], "dp", axis=0, tiled=True),
        lax.all_gather(out_bias[1], "dp", axis=0, tiled=True),
        lax.all_gather(first_gain[1], "dp", axis=0, tiled=True),
        lax.all_gather(first_shift[1], "dp", axis=0, tiled=True),
        lax.all_gather(up_weight[1], "dp", axis=0, tiled=True),
        lax.all_gather(up_bias[1], "dp", axis=0, tiled=True),
        lax.all_gather(down_weight[1], "dp", axis=0, tiled=True),
        lax.all_gather(down_bias[1], "dp", axis=0, tiled=True),
        lax.all_gather(second_gain[1], "dp", axis=0, tiled=True),
        lax.all_gather(second_shift[1], "dp", axis=0, tiled=True),
    )
    final_hidden, unused_upper = layer_apply(middle_hidden, params_upper, same_doc)
    block_output = final_hidden.astype(jnp.bfloat16)

    def weights_for(layer_index):
        return (
            lax.all_gather(qkv_weight[layer_index], "dp", axis=0, tiled=True),
            lax.all_gather(qv_bias[layer_index], "dp", axis=0, tiled=True),
            lax.all_gather(out_weight[layer_index], "dp", axis=0, tiled=True),
            lax.all_gather(out_bias[layer_index], "dp", axis=0, tiled=True),
            lax.all_gather(first_gain[layer_index], "dp", axis=0, tiled=True),
            lax.all_gather(first_shift[layer_index], "dp", axis=0, tiled=True),
            lax.all_gather(up_weight[layer_index], "dp", axis=0, tiled=True),
            lax.all_gather(up_bias[layer_index], "dp", axis=0, tiled=True),
            lax.all_gather(down_weight[layer_index], "dp", axis=0, tiled=True),
            lax.all_gather(down_bias[layer_index], "dp", axis=0, tiled=True),
            lax.all_gather(second_gain[layer_index], "dp", axis=0, tiled=True),
            lax.all_gather(second_shift[layer_index], "dp", axis=0, tiled=True),
        )

    grad_upper_in, upper_grads = plain_back(
        middle_hidden, weights_for(1), same_doc, cotangent.astype(jnp.float32)
    )

    def send_upper(sent, level):
        return jax.tree.map(
            lambda part, own: part.astype(own.dtype), partner(shortened(sent), "dp", level), sent
        )

    upper_shards = halving_sum(upper_grads, send_upper)
    input_grad, lower_grads = plain_back(start, weights_for(0), same_doc, grad_upper_in)
    doc_grads = jnp.einsum("ts,td->sd", doc_hot, input_grad, precision=lax.Precision.HIGHEST)
    table_full_grad = jnp.einsum(
        "sn,sd->nd", step_hot.astype(jnp.float32), doc_grads, precision=lax.Precision.HIGHEST
    )

    def send_lower(sent, level):
        return jax.tree.map(
            lambda part, own: part.astype(own.dtype), partner(shortened(sent), "dp", level), sent
        )

    lower_all = halving_sum(tuple(lower_grads) + (table_full_grad,), send_lower)
    lower_shards = lower_all[:12]
    table_shard = lower_all[12]
    stacked = [jnp.stack([lower_shards[index], upper_shards[index]], axis=0) for index in range(12)]
    return (
        block_output,
        input_grad,
        table_shard,
        stacked[0],
        stacked[1],
        stacked[2],
        stacked[3],
        stacked[4],
        stacked[5],
        stacked[6],
        stacked[7],
        stacked[8],
        stacked[9],
        stacked[10],
        stacked[11],
    )


def is_middle():
    level = lax.axis_index("dp") // 8
    return (level == 1) | (level == 2)


def middle_column(value):
    return value.shape[-1] // 256 * 128


def gather_parts(own):
    middle = is_middle()
    first = swap(own, ALONG_Z)
    third_middle = swap_from(own, MIDDLE, (1, 2))
    second_middle = swap_from(first, MIDDLE, (1, 2))
    second_end = swap_from(third_middle, ALONG_Z, (1, 2))
    third_end = swap_from(second_middle, ALONG_Z, (1, 2))
    levels = [
        own,
        first,
        jnp.where(middle, second_middle, second_end),
        jnp.where(middle, third_middle, third_end),
    ]
    cut = middle_column(own)
    parts = []
    for level in levels:
        by_x = swap(level, ALONG_X)
        by_y = swap(level, ALONG_Y)
        by_both = jnp.concatenate([swap(by_x[:, :cut], ALONG_Y), swap(by_y[:, cut:], ALONG_X)], axis=1)
        parts.append(jnp.stack([level, by_x, by_y, by_both]))
    return parts


def reduce_parts(parts):
    def add(*values):
        return sum(v.astype(F32) for v in values).astype(BF)

    cut = middle_column(parts[0][0])
    levels = [None] * 4
    for distance in (3, 2, 1, 0):
        own, by_x, by_y, by_both = parts[distance]
        back_y = swap(by_both[:, :cut], ALONG_Y)
        back_x = swap(by_both[:, cut:], ALONG_X)
        to_x = jnp.concatenate([add(by_x[:, :cut], back_y), by_x[:, cut:]], axis=1)
        to_y = jnp.concatenate([by_y[:, :cut], add(by_y[:, cut:], back_x)], axis=1)
        levels[distance] = add(own, swap(to_x, ALONG_X), swap(to_y, ALONG_Y))
    own, first, second, third = levels
    end_third = swap_from(third, ALONG_Z, (0, 3))
    end_second = swap_from(second, ALONG_Z, (0, 3))
    across_second = swap_from(add(second, end_third), MIDDLE, (1, 2))
    across_third = swap_from(add(third, end_second), MIDDLE, (1, 2))
    last = swap(add(first, across_second), ALONG_Z)
    return sum(v.astype(F32) for v in (own, across_third, last))


def layout(with_extra):
    names = [("qkv", 1152), ("out", 384), ("up", 1536), ("down", 1536)]
    return names + [("extra", 768)] if with_extra else names


def assemble(mine, other, with_extra):
    names = layout(with_extra)
    shapes = {"qkv": (768, 2304), "out": (768, 768), "up": (768, 3072), "down": (3072, 768), "extra": (768, 1536)}

    def body(*refs):
        sources = refs[:8]
        outputs = refs[8 : 8 + len(names)]
        held = refs[8 + len(names) : 8 + 2 * len(names)]
        targets = dict(zip([name for name, _ in names], held))
        sems, out_sems = refs[-2:]
        index = lax.axis_index("dp")
        core, chip = index % 2, index // 2
        copies = []
        for which in range(8):
            half = core if which < 4 else 1 - core
            for step in range(4):
                there = chip ^ (4 * (which % 4) + step)
                start = 0
                for name, width in names:
                    target = targets[name]
                    if name == "down":
                        for block in range(4):
                            copies.append(
                                (
                                    sources[which].at[step, :, pl.ds(start + block * HALF, HALF)],
                                    target.at[
                                        pl.ds(pl.multiple_of(there * 192 + block * SLAB, SLAB), SLAB),
                                        pl.ds(pl.multiple_of(half * HALF, HALF), HALF),
                                    ],
                                )
                            )
                    else:
                        copies.append(
                            (
                                sources[which].at[step, :, pl.ds(start, width)],
                                target.at[
                                    pl.ds(pl.multiple_of(there * SLAB, SLAB), SLAB),
                                    pl.ds(pl.multiple_of(half * width, 128), width),
                                ],
                            )
                        )
                    start += width
        started = [pltpu.make_async_copy(a, b, sems.at[n]) for n, (a, b) in enumerate(copies)]
        for copy in started:
            copy.start()
        for copy in started:
            copy.wait()
        written = [pltpu.make_async_copy(a, b, out_sems.at[n]) for n, (a, b) in enumerate(zip(held, outputs))]
        for copy in written:
            copy.start()
        for copy in written:
            copy.wait()

    count = 32 * (8 if with_extra else 7)
    return pl.pallas_call(
        body,
        out_shape=[jax.ShapeDtypeStruct(shapes[name], BF) for name, _ in names],
        in_specs=[pl.BlockSpec(memory_space=pl.ANY)] * 8,
        out_specs=[pl.BlockSpec(memory_space=pl.ANY)] * len(names),
        scratch_shapes=[pltpu.VMEM(shapes[name], BF) for name, _ in names]
        + [pltpu.SemaphoreType.DMA((count,)), pltpu.SemaphoreType.DMA((len(names),))],
        compiler_params=pltpu.CompilerParams(vmem_limit_bytes=24 * 2**20),
        cost_estimate=pl.CostEstimate(flops=0, bytes_accessed=2 * 14 * 2**20, transcendentals=0),
    )(*mine, *other)


def chip_share(layer_weights, extra):
    qkv, out, up, down = layer_weights
    core, _, _ = place()

    def halves(half):
        narrow = jnp.concatenate(
            [qkv[:, half * 1152 : half * 1152 + 1152], out[:, half * 384 : half * 384 + 384], up[:, half * 1536 : half * 1536 + 1536]],
            axis=1,
        )
        low = down[:, half * HALF : half * HALF + HALF]
        wide = [low[:SLAB], low[SLAB:]]
        if extra is not None:
            wide.append(extra[:, half * HALF : half * HALF + HALF])
        wide = jnp.concatenate(wide, axis=1)
        return jnp.concatenate([narrow, wide[:24], wide[24:]], axis=1)

    left, right = halves(0), halves(1)
    kept = jnp.where(core == 0, left, right)
    came = swap(jnp.where(core == 0, right, left), CORE)
    lower = jnp.where(core == 0, kept, came)
    upper = jnp.where(core == 0, came, kept)
    wide = (lower.shape[1] - 3072) // 2

    def wide_of(part):
        return jnp.concatenate([part[:, 3072 : 3072 + wide], part[:, 3072 + wide :]], axis=0)

    low_wide, high_wide = wide_of(lower), wide_of(upper)
    columns = [jnp.concatenate([lower[:, :3072], upper[:, :3072]], axis=0), low_wide[:, :768], high_wide[:, :768]]
    if extra is not None:
        columns += [low_wide[:, 768:], high_wide[:, 768:]]
    return jnp.concatenate(columns, axis=1)


def fetch_layer(layer_weights, extra):
    share = chip_share(layer_weights, extra)
    mine = gather_parts(share)
    other = [swap(part, CORE) for part in mine]
    return assemble(mine, other, extra is not None)


def reduce_chunk(kept, sent):
    _, chip, level = place()
    came = swap(sent, CORE)
    columns = kept.shape[1]
    both = [v.reshape(4, 4, SLAB, columns) for v in (kept, came)]
    parts = []
    for distance in range(4):
        planes = [lax.dynamic_index_in_dim(v, level ^ distance, 0, keepdims=False) for v in both]
        part = []
        for step in range(4):
            pair = [lax.dynamic_index_in_dim(v, (chip % 4) ^ step, 0, keepdims=False) for v in planes]
            part.append((pair[0].astype(F32) + pair[1].astype(F32)).astype(BF))
        parts.append(part)
    return reduce_parts(parts)


def split_small(row, layer_count_width):
    pieces = []
    start = 0
    for size in SMALL_SIZES:
        pieces.append(row[:, start : start + size].reshape(-1))
        start += size
    return pieces


def tuned(
    embedded,
    doc_ids,
    step_ids,
    step_table,
    qkv_weight,
    qv_bias,
    out_weight,
    out_bias,
    first_gain,
    first_shift,
    up_weight,
    up_bias,
    down_weight,
    down_bias,
    second_gain,
    second_shift,
    cotangent,
):
    core, chip, level = place()
    docs_row = doc_ids[0]
    same_doc = docs_row[:, None] == docs_row[None, :]
    doc_count = step_ids.shape[1]
    doc_hot = (docs_row[:, None] == jnp.arange(doc_count, dtype=jnp.int32)[None, :]).astype(jnp.float32)
    smalls = (qv_bias, out_bias, first_gain, first_shift, up_bias, down_bias, second_gain, second_shift)
    small_rows = [jnp.pad(jnp.concatenate([v[layer] for v in smalls]), (0, HALF - 288)) for layer in range(2)]
    extra = jnp.concatenate(
        [step_table, jnp.concatenate(small_rows)[None], jnp.zeros((SLAB - 33, 768), BF)], axis=0
    )
    lower_w = fetch_layer((qkv_weight[0], out_weight[0], up_weight[0], down_weight[0]), extra)
    upper_w = fetch_layer((qkv_weight[1], out_weight[1], up_weight[1], down_weight[1]), None)
    extra_all = lower_w[4].reshape(16, SLAB, 2, 2, HALF)
    table_whole = extra_all[:, :32].transpose(0, 3, 1, 2, 4).reshape(1024, 768)
    small_all = extra_all[:, 32].transpose(1, 0, 2, 3).reshape(2, TUNED, HALF)

    def with_smalls(layer, weights):
        qv_b, out_b, gain_a, shift_a, up_b, down_b, gain_b, shift_b = split_small(small_all[layer], HALF)
        qkv_w, out_w, up_w, down_w = weights[:4]
        return (qkv_w, qv_b, out_w, out_b, gain_a, shift_a, up_w, up_b, down_w, down_b, gain_b, shift_b)

    params_lower = with_smalls(0, lower_w)
    params_upper = with_smalls(1, upper_w)
    step_hot = step_ids[0][:, None] == jnp.arange(table_whole.shape[0], dtype=jnp.int32)[None, :]
    doc_rows = jnp.dot(step_hot.astype(BF), table_whole, preferred_element_type=F32)
    start = embedded.astype(F32) + jnp.dot(doc_hot, doc_rows, precision=lax.Precision.HIGHEST)
    middle_hidden, lower_saved = layer_apply(start, params_lower, same_doc)
    final_hidden, upper_saved = layer_apply(middle_hidden, params_upper, same_doc)
    block_output = final_hidden.astype(BF)
    grad_upper_in, upper_grads, upper_small = layer_back(
        params_upper, upper_saved, cotangent.astype(F32), core
    )
    upper_mlp = reduce_chunk(*upper_grads[0])
    upper_attn = reduce_chunk(*upper_grads[1])
    input_grad, lower_grads, lower_small = layer_back(params_lower, lower_saved, grad_upper_in, core)
    lower_mlp = reduce_chunk(*lower_grads[0])
    doc_grads = jnp.einsum("ts,td->sd", doc_hot, input_grad, precision=lax.Precision.HIGHEST)
    table_full = jnp.einsum("sn,sd->nd", step_hot.astype(F32), doc_grads, precision=lax.Precision.HIGHEST)
    table_full = table_full.astype(BF).reshape(16, 2, 32, 2, HALF).transpose(3, 0, 2, 1, 4).reshape(2, 16, 32, 768)

    def small_columns(pieces):
        rows = [p.reshape(TUNED, size) for p, size in zip(pieces, SMALL_SIZES)]
        row = jnp.pad(jnp.concatenate(rows, axis=1), ((0, 0), (0, HALF - 288)))
        return row.astype(BF).reshape(16, 1, 768)

    small_full = jnp.stack([small_columns(lower_small), small_columns(upper_small)])
    extra_grad = jnp.concatenate([table_full, small_full, jnp.zeros((2, 16, SLAB - 33, 768), BF)], axis=2)
    extra_grad = extra_grad.reshape(2, 768, 768)
    extra_kept = lax.dynamic_index_in_dim(extra_grad, core, 0, keepdims=False)
    extra_sent = lax.dynamic_index_in_dim(extra_grad, 1 - core, 0, keepdims=False)
    lower_attn = reduce_chunk(
        jnp.concatenate([lower_grads[1][0], extra_kept], axis=1),
        jnp.concatenate([lower_grads[1][1], extra_sent], axis=1),
    )

    def finish(attn, mlp):
        pieces = [attn[:, :1152], attn[:, 1152:1536], mlp[:, :1536]]
        return jnp.concatenate(pieces, axis=1), mlp[:, 1536:]

    def exchange(narrow, wide):
        mine_n = lax.dynamic_slice_in_dim(narrow, core * 24, 24, 0)
        theirs_n = lax.dynamic_slice_in_dim(narrow, (1 - core) * 24, 24, 0)
        m = wide.shape[1] // 2
        mine_w = lax.dynamic_slice_in_dim(wide, core * m, m, 1)
        theirs_w = lax.dynamic_slice_in_dim(wide, (1 - core) * m, m, 1)
        send = jnp.concatenate([theirs_n, theirs_w[:24], theirs_w[24:]], axis=1).astype(BF)
        came = swap(send, CORE).astype(F32)
        n = narrow.shape[1]
        came_n = came[:, :n]
        came_w = jnp.concatenate([came[:, n : n + m], came[:, n + m :]], axis=0)

        def ordered(mine, other):
            return jnp.where(core == 0, mine, other), jnp.where(core == 0, other, mine)

        return ordered(mine_n, came_n), ordered(mine_w, came_w)

    def natural(attn, mlp, extra_part):
        narrow, wide = finish(attn, mlp)
        if extra_part is not None:
            wide = jnp.concatenate([wide[:, :768], extra_part[:, :HALF], wide[:, 768:], extra_part[:, HALF:]], axis=1)
        (left, right), (wide_left, wide_right) = exchange(narrow, wide)
        qkv = jnp.concatenate([left[:, :1152], right[:, :1152]], axis=1)
        out = jnp.concatenate([left[:, 1152:1536], right[:, 1152:1536]], axis=1)
        up = jnp.concatenate([left[:, 1536:], right[:, 1536:]], axis=1)
        down = jnp.concatenate(
            [
                jnp.concatenate([w[:, :HALF], w[:, HALF:768]], axis=0) for w in (wide_left, wide_right)
            ],
            axis=1,
        )
        if extra_part is None:
            return qkv, out, up, down
        return qkv, out, up, down, wide_left[:, 768:], wide_right[:, 768:]

    upper_out = natural(upper_attn, upper_mlp, None)
    lower_out = natural(lower_attn[:, :1536], lower_mlp, lower_attn[:, 1536:])
    extra_left, extra_right = lower_out[4:]
    table_shard = jnp.concatenate([extra_left[:32], extra_right[:32]], axis=1)
    small_out = jnp.stack([extra_left[32], extra_right[32]])
    pieces = []
    begin = 0
    for size in SMALL_SIZES:
        pieces.append(small_out[:, begin : begin + size])
        begin += size
    qv_g, out_b_g, gain_a_g, shift_a_g, up_b_g, down_b_g, gain_b_g, shift_b_g = pieces
    qkv_g, out_g, up_g, down_g = [jnp.stack([a, b]) for a, b in zip(lower_out[:4], upper_out)]
    return (
        block_output,
        input_grad,
        table_shard,
        qkv_g,
        qv_g,
        out_g,
        out_b_g,
        gain_a_g,
        shift_a_g,
        up_g,
        up_b_g,
        down_g,
        down_b_g,
        gain_b_g,
        shift_b_g,
    )


def solution(mesh):
    local = tuned if mesh.shape["dp"] == TUNED else plain
    in_specs = (
        P("dp", None),
        P("dp", None),
        P("dp", None),
        P("dp", None),
        P(None, "dp", None),
        P(None, "dp"),
        P(None, "dp", None),
        P(None, "dp"),
        P(None, "dp"),
        P(None, "dp"),
        P(None, "dp", None),
        P(None, "dp"),
        P(None, "dp", None),
        P(None, "dp"),
        P(None, "dp"),
        P(None, "dp"),
        P("dp", None),
    )
    out_specs = (
        P("dp", None),
        P("dp", None),
        P("dp", None),
        P(None, "dp", None),
        P(None, "dp"),
        P(None, "dp", None),
        P(None, "dp"),
        P(None, "dp"),
        P(None, "dp"),
        P(None, "dp", None),
        P(None, "dp"),
        P(None, "dp", None),
        P(None, "dp"),
        P(None, "dp"),
        P(None, "dp"),
    )
    return jax.shard_map(local, mesh=mesh, in_specs=in_specs, out_specs=out_specs, check_vma=False)
```

```python
import math

import jax
import jax.numpy as jnp
import numpy as np
from jax import lax
from jax.experimental import pallas as pl
from jax.experimental.pallas import tpu as pltpu
from jax.sharding import PartitionSpec as P

HEADS = 12
HEAD_DIM = 64
EPSILON = 1e-05
BF = jnp.bfloat16
F32 = jnp.float32

TUNED = 32
CORE, ALONG_X, ALONG_Y, ALONG_Z, MIDDLE = 1, 2, 4, 8, 24
SLAB = 48
HALF = 384


def swap(value, stride):
    return lax.ppermute(value, "dp", [(i, i ^ stride) for i in range(TUNED)])


def swap_from(value, stride, zs):
    return lax.ppermute(value, "dp", [(i, i ^ stride) for i in range(TUNED) if i // 8 in zs])


def after(done, waiting):
    return lax.optimization_barrier((done, waiting))


def place():
    index = lax.axis_index("dp")
    return index % 2, index // 2


WIDTH = HEADS * HEAD_DIM
HIDDEN = 4 * WIDTH
PAIR = 2 * HEAD_DIM
ANY = pl.BlockSpec(memory_space=pl.ANY)
WHOLE = pl.BlockSpec(memory_space=pltpu.VMEM)
ATTN = {"qkv": 1152, "out": 384}
MLP = {"up": 1536, "down": 1536}
SHAPES = {"qkv": (768, 2304), "out": (768, 768), "up": (768, 3072), "down": (3072, 768), "extra": (768, 1536)}


SPOTS = {"gain_a": 0, "shift_a": 768, "out_b": 1536, "gain_b": 2304, "shift_b": 3072, "down_b": 3840}
BIAS_AT, UP_AT, ROW_LENGTH = 4608, 6912, 9984


def spot(ref, name):
    return ref[:, SPOTS[name] : SPOTS[name] + WIDTH]


class Part:
    def __init__(self, array, entries, first, own):
        self.array, self.entries, self.first, self.own = array, entries, first, own


def fetch(parts, refs, starts, targets, sems):
    index = lax.axis_index("dp")
    core, chip = index % 2, index // 2
    for part, ref in zip(parts, refs):
        half = core if part.own else 1 - core
        last = part.first + part.array.shape[-1]
        for name, target in targets.items():
            begin = starts[name]
            if name == "down":
                pieces = [(begin + block * HALF, HALF, block) for block in range(4)]
            else:
                pieces = [(begin, target.shape[1] // 2, None)]
            for start, width, block in pieces:
                low, high = max(start, part.first), min(start + width, last)
                if low >= high:
                    continue
                columns = pl.ds(pl.multiple_of(half * width + (low - start), 128), high - low)
                for leading, code in part.entries:
                    there = chip ^ code
                    row = there * SLAB if block is None else there * (4 * SLAB) + block * SLAB
                    pltpu.make_async_copy(
                        ref.at[leading + (slice(None), pl.ds(low - part.first, high - low))],
                        target.at[pl.ds(pl.multiple_of(row, SLAB), SLAB), columns],
                        sems[name],
                    ).start()


NATURAL = {"qkv": 0, "out": 2304, "up": 3072, "down": 6144}


def natural_pieces(array, name, whole):
    if name == "down":
        for block in range(4):
            columns = pl.ds(NATURAL[name] + block * WIDTH, WIDTH)
            yield array.at[:, columns], whole.at[pl.ds(block * WIDTH, WIDTH), :]
    else:
        yield array.at[:, pl.ds(NATURAL[name], whole.shape[1])], whole


def start_fetch(weights, refs, starts, targets, sems):
    if isinstance(weights, list):
        return fetch(weights, refs, starts, targets, sems)
    for name, target in targets.items():
        for piece, place_of in natural_pieces(refs[0], name, target):
            pltpu.make_async_copy(piece, place_of, sems[name]).start()


def arrays_of(weights):
    return [p.array for p in weights] if isinstance(weights, list) else [weights]


def arrived(target, sem):
    pltpu.make_async_copy(target, target, sem).wait()


def dot(left, right, contract):
    return lax.dot_general(left, right, ((contract[:1], contract[1:]), ((), ())), preferred_element_type=F32)


def unit_of(hidden):
    average = jnp.mean(hidden, axis=-1, keepdims=True)
    centred = hidden - average
    inverse = lax.rsqrt(jnp.mean(centred * centred, axis=-1, keepdims=True) + EPSILON)
    return centred * inverse, inverse


def back_of_norm(grad_rows, unit_rows, inverse, gain):
    scaled = grad_rows * gain
    first_mean = jnp.mean(scaled, axis=-1, keepdims=True)
    second_mean = jnp.mean(scaled * unit_rows, axis=-1, keepdims=True)
    return inverse * (scaled - first_mean - unit_rows * second_mean)


def gelu_pair(value):
    factor = math.sqrt(2.0 / math.pi)
    square = value * value
    bend = jnp.tanh(factor * value * (1.0 + 0.044715 * square))
    half_up = 0.5 * (1.0 + bend)
    slope = half_up + 0.5 * value * (1.0 - bend * bend) * factor * (1.0 + 3.0 * 0.044715 * square)
    return value * half_up, slope


def softmax_rows(query, keys, same):
    scores = dot(query, keys, (1, 1)) * (1.0 / math.sqrt(HEAD_DIM))
    masked = jnp.where(same, scores, -1e30)
    expo = jnp.exp(masked - jnp.max(masked, axis=-1, keepdims=True))
    return expo / jnp.sum(expo, axis=-1, keepdims=True)


def head_lanes(count):
    return lax.broadcasted_iota(jnp.int32, (count, PAIR), 1) < HEAD_DIM


def pair_slice(pair, block):
    return pl.ds(pl.multiple_of(block * WIDTH + pair * PAIR, PAIR), PAIR)


def attn_forward(hidden, row, docs, weights, starts):
    arrays = arrays_of(weights)
    tokens = hidden.shape[0]

    def body(hidden_ref, row_ref, down_docs, across_docs, *rest):
        refs, rest = rest[: len(arrays)], rest[len(arrays) :]
        packed_ref, mixed_ref, middle_ref, qkv_ref, out_ref, sems = rest
        targets = {"qkv": qkv_ref, "out": out_ref}
        named = {"qkv": sems.at[0], "out": sems.at[1]}
        start_fetch(weights, refs, starts, targets, named)
        unit, _ = unit_of(hidden_ref[...])
        normed = (unit * spot(row_ref, "gain_a") + spot(row_ref, "shift_a")).astype(BF)
        arrived(qkv_ref, named["qkv"])
        for block in range(3):
            columns = slice(block * WIDTH, (block + 1) * WIDTH)
            packed_ref[:, columns] = (
                dot(normed, qkv_ref[:, columns], (1, 0))
                + row_ref[:, BIAS_AT + block * WIDTH : BIAS_AT + (block + 1) * WIDTH]
            ).astype(BF)
        same = down_docs[...] == across_docs[...]
        first_head = head_lanes(tokens)

        def one_pair(pair, carry):
            query = packed_ref[:, pair_slice(pair, 0)]
            keys = packed_ref[:, pair_slice(pair, 1)]
            values = packed_ref[:, pair_slice(pair, 2)]
            blank = jnp.zeros_like(query)
            mixes = []
            for own in (jnp.where(first_head, query, blank), jnp.where(first_head, blank, query)):
                mixes.append(dot(softmax_rows(own, keys, same).astype(BF), values, (1, 0)))
            mixed_ref[:, pair_slice(pair, 0)] = jnp.where(first_head, mixes[0], mixes[1]).astype(BF)
            return carry

        lax.fori_loop(0, HEADS // 2, one_pair, 0)
        arrived(out_ref, named["out"])
        middle_ref[...] = hidden_ref[...] + dot(mixed_ref[...], out_ref[...], (1, 0)) + spot(row_ref, "out_b")

    return pl.pallas_call(
        body,
        out_shape=[
            jax.ShapeDtypeStruct((tokens, 3 * WIDTH), BF),
            jax.ShapeDtypeStruct((tokens, WIDTH), BF),
            jax.ShapeDtypeStruct((tokens, WIDTH), F32),
        ],
        in_specs=[WHOLE] * 4 + [ANY] * len(arrays),
        out_specs=[WHOLE] * 3,
        scratch_shapes=[pltpu.VMEM(SHAPES["qkv"], BF), pltpu.VMEM(SHAPES["out"], BF), pltpu.SemaphoreType.DMA((2,))],
        compiler_params=pltpu.CompilerParams(vmem_limit_bytes=40 * 2**20),
        cost_estimate=pl.CostEstimate(flops=1, bytes_accessed=1, transcendentals=1),
        name="attn_forward",
    )(hidden, row, docs.reshape(-1, 1), docs.reshape(1, -1), *arrays)


def mlp_forward(middle, row, weights, starts):
    arrays = arrays_of(weights)
    tokens = middle.shape[0]

    def body(middle_ref, row_ref, *rest):
        refs, rest = rest[: len(arrays)], rest[len(arrays) :]
        top_ref, up_ref, down_ref, sems = rest
        named = {"up": sems.at[0], "down": sems.at[1]}
        start_fetch(weights, refs, starts, {"up": up_ref, "down": down_ref}, named)
        unit, _ = unit_of(middle_ref[...])
        normed = (unit * spot(row_ref, "gain_b") + spot(row_ref, "shift_b")).astype(BF)
        total = middle_ref[...] + spot(row_ref, "down_b")
        arrived(up_ref, named["up"])
        arrived(down_ref, named["down"])
        for tile in range(4):
            columns = slice(tile * WIDTH, (tile + 1) * WIDTH)
            lifted = dot(normed, up_ref[:, columns], (1, 0))
            lifted = lifted + row_ref[:, UP_AT + tile * WIDTH : UP_AT + (tile + 1) * WIDTH]
            active, _ = gelu_pair(lifted)
            total = total + dot(active.astype(BF), down_ref[columns, :], (1, 0))
        top_ref[...] = total

    return pl.pallas_call(
        body,
        out_shape=jax.ShapeDtypeStruct((tokens, WIDTH), F32),
        in_specs=[WHOLE] * 2 + [ANY] * len(arrays),
        out_specs=WHOLE,
        scratch_shapes=[pltpu.VMEM(SHAPES["up"], BF), pltpu.VMEM(SHAPES["down"], BF), pltpu.SemaphoreType.DMA((2,))],
        compiler_params=pltpu.CompilerParams(vmem_limit_bytes=40 * 2**20),
        cost_estimate=pl.CostEstimate(flops=1, bytes_accessed=1, transcendentals=1),
        name="mlp_forward",
    )(middle, row, *arrays)


def send_rows(source, rows, columns, targets, half, first, sem):
    index = lax.axis_index("dp")
    core, chip = index % 2, index // 2
    for side, target in enumerate(targets):

        @pl.when(core == half ^ side)
        def _(target=target):
            for there, row in rows:
                pltpu.make_async_copy(
                    source.at[pl.ds(row, SLAB), columns],
                    target.at[chip ^ there, :, pl.ds(first, columns.size)],
                    sem,
                ).start()


def mlp_backward(middle, grad_top, row, weights, starts, with_top):
    natural = not isinstance(weights, list)
    arrays = arrays_of(weights)
    tokens = middle.shape[0]

    def body(middle_ref, grad_ref, row_ref, *rest):
        refs, rest = rest[: len(arrays)], rest[len(arrays) :]
        grads_ref, rest = rest[:2], rest[2:]
        mid_ref, small_ref = rest[:2]
        top_ref = rest[2] if with_top else None
        up_ref, down_ref, up_stage, down_stage, sems = rest[-5:]
        named = {"up": sems.at[0], "down": sems.at[1]}
        tiles = [slice(tile * WIDTH, (tile + 1) * WIDTH) for tile in range(4)]
        start_fetch(weights, refs, starts, {"up": up_ref, "down": down_ref}, named)
        unit, inverse = unit_of(middle_ref[...])
        normed = (unit * spot(row_ref, "gain_b") + spot(row_ref, "shift_b")).astype(BF)
        grad_top_rows = grad_ref[...].astype(F32)
        grad_down = grad_top_rows.astype(BF)
        small_ref[:, HIDDEN : HIDDEN + WIDTH] = jnp.sum(grad_down.astype(F32), axis=0, keepdims=True)
        grad_nb = jnp.zeros((tokens, WIDTH), F32)
        total = middle_ref[...] + spot(row_ref, "down_b") if with_top else None
        arrived(up_ref, named["up"])
        arrived(down_ref, named["down"])
        for tile, columns in enumerate(tiles):
            lifted = dot(normed, up_ref[:, columns], (1, 0))
            lifted = lifted + row_ref[:, UP_AT + tile * WIDTH : UP_AT + (tile + 1) * WIDTH]
            active, slope = gelu_pair(lifted)
            active = active.astype(BF)
            if with_top:
                total = total + dot(active, down_ref[columns, :], (1, 0))
            grad_act = dot(grad_down, down_ref[columns, :], (1, 1))
            grad_lift = (grad_act * slope).astype(BF)
            small_ref[:, columns] = jnp.sum(grad_lift.astype(F32), axis=0, keepdims=True)
            grad_nb = grad_nb + dot(grad_lift, up_ref[:, columns], (1, 1))
            up_stage[:, columns] = dot(normed, grad_lift, (0, 0)).astype(BF)
            down_stage[columns, :] = dot(active, grad_down, (0, 0)).astype(BF)
            send_rows(
                up_stage,
                [(there, there * SLAB) for there in range(16)],
                pl.ds(tile * WIDTH, WIDTH),
                grads_ref,
                tile // 2,
                tile % 2 * WIDTH,
                sems.at[2],
            )
            if natural:
                pieces = [(tile, [(there, tile * WIDTH + there * SLAB) for there in range(16)])]
            else:
                chips = range(4 * tile, 4 * tile + 4)
                pieces = [(b, [(there, there * 4 * SLAB + b * SLAB) for there in chips]) for b in range(4)]
            for half in range(2):
                for block, rows in pieces:
                    send_rows(
                        down_stage,
                        rows,
                        pl.ds(half * HALF, HALF),
                        grads_ref,
                        half,
                        4 * HALF + block * HALF,
                        sems.at[3],
                    )
        if with_top:
            top_ref[...] = total.astype(BF)
        small_ref[:, HIDDEN + WIDTH : HIDDEN + 2 * WIDTH] = jnp.sum(grad_nb * unit, axis=0, keepdims=True)
        small_ref[:, HIDDEN + 2 * WIDTH :] = jnp.sum(grad_nb, axis=0, keepdims=True)
        mid_ref[...] = grad_top_rows + back_of_norm(grad_nb, unit, inverse, spot(row_ref, "gain_b"))
        arrived(up_stage, sems.at[2])
        arrived(down_stage, sems.at[3])

    sums = [(16, SLAB, HIDDEN)] * 2
    outs = [jax.ShapeDtypeStruct(shape, BF) for shape in sums] + [
        jax.ShapeDtypeStruct((tokens, WIDTH), F32),
        jax.ShapeDtypeStruct((1, HIDDEN + 3 * WIDTH), F32),
    ]
    if with_top:
        outs.append(jax.ShapeDtypeStruct((tokens, WIDTH), BF))
    return pl.pallas_call(
        body,
        out_shape=outs,
        in_specs=[WHOLE] * 3 + [ANY] * len(arrays),
        out_specs=[ANY] * len(sums) + [WHOLE] * (len(outs) - len(sums)),
        scratch_shapes=[pltpu.VMEM(SHAPES["up"], BF), pltpu.VMEM(SHAPES["down"], BF)] * 2
        + [pltpu.SemaphoreType.DMA((4,))],
        compiler_params=pltpu.CompilerParams(vmem_limit_bytes=50 * 2**20),
        cost_estimate=pl.CostEstimate(flops=1, bytes_accessed=1, transcendentals=1),
        name="mlp_backward",
    )(middle, grad_top, row, *arrays)


def attn_backward(hidden, grad_mid, packed, mixed, row, docs, weights, starts, steps):
    arrays = arrays_of(weights)
    tokens = hidden.shape[0]
    scale = 1.0 / math.sqrt(HEAD_DIM)

    def body(hidden_ref, mid_ref, packed_ref, mixed_ref, row_ref, down_docs, across_docs, *rest):
        if steps is not None:
            steps_ref, rest = rest[0], rest[1:]
        refs, rest = rest[: len(arrays)], rest[len(arrays) :]
        grads_ref, rest = rest[:2], rest[2:]
        in_ref, small_ref = rest[:2]
        qkv_ref, out_ref, qkv_stage, out_stage, gm_ref, gp_ref, sems = rest[2:9]
        named = {"qkv": sems.at[0], "out": sems.at[1]}
        start_fetch(weights, refs, starts, {"qkv": qkv_ref, "out": out_ref}, named)
        unit, inverse = unit_of(hidden_ref[...])
        normed = (unit * spot(row_ref, "gain_a") + spot(row_ref, "shift_a")).astype(BF)
        grad_branch = mid_ref[...].astype(BF)
        small_ref[:, 2 * WIDTH : 3 * WIDTH] = jnp.sum(grad_branch.astype(F32), axis=0, keepdims=True)
        out_stage[...] = dot(mixed_ref[...], grad_branch, (0, 0)).astype(BF)
        chips = [(there, there * SLAB) for there in range(16)]
        for half in range(2):
            send_rows(out_stage, chips, pl.ds(half * HALF, HALF), grads_ref, half, 3 * HALF, sems.at[2])
        arrived(out_ref, named["out"])
        gm_ref[...] = dot(grad_branch, out_ref[...], (1, 1)).astype(BF)
        same = down_docs[...] == across_docs[...]
        first_head = head_lanes(tokens)

        def one_pair(pair, carry):
            query = packed_ref[:, pair_slice(pair, 0)]
            keys = packed_ref[:, pair_slice(pair, 1)]
            values = packed_ref[:, pair_slice(pair, 2)]
            grad_mixed = gm_ref[:, pair_slice(pair, 0)]
            blank = jnp.zeros_like(query)
            results = []
            for head in range(2):
                lanes = first_head if head == 0 else jnp.logical_not(first_head)
                probs = softmax_rows(jnp.where(lanes, query, blank), keys, same)
                low = probs.astype(BF)
                grad_probs = dot(jnp.where(lanes, grad_mixed, blank), values, (1, 1))
                grad_scores = probs * (grad_probs - jnp.sum(probs * grad_probs, axis=-1, keepdims=True))
                scores_low = grad_scores.astype(BF)
                results.append(
                    (
                        dot(scores_low, keys, (1, 0)) * scale,
                        dot(scores_low, query, (0, 0)) * scale,
                        dot(low, grad_mixed, (0, 0)),
                    )
                )
            for block in range(3):
                gp_ref[:, pair_slice(pair, block)] = jnp.where(
                    first_head, results[0][block], results[1][block]
                ).astype(BF)
            return carry

        lax.fori_loop(0, HEADS // 2, one_pair, 0)
        arrived(qkv_ref, named["qkv"])
        grad_na = jnp.zeros((tokens, WIDTH), F32)
        for block in range(3):
            columns = slice(block * WIDTH, (block + 1) * WIDTH)
            piece = gp_ref[:, columns]
            sums = jnp.sum(piece.astype(F32), axis=0, keepdims=True)
            if block != 1:
                small_ref[:, block // 2 * WIDTH : (block // 2 + 1) * WIDTH] = sums
            qkv_stage[:, columns] = dot(normed, piece, (0, 0)).astype(BF)
            grad_na = grad_na + dot(piece, qkv_ref[:, columns], (1, 1))
        for half in range(2):
            send_rows(qkv_stage, chips, pl.ds(half * 3 * HALF, 3 * HALF), grads_ref, half, 0, sems.at[3])
        small_ref[:, 3 * WIDTH : 4 * WIDTH] = jnp.sum(grad_na * unit, axis=0, keepdims=True)
        small_ref[:, 4 * WIDTH :] = jnp.sum(grad_na, axis=0, keepdims=True)
        grad_in = mid_ref[...] + back_of_norm(grad_na, unit, inverse, spot(row_ref, "gain_a"))
        in_ref[...] = grad_in
        if steps is not None:
            sums_ref, table_stages = rest[9], rest[10:]
            index = lax.axis_index("dp")
            core, chip = index % 2, index // 2
            for doc in range(8):
                sums_ref[doc : doc + 1, :] = (
                    jnp.sum(jnp.where(down_docs[...] == doc, grad_in, 0.0), axis=0, keepdims=True)
                    if doc < steps.shape[1]
                    else jnp.zeros((1, WIDTH), F32)
                )
            spots = [lax.broadcasted_iota(jnp.int32, (16, SLAB, 8), axis) for axis in range(2)]
            for side, half in enumerate((core, 1 - core)):
                sums = sums_ref[:, pl.ds(pl.multiple_of(half * HALF, HALF), HALF)].astype(BF)
                for owner in range(2):
                    line = ((chip ^ spots[0]) * 2 + owner) * 32 + spots[1]
                    line = jnp.where(spots[1] < 32, line, -1)
                    hot = jnp.where(line == steps_ref[...][None], 1.0, 0.0).reshape(16 * SLAB, 8).astype(BF)
                    block = dot(hot, sums, (1, 0)).astype(BF).reshape(16, SLAB, HALF)
                    stage = table_stages[side]
                    stage[:, :, owner * HALF : (owner + 1) * HALF] = block
                pltpu.make_async_copy(
                    table_stages[side], grads_ref[side].at[:, :, pl.ds(1536, 2 * HALF)], sems.at[4 + side]
                ).start()
            for side in range(2):
                arrived(table_stages[side], sems.at[4 + side])
        arrived(out_stage, sems.at[2])
        arrived(qkv_stage, sems.at[3])

    sums = [(16, SLAB, 1536 if steps is None else 2304)] * 2
    outs = [jax.ShapeDtypeStruct(shape, BF) for shape in sums] + [
        jax.ShapeDtypeStruct((tokens, WIDTH), F32),
        jax.ShapeDtypeStruct((1, 5 * WIDTH), F32),
    ]
    operands = [hidden, grad_mid, packed, mixed, row, docs.reshape(-1, 1), docs.reshape(1, -1)]
    scratch = [pltpu.VMEM(SHAPES["qkv"], BF), pltpu.VMEM(SHAPES["out"], BF)] * 2 + [
        pltpu.VMEM((tokens, WIDTH), BF),
        pltpu.VMEM((tokens, 3 * WIDTH), BF),
        pltpu.SemaphoreType.DMA((6,)),
    ]
    if steps is not None:
        operands.append(jnp.pad(steps, ((0, 0), (0, 8 - steps.shape[1])), constant_values=-2))
        scratch += [pltpu.VMEM((8, WIDTH), F32)] + [pltpu.VMEM((16, SLAB, 2 * HALF), BF)] * 2
    return pl.pallas_call(
        body,
        out_shape=outs,
        in_specs=[WHOLE] * len(operands) + [ANY] * len(arrays),
        out_specs=[ANY] * len(sums) + [WHOLE] * (len(outs) - len(sums)),
        scratch_shapes=scratch,
        compiler_params=pltpu.CompilerParams(vmem_limit_bytes=50 * 2**20),
        cost_estimate=pl.CostEstimate(flops=1, bytes_accessed=1, transcendentals=1),
        name="attn_backward",
    )(*operands, *arrays)


def lay_extra(parts, first):
    def body(*rest):
        refs, (extra_ref, sems) = rest[: len(parts)], rest[len(parts) :]
        named = {"extra": sems.at[0]}
        fetch(parts, refs, {"extra": first}, {"extra": extra_ref}, named)
        arrived(extra_ref, named["extra"])

    return pl.pallas_call(
        body,
        out_shape=jax.ShapeDtypeStruct(SHAPES["extra"], BF),
        in_specs=[ANY] * len(parts),
        out_specs=WHOLE,
        scratch_shapes=[pltpu.SemaphoreType.DMA((1,))],
        compiler_params=pltpu.CompilerParams(vmem_limit_bytes=16 * 2**20),
        cost_estimate=pl.CostEstimate(flops=1, bytes_accessed=1, transcendentals=1),
        name="lay_extra",
    )(*[p.array for p in parts])


def is_middle():
    level = lax.axis_index("dp") // 8
    return (level == 1) | (level == 2)


def cut_of(value):
    return value.shape[-1] // 256 * 128


def chip_share(layer_weights, extra):
    core, _ = place()
    down = layer_weights.get("down")

    def halves(half):
        def columns(value):
            width = value.shape[1] // 2
            return value[:, half * width : half * width + width]

        narrow = [columns(layer_weights[name]) for name in ("qkv", "out", "up") if name in layer_weights]
        wide = []
        if down is not None:
            wide += [columns(down)[:SLAB], columns(down)[SLAB:]]
        if extra is not None:
            wide.append(columns(extra))
        parts = narrow
        if wide:
            wide = jnp.concatenate(wide, axis=1)
            parts = parts + [wide[:24], wide[24:]]
        return jnp.concatenate(parts, axis=1), sum(v.shape[1] for v in narrow)

    (left, count), (right, _) = halves(0), halves(1)
    kept = jnp.where(core == 0, left, right)
    came = swap(jnp.where(core == 0, right, left), CORE)
    lower = jnp.where(core == 0, kept, came)
    upper = jnp.where(core == 0, came, kept)
    columns = [jnp.concatenate([lower[:, :count], upper[:, :count]], axis=0)]
    wide = (lower.shape[1] - count) // 2
    if wide:
        low, high = [
            jnp.concatenate([v[:, count : count + wide], v[:, count + wide :]], axis=0) for v in (lower, upper)
        ]
        if down is not None:
            columns += [low[:, : 2 * HALF], high[:, : 2 * HALF]]
        if extra is not None:
            columns += [low[:, wide - HALF :], high[:, wide - HALF :]]
    return jnp.concatenate(columns, axis=1)


def line_second(first, third_middle):
    return swap_from(first, MIDDLE, (1, 2)), swap_from(third_middle, ALONG_Z, (1, 2))


def line_third(second_middle):
    return swap_from(second_middle, ALONG_Z, (1, 2))


def line_first(own):
    return swap(own, ALONG_Z), swap_from(own, MIDDLE, (1, 2))


def by_place(middle, end):
    return jnp.where(is_middle(), middle, end)


def along_each(to_x, to_y):
    return swap(to_x, ALONG_X), swap(to_y, ALONG_Y)


def diagonal(by_x, by_y):
    cut = cut_of(by_x)
    return swap(by_x[..., :cut], ALONG_Y), swap(by_y[..., cut:], ALONG_X)


def with_other_core(own, by_x, by_y, low, high, distances, first):
    sides = jnp.stack([own, by_x, by_y])
    across = jnp.concatenate([low, high], axis=-1)
    parts = []
    for array, steps in ((sides, (0, 1, 2)), (across, (3,))):
        if len(steps) > 1:
            entries = [((n, k), 4 * d + step) for n, step in enumerate(steps) for k, d in enumerate(distances)]
        else:
            entries = [((k,), 4 * d + 3) for k, d in enumerate(distances)]
        parts.append(Part(array, entries, first, True))
        parts.append(Part(swap(array, CORE), entries, first, False))
    return parts


def direct_line(levels):
    return [swap(levels[k], ALONG_Z * k) for k in (1, 2, 3)]


def total(*values):
    return sum(v.astype(F32) for v in values)


class PlaneSums:
    def __init__(self, *pairs):
        self.pairs = [[v.reshape(4, 4, SLAB, v.shape[-1]) for v in pair] for pair in pairs]
        self.columns = sum(pair[0].shape[-1] for pair in pairs)
        self.cut = self.columns // 256 * 128

    def pair(self, step, first=0, last=None):
        last = self.columns if last is None else last
        pieces = []
        begin = 0
        for pair in self.pairs:
            end = begin + pair[0].shape[-1]
            low, high = max(first, begin) - begin, min(last, end) - begin
            if low < high:
                pieces.append(total(*[v[:, step, :, low:high] for v in pair]))
            begin = end
        return pieces[0] if len(pieces) == 1 else jnp.concatenate(pieces, axis=-1)

    def diagonals(self):
        return self.pair(3, 0, self.cut).astype(BF), self.pair(3, self.cut).astype(BF)

    def sides(self, low, high):
        room = [(0, 0)] * 2
        low = jnp.pad(low, room + [(0, self.columns - self.cut)])
        high = jnp.pad(high, room + [(self.cut, 0)])
        return (self.pair(1) + low.astype(F32)).astype(BF), (self.pair(2) + high.astype(F32)).astype(BF)

    def levels(self, by_x, by_y):
        return (self.pair(0) + total(by_x, by_y)).astype(BF)


def by_half(core, mine, other, axis):
    return jnp.where(
        core == 0, jnp.concatenate([mine, other], axis=axis), jnp.concatenate([other, mine], axis=axis)
    )


def own_rows(names, share):
    core, _ = place()
    widths = {"qkv": 1152, "out": 384, "up": 1536, "down": 1536, "down_by_core": 1536, "extra": 768}
    pieces = []
    start = 0
    for name in names:
        piece = share[:, start : start + widths[name]]
        start += widths[name]
        if name in ("down", "extra"):
            m = widths[name] // 2
            mine, theirs = [lax.dynamic_slice_in_dim(piece, side * m, m, 1) for side in (core, 1 - core)]
            if name == "down":
                mine, theirs = [jnp.concatenate([v[:, :HALF], v[:, HALF:]], axis=0) for v in (mine, theirs)]
        else:
            mine, theirs = [lax.dynamic_slice_in_dim(piece, side * 24, 24, 0) for side in (core, 1 - core)]
        pieces.append((mine, theirs))
    sizes = [theirs.shape for _, theirs in pieces]
    packed = jnp.concatenate([theirs.astype(BF).reshape(24, -1) for _, theirs in pieces], axis=1)
    came = swap(packed, CORE)
    outs = []
    start = 0
    for (mine, _), (rows, columns) in zip(pieces, sizes):
        count = rows * columns // 24
        other = came[:, start : start + count].reshape(rows, columns).astype(F32)
        start += count
        outs.append((mine, other))
    for n, name in enumerate(names):
        if name == "down_by_core":
            outs[n] = [jnp.concatenate(jnp.split(v, 4, axis=1), axis=0) for v in outs[n]]
    return [by_half(core, mine, other, 1) for mine, other in outs]


def small_maps(layer):
    device = np.full(ROW_LENGTH, -1, np.int32)
    inner = np.full(ROW_LENGTH, -1, np.int32)

    def put(at, count, each, begin):
        spots = np.arange(count)
        device[at : at + count] = spots // each
        inner[at : at + count] = begin + spots % each

    for n, name in enumerate(WIDE_SMALLS):
        put(SPOTS[name], WIDTH, 24, 24 * n)
    put(BIAS_AT, 2 * WIDTH, 48, 144)
    for array in (device, inner):
        array[BIAS_AT + 2 * WIDTH : BIAS_AT + 3 * WIDTH] = array[BIAS_AT + WIDTH : BIAS_AT + 2 * WIDTH]
        array[BIAS_AT + WIDTH : BIAS_AT + 2 * WIDTH] = -1
    put(UP_AT, HIDDEN, 96, 192)
    if layer == 1:
        block, there, at = np.unravel_index(np.arange(HIDDEN), (4, TUNED, 24))
        device[UP_AT:], inner[UP_AT:] = there, 192 + 24 * block + at
    return device, inner


WIDE_SMALLS = ("out_b", "gain_a", "shift_a", "down_b", "gain_b", "shift_b")
GRAD_ORDER = ("up", "down_b", "gain_b", "shift_b", "query", "value", "out_b", "gain_a", "shift_a")


def grad_maps(layer):
    device, inner = small_maps(layer)
    pieces = {"up": (UP_AT, HIDDEN), "query": (BIAS_AT, WIDTH), "value": (BIAS_AT + 2 * WIDTH, WIDTH)}
    pieces.update({name: (at, WIDTH) for name, at in SPOTS.items()})
    order = np.concatenate([np.arange(at, at + count) for at, count in (pieces[name] for name in GRAD_ORDER)])
    return device[order], inner[order]


def spread_smalls(gathered, layer):
    device, inner = small_maps(layer)
    hot = (jnp.arange(HALF, dtype=jnp.int32)[:, None] == inner[None, :]).astype(BF)
    wide = jnp.dot(gathered, hot, preferred_element_type=F32)
    mine = jnp.arange(TUNED, dtype=jnp.int32)[:, None] == device[None, :]
    return jnp.sum(jnp.where(mine, wide, 0.0), axis=0, keepdims=True)


def collect_smalls(row, layer):
    device, inner = grad_maps(layer)
    mine = jnp.arange(TUNED, dtype=jnp.int32)[:, None] == device[None, :]
    masked = jnp.where(mine, row.astype(BF), jnp.zeros((), BF))
    hot = (inner[:, None] == jnp.arange(HALF, dtype=jnp.int32)[None, :]).astype(BF)
    return jnp.dot(masked, hot, preferred_element_type=F32).astype(BF)


gate = lax.optimization_barrier


def tuned(
    embedded,
    doc_ids,
    step_ids,
    step_table,
    qkv_weight,
    qv_bias,
    out_weight,
    out_bias,
    first_gain,
    first_shift,
    up_weight,
    up_bias,
    down_weight,
    down_bias,
    second_gain,
    second_shift,
    cotangent,
):
    core, chip = place()
    docs = doc_ids[0]
    doc_count = step_ids.shape[1]
    steps = step_ids[0]
    smalls = (out_bias, first_gain, first_shift, down_bias, second_gain, second_shift, qv_bias, up_bias)
    small_rows = jnp.pad(jnp.concatenate(smalls, axis=1), ((0, 0), (0, HALF - 288))).reshape(1, 2 * HALF)
    extra = jnp.concatenate([step_table, jnp.pad(small_rows, ((0, 15), (0, 0)))], axis=0)
    down_blocks = [down_weight[1][24 * b : 24 * b + 24] for b in range(4)]
    up_order = up_weight[1].reshape(24, TUNED, 4, 24).transpose(0, 2, 1, 3).reshape(24, HIDDEN)
    upper_share = jnp.concatenate([qkv_weight[1], out_weight[1], up_order] + down_blocks, axis=1)
    lower_share = chip_share(
        {"qkv": qkv_weight[0], "out": out_weight[0], "up": up_weight[0], "down": down_weight[0]}, extra
    )
    starts = {"qkv": 0, "out": 1152, "up": 1536, "down": 3072, "extra": 4608}
    upper = lax.all_gather(upper_share, "dp", axis=0, tiled=True)

    block1, block3_middle = line_first(lower_share)
    second_middle, second_end = line_second(block1, block3_middle)
    third_end = line_third(second_middle)
    blocks = [lower_share, block1, by_place(second_middle, second_end), by_place(block3_middle, third_end)]
    parts = []
    for distance, block in enumerate(blocks):
        by_x, by_y = along_each(block, block)
        plane = jnp.stack([block, by_x, by_y, jnp.concatenate(diagonal(by_x, by_y), axis=1)])
        entries = [((step,), 4 * distance + step) for step in range(4)]
        parts += [Part(plane, entries, 0, True), Part(swap(plane, CORE), entries, 0, False)]

    all_extra = lay_extra(parts, starts["extra"])
    small_all = all_extra[32::SLAB].reshape(16, 2, 2, HALF).transpose(1, 0, 2, 3).reshape(2, TUNED, HALF)
    rows = [spread_smalls(small_all[layer], layer) for layer in range(2)]
    owner = steps // 32
    row_of = (owner // 2) * SLAB + steps % 32
    row_hot = (row_of[:, None] == jnp.arange(16 * SLAB, dtype=jnp.int32)[None, :]).astype(BF)
    both_rows = jnp.dot(row_hot, all_extra, preferred_element_type=F32).reshape(doc_count, 2, 2, HALF)
    doc_rows = jnp.where((owner % 2 == 0)[:, None, None], both_rows[:, :, 0], both_rows[:, :, 1])
    doc_rows = doc_rows.reshape(doc_count, WIDTH)
    of_doc = [(docs == s)[:, None] for s in range(doc_count)]
    start = embedded.astype(F32) + sum(jnp.where(of_doc[s], doc_rows[s][None], 0.0) for s in range(doc_count))

    packed0, mixed0, middle0 = attn_forward(start, rows[0], docs, parts, starts)
    between = mlp_forward(middle0, rows[0], parts, starts)
    packed1, mixed1, middle1 = attn_forward(between, rows[1], docs, upper, None)

    kept_m, sent_m, mid1, small_mlp1, block_output = mlp_backward(middle1, cotangent, rows[1], upper, None, True)
    came_m = swap(sent_m, CORE)
    kept_t, sent_t, in1, small_attn1 = attn_backward(
        between, mid1, packed1, mixed1, rows[1], docs, upper, None, None
    )
    in1, came_m, sent_t = gate((in1, came_m, sent_t))
    came_t = swap(sent_t, CORE)
    in1, came_t = gate((in1, came_t))
    sums_a = PlaneSums((kept_m, came_m), (kept_t, came_t))
    in1, to_go = gate((in1, sums_a.diagonals()))
    low_a, high_a = swap(to_go[0], ALONG_Y), swap(to_go[1], ALONG_X)
    kept_b, sent_b, mid0, small_mlp0 = mlp_backward(middle0, in1, rows[0], parts, starts, False)
    mid0, low_a, high_a, sent_b = gate((mid0, low_a, high_a, sent_b))
    mid0, to_go, sent_b, small_mlp1, small_attn1 = gate(
        (mid0, sums_a.sides(low_a, high_a), sent_b, small_mlp1, small_attn1)
    )
    x_a, y_a = along_each(*to_go)
    came_b = swap(sent_b, CORE)
    kept_c, sent_c, input_grad, small_attn0 = attn_backward(
        start, mid0, packed0, mixed0, rows[0], docs, parts, starts, step_ids
    )
    small_grads = jnp.stack(
        [
            collect_smalls(jnp.concatenate([small_mlp0, small_attn0], axis=1), 0),
            collect_smalls(jnp.concatenate([small_mlp1, small_attn1], axis=1), 1),
        ]
    ).reshape(2, 16, 2 * HALF)
    small_grads = small_grads[:, chip ^ jnp.arange(16, dtype=jnp.int32)][:, :, None]
    small_grads = jnp.pad(small_grads, ((0, 0), (0, 0), (0, 15), (0, 0)))
    kept_c, sent_c = [
        lax.dynamic_update_slice(
            v, lax.dynamic_index_in_dim(small_grads, side, 0, keepdims=False), (0, 32, 1536)
        )
        for v, side in ((kept_c, core), (sent_c, 1 - core))
    ]
    sums_b = PlaneSums((kept_b, came_b))
    input_grad, kept_c, sent_c, x_a, y_a, to_go = gate((input_grad, kept_c, sent_c, x_a, y_a, sums_b.diagonals()))
    low_b, high_b = swap(to_go[0], ALONG_Y), swap(to_go[1], ALONG_X)
    came_c = swap(sent_c, CORE)
    levels_a = sums_a.levels(x_a, y_a)
    low_b, high_b, levels_a = gate((low_b, high_b, levels_a))
    to_go, levels_a = gate((sums_b.sides(low_b, high_b), levels_a))
    x_b, y_b = along_each(*to_go)
    back_a = direct_line(levels_a)
    sums_c = PlaneSums((kept_c, came_c))
    x_b, y_b, to_go = gate((x_b, y_b, sums_c.diagonals()))
    low_c, high_c = swap(to_go[0], ALONG_Y), swap(to_go[1], ALONG_X)
    levels_b = sums_b.levels(x_b, y_b)
    low_c, high_c, back_a, levels_b = gate((low_c, high_c, back_a, levels_b))
    to_go, back_a, levels_b = gate((sums_c.sides(low_c, high_c), back_a, levels_b))
    x_c, y_c = along_each(*to_go)
    back_b = direct_line(levels_b)
    x_c, y_c, back_b, back_a = gate((x_c, y_c, back_b, back_a))
    levels_c = sums_c.levels(x_c, y_c)
    back_c = direct_line(levels_c)
    up_1, down_1, qkv_1, out_1 = own_rows(("up", "down_by_core", "qkv", "out"), total(levels_a[0], *back_a))
    up_1 = up_1.reshape(24, 4, TUNED, 24).transpose(0, 2, 1, 3).reshape(24, HIDDEN)
    up_0, down_0 = own_rows(("up", "down"), total(levels_b[0], *back_b))
    up, down = jnp.stack([up_0, up_1]), jnp.stack([down_0, down_1])
    up, down, qkv_1, out_1, back_c = gate((up, down, qkv_1, out_1, back_c))
    sum_c = total(levels_c[0], *back_c)
    qkv_0, out_0, extra_0 = own_rows(("qkv", "out", "extra"), sum_c)
    small_out = extra_0[32].reshape(2, HALF)
    out_b, gain_a, shift_a, down_b, gain_b, shift_b = [small_out[:, n * 24 : n * 24 + 24] for n in range(6)]
    return (
        block_output,
        input_grad,
        extra_0[:32],
        jnp.stack([qkv_0, qkv_1]),
        small_out[:, 144:192],
        jnp.stack([out_0, out_1]),
        out_b,
        gain_a,
        shift_a,
        up,
        small_out[:, 192:288],
        down,
        down_b,
        gain_b,
        shift_b,
    )


def shortened(value):
    return jax.tree.map(lambda a: a.astype(jnp.bfloat16) if a.dtype == jnp.float32 else a, value)


def partner(value, axis, stride):
    return lax.ppermute(value, axis, [(i, i ^ 1 << stride) for i in range(lax.axis_size(axis))])


def norm_rows(hidden, gain_vec, shift_vec):
    average = jnp.mean(hidden, axis=-1, keepdims=True)
    centred = hidden - average
    variance = jnp.mean(centred * centred, axis=-1, keepdims=True)
    inverse = lax.rsqrt(variance + EPSILON)
    unit_rows = centred * inverse
    normed = unit_rows * gain_vec.astype(jnp.float32) + shift_vec.astype(jnp.float32)
    return (normed, unit_rows, inverse)


def norm_back(grad_rows, unit_rows, inverse, gain_vec):
    scaled = grad_rows * gain_vec.astype(jnp.float32)
    first_mean = jnp.mean(scaled, axis=-1, keepdims=True)
    second_mean = jnp.mean(scaled * unit_rows, axis=-1, keepdims=True)
    return inverse * (scaled - first_mean - unit_rows * second_mean)


def smooth_gate(lifted):
    return jax.nn.gelu(lifted, approximate=True)


def halving_sum(members, send_fn):
    levels = lax.axis_size("dp").bit_length() - 1
    position = lax.axis_index("dp")
    current = tuple(members)
    for level in range(levels - 1, -1, -1):
        upper_side = position // (1 << level) % 2 == 1
        kept_list = []
        sent_list = []
        for member in current:
            half = member.shape[0] // 2
            lower_part = member[:half]
            upper_part = member[half:]
            kept_list.append(jnp.where(upper_side, upper_part, lower_part))
            sent_list.append(jnp.where(upper_side, lower_part, upper_part))
        received = send_fn(tuple(sent_list), level)
        current = tuple((kept + came for kept, came in zip(kept_list, received)))
    return current


def layer_apply(hidden, params, same_doc):
    qkv_w, qv_b, out_w, out_b, gain_a, shift_a, up_w, up_b, down_w, down_b, gain_b, shift_b = params
    width = out_w.shape[0]
    tok_count = hidden.shape[0]
    scale = 1.0 / math.sqrt(HEAD_DIM)
    normed_a, unit_a, inverse_a = norm_rows(hidden, gain_a, shift_a)
    normed_a = normed_a.astype(jnp.bfloat16)
    qv_float = qv_b.astype(jnp.float32)
    bias_full = jnp.concatenate(
        [qv_float[:width], jnp.zeros((width,), jnp.float32), qv_float[width:]]
    )
    packed = (jnp.dot(normed_a, qkv_w, preferred_element_type=jnp.float32) + bias_full).astype(
        jnp.bfloat16
    )
    queries = packed[:, :width].reshape(tok_count, HEADS, HEAD_DIM)
    key_rows = packed[:, width : 2 * width].reshape(tok_count, HEADS, HEAD_DIM)
    value_rows = packed[:, 2 * width :].reshape(tok_count, HEADS, HEAD_DIM)
    scores = (
        jnp.einsum("qhd,khd->hqk", queries, key_rows, preferred_element_type=jnp.float32) * scale
    )
    masked = jnp.where(same_doc[None], scores, -1e30)
    top_score = jnp.max(masked, axis=-1, keepdims=True)
    expo_rows = jnp.exp(masked - top_score)
    probs = expo_rows / jnp.sum(expo_rows, axis=-1, keepdims=True)
    probs_low = probs.astype(jnp.bfloat16)
    mixed = jnp.einsum("hqk,khd->qhd", probs_low, value_rows, preferred_element_type=jnp.float32)
    mixed = mixed.reshape(tok_count, width).astype(jnp.bfloat16)
    middle = (
        hidden
        + jnp.dot(mixed, out_w, preferred_element_type=jnp.float32)
        + out_b.astype(jnp.float32)
    )
    normed_b, unit_b, inverse_b = norm_rows(middle, gain_b, shift_b)
    normed_b = normed_b.astype(jnp.bfloat16)
    lifted = jnp.dot(normed_b, up_w, preferred_element_type=jnp.float32) + up_b.astype(jnp.float32)
    activated = smooth_gate(lifted).astype(jnp.bfloat16)
    output = (
        middle
        + jnp.dot(activated, down_w, preferred_element_type=jnp.float32)
        + down_b.astype(jnp.float32)
    )
    saved = (
        unit_a,
        inverse_a,
        normed_a,
        queries,
        key_rows,
        value_rows,
        probs,
        probs_low,
        mixed,
        unit_b,
        inverse_b,
        normed_b,
        lifted,
        activated,
    )
    return (output, saved)


def layer_back(hidden, params, same_doc, grad_top):
    qkv_w, qv_b, out_w, out_b, gain_a, shift_a, up_w, up_b, down_w, down_b, gain_b, shift_b = params
    unused_output, saved = layer_apply(hidden, params, same_doc)
    (
        unit_a,
        inverse_a,
        normed_a,
        queries,
        key_rows,
        value_rows,
        probs,
        probs_low,
        mixed,
        unit_b,
        inverse_b,
        normed_b,
        lifted,
        activated,
    ) = saved
    width = out_w.shape[0]
    tok_count = hidden.shape[0]
    scale = 1.0 / math.sqrt(HEAD_DIM)
    grad_down = grad_top.astype(jnp.bfloat16)
    down_b_grad = jnp.sum(grad_down.astype(jnp.float32), axis=0)
    down_w_grad = jnp.einsum("tf,td->fd", activated, grad_down, preferred_element_type=jnp.float32)
    grad_act = jnp.einsum("td,fd->tf", grad_down, down_w, preferred_element_type=jnp.float32)
    unused_gate, gate_pull = jax.vjp(smooth_gate, lifted)
    grad_lift = gate_pull(grad_act)[0].astype(jnp.bfloat16)
    up_b_grad = jnp.sum(grad_lift.astype(jnp.float32), axis=0)
    up_w_grad = jnp.einsum("td,tf->df", normed_b, grad_lift, preferred_element_type=jnp.float32)
    grad_nb = jnp.einsum("tf,df->td", grad_lift, up_w, preferred_element_type=jnp.float32)
    gain_b_grad = jnp.sum(grad_nb * unit_b, axis=0)
    shift_b_grad = jnp.sum(grad_nb, axis=0)
    grad_mid = grad_top + norm_back(grad_nb, unit_b, inverse_b, gain_b)
    grad_branch = grad_mid.astype(jnp.bfloat16)
    out_b_grad = jnp.sum(grad_branch.astype(jnp.float32), axis=0)
    out_w_grad = jnp.einsum("te,td->ed", mixed, grad_branch, preferred_element_type=jnp.float32)
    grad_mixed = jnp.einsum("td,ed->te", grad_branch, out_w, preferred_element_type=jnp.float32)
    grad_mixed = grad_mixed.astype(jnp.bfloat16).reshape(tok_count, HEADS, HEAD_DIM)
    grad_probs = jnp.einsum(
        "qhd,khd->hqk", grad_mixed, value_rows, preferred_element_type=jnp.float32
    )
    grad_values = jnp.einsum(
        "hqk,qhd->khd", probs_low, grad_mixed, preferred_element_type=jnp.float32
    )
    grad_scores = probs * (grad_probs - jnp.sum(probs * grad_probs, axis=-1, keepdims=True))
    scores_low = grad_scores.astype(jnp.bfloat16)
    grad_queries = (
        jnp.einsum("hqk,khd->qhd", scores_low, key_rows, preferred_element_type=jnp.float32) * scale
    )
    grad_keys = (
        jnp.einsum("hqk,qhd->khd", scores_low, queries, preferred_element_type=jnp.float32) * scale
    )
    grad_packed = jnp.concatenate(
        [
            grad_queries.reshape(tok_count, width),
            grad_keys.reshape(tok_count, width),
            grad_values.reshape(tok_count, width),
        ],
        axis=1,
    ).astype(jnp.bfloat16)
    packed_sums = jnp.sum(grad_packed.astype(jnp.float32), axis=0)
    qv_b_grad = jnp.concatenate([packed_sums[:width], packed_sums[2 * width :]])
    qkv_w_grad = jnp.einsum("td,te->de", normed_a, grad_packed, preferred_element_type=jnp.float32)
    grad_na = jnp.einsum("te,de->td", grad_packed, qkv_w, preferred_element_type=jnp.float32)
    gain_a_grad = jnp.sum(grad_na * unit_a, axis=0)
    shift_a_grad = jnp.sum(grad_na, axis=0)
    grad_in = grad_mid + norm_back(grad_na, unit_a, inverse_a, gain_a)
    grads = (
        qkv_w_grad,
        qv_b_grad,
        out_w_grad,
        out_b_grad,
        gain_a_grad,
        shift_a_grad,
        up_w_grad,
        up_b_grad,
        down_w_grad,
        down_b_grad,
        gain_b_grad,
        shift_b_grad,
    )
    return (grad_in, grads)


def plain(
    embedded,
    doc_ids,
    step_ids,
    step_table,
    qkv_weight,
    qv_bias,
    out_weight,
    out_bias,
    first_gain,
    first_shift,
    up_weight,
    up_bias,
    down_weight,
    down_bias,
    second_gain,
    second_shift,
    cotangent,
):
    docs_row = doc_ids[0]
    same_doc = docs_row[:, None] == docs_row[None, :]
    doc_count = step_ids.shape[1]
    doc_hot = (docs_row[:, None] == jnp.arange(doc_count, dtype=jnp.int32)[None, :]).astype(
        jnp.float32
    )
    gathered_first = (
        lax.all_gather(qkv_weight[0], "dp", axis=0, tiled=True),
        lax.all_gather(qv_bias[0], "dp", axis=0, tiled=True),
        lax.all_gather(out_weight[0], "dp", axis=0, tiled=True),
        lax.all_gather(out_bias[0], "dp", axis=0, tiled=True),
        lax.all_gather(first_gain[0], "dp", axis=0, tiled=True),
        lax.all_gather(first_shift[0], "dp", axis=0, tiled=True),
        lax.all_gather(up_weight[0], "dp", axis=0, tiled=True),
        lax.all_gather(up_bias[0], "dp", axis=0, tiled=True),
        lax.all_gather(down_weight[0], "dp", axis=0, tiled=True),
        lax.all_gather(down_bias[0], "dp", axis=0, tiled=True),
        lax.all_gather(second_gain[0], "dp", axis=0, tiled=True),
        lax.all_gather(second_shift[0], "dp", axis=0, tiled=True),
        lax.all_gather(step_table, "dp", axis=0, tiled=True),
    )
    params_lower = gathered_first[:12]
    table_whole = gathered_first[12]
    step_hot = step_ids[0][:, None] == jnp.arange(table_whole.shape[0], dtype=jnp.int32)[None, :]
    doc_rows = jnp.dot(
        step_hot.astype(jnp.bfloat16), table_whole, preferred_element_type=jnp.float32
    )
    start = embedded.astype(jnp.float32) + jnp.dot(
        doc_hot, doc_rows, precision=lax.Precision.HIGHEST
    )
    middle_hidden, unused_lower = layer_apply(start, params_lower, same_doc)
    params_upper = (
        lax.all_gather(qkv_weight[1], "dp", axis=0, tiled=True),
        lax.all_gather(qv_bias[1], "dp", axis=0, tiled=True),
        lax.all_gather(out_weight[1], "dp", axis=0, tiled=True),
        lax.all_gather(out_bias[1], "dp", axis=0, tiled=True),
        lax.all_gather(first_gain[1], "dp", axis=0, tiled=True),
        lax.all_gather(first_shift[1], "dp", axis=0, tiled=True),
        lax.all_gather(up_weight[1], "dp", axis=0, tiled=True),
        lax.all_gather(up_bias[1], "dp", axis=0, tiled=True),
        lax.all_gather(down_weight[1], "dp", axis=0, tiled=True),
        lax.all_gather(down_bias[1], "dp", axis=0, tiled=True),
        lax.all_gather(second_gain[1], "dp", axis=0, tiled=True),
        lax.all_gather(second_shift[1], "dp", axis=0, tiled=True),
    )
    final_hidden, unused_upper = layer_apply(middle_hidden, params_upper, same_doc)
    block_output = final_hidden.astype(jnp.bfloat16)

    def weights_for(layer_index):
        return (
            lax.all_gather(qkv_weight[layer_index], "dp", axis=0, tiled=True),
            lax.all_gather(qv_bias[layer_index], "dp", axis=0, tiled=True),
            lax.all_gather(out_weight[layer_index], "dp", axis=0, tiled=True),
            lax.all_gather(out_bias[layer_index], "dp", axis=0, tiled=True),
            lax.all_gather(first_gain[layer_index], "dp", axis=0, tiled=True),
            lax.all_gather(first_shift[layer_index], "dp", axis=0, tiled=True),
            lax.all_gather(up_weight[layer_index], "dp", axis=0, tiled=True),
            lax.all_gather(up_bias[layer_index], "dp", axis=0, tiled=True),
            lax.all_gather(down_weight[layer_index], "dp", axis=0, tiled=True),
            lax.all_gather(down_bias[layer_index], "dp", axis=0, tiled=True),
            lax.all_gather(second_gain[layer_index], "dp", axis=0, tiled=True),
            lax.all_gather(second_shift[layer_index], "dp", axis=0, tiled=True),
        )

    grad_upper_in, upper_grads = layer_back(
        middle_hidden, weights_for(1), same_doc, cotangent.astype(jnp.float32)
    )

    def send_upper(sent, level):
        return jax.tree.map(
            lambda part, own: part.astype(own.dtype), partner(shortened(sent), "dp", level), sent
        )

    upper_shards = halving_sum(upper_grads, send_upper)
    input_grad, lower_grads = layer_back(start, weights_for(0), same_doc, grad_upper_in)
    doc_grads = jnp.einsum("ts,td->sd", doc_hot, input_grad, precision=lax.Precision.HIGHEST)
    table_full_grad = jnp.einsum(
        "sn,sd->nd", step_hot.astype(jnp.float32), doc_grads, precision=lax.Precision.HIGHEST
    )

    def send_lower(sent, level):
        return jax.tree.map(
            lambda part, own: part.astype(own.dtype), partner(shortened(sent), "dp", level), sent
        )

    lower_all = halving_sum(tuple(lower_grads) + (table_full_grad,), send_lower)
    lower_shards = lower_all[:12]
    table_shard = lower_all[12]
    stacked = [jnp.stack([lower_shards[index], upper_shards[index]], axis=0) for index in range(12)]
    return (
        block_output,
        input_grad,
        table_shard,
        stacked[0],
        stacked[1],
        stacked[2],
        stacked[3],
        stacked[4],
        stacked[5],
        stacked[6],
        stacked[7],
        stacked[8],
        stacked[9],
        stacked[10],
        stacked[11],
    )


def solution(mesh):
    local = tuned if mesh.shape["dp"] == TUNED else plain
    in_specs = (
        P("dp", None),
        P("dp", None),
        P("dp", None),
        P("dp", None),
        P(None, "dp", None),
        P(None, "dp"),
        P(None, "dp", None),
        P(None, "dp"),
        P(None, "dp"),
        P(None, "dp"),
        P(None, "dp", None),
        P(None, "dp"),
        P(None, "dp", None),
        P(None, "dp"),
        P(None, "dp"),
        P(None, "dp"),
        P("dp", None),
    )
    out_specs = (
        P("dp", None),
        P("dp", None),
        P("dp", None),
        P(None, "dp", None),
        P(None, "dp"),
        P(None, "dp", None),
        P(None, "dp"),
        P(None, "dp"),
        P(None, "dp"),
        P(None, "dp", None),
        P(None, "dp"),
        P(None, "dp", None),
        P(None, "dp"),
        P(None, "dp"),
        P(None, "dp"),
    )
    return jax.shard_map(local, mesh=mesh, in_specs=in_specs, out_specs=out_specs, check_vma=False)
```

```python
import math

import jax
import jax.numpy as jnp
import numpy as np
from jax import lax
from jax.experimental import pallas as pl
from jax.experimental.pallas import tpu as pltpu
from jax.sharding import PartitionSpec as P

HEADS = 12
HEAD_DIM = 64
EPSILON = 1e-05
BF = jnp.bfloat16
F32 = jnp.float32

TUNED = 32
CORE, ALONG_X, ALONG_Y, ALONG_Z, MIDDLE = 1, 2, 4, 8, 24
SLAB = 48
HALF = 384


def swap(value, stride):
    return lax.ppermute(value, "dp", [(i, i ^ stride) for i in range(TUNED)])


def swap_from(value, stride, zs):
    return lax.ppermute(value, "dp", [(i, i ^ stride) for i in range(TUNED) if i // 8 in zs])


def after(done, waiting):
    return lax.optimization_barrier((done, waiting))


def place():
    index = lax.axis_index("dp")
    return index % 2, index // 2


WIDTH = HEADS * HEAD_DIM
HIDDEN = 4 * WIDTH
PAIR = 2 * HEAD_DIM
ANY = pl.BlockSpec(memory_space=pl.ANY)
WHOLE = pl.BlockSpec(memory_space=pltpu.VMEM)
ATTN = {"qkv": 1152, "out": 384}
MLP = {"up": 1536, "down": 1536}
SHAPES = {"qkv": (768, 2304), "out": (768, 768), "up": (768, 3072), "down": (3072, 768), "extra": (768, 1536)}


SPOTS = {"gain_a": 0, "shift_a": 768, "out_b": 1536, "gain_b": 2304, "shift_b": 3072, "down_b": 3840}
BIAS_AT, UP_AT, ROW_LENGTH = 4608, 6912, 9984


def spot(ref, name):
    return ref[:, SPOTS[name] : SPOTS[name] + WIDTH]


class Part:
    def __init__(self, array, entries, own):
        self.array, self.entries, self.own = array, entries, own


class Source:
    def __init__(self, weights, starts):
        self.weights, self.starts = weights, starts
        self.natural = not isinstance(weights, list)
        self.arrays = [weights] if self.natural else [part.array for part in weights]


def fetch_parts(parts, refs, starts, targets, sems):
    index = lax.axis_index("dp")
    core, chip = index % 2, index // 2
    for part, ref in zip(parts, refs):
        half = core if part.own else 1 - core
        for leading, code, first in part.entries:
            last = first + part.array.shape[-1]
            there = chip ^ code
            for name, target in targets.items():
                begin = starts[name]
                if name == "down":
                    pieces = [(begin + block * HALF, HALF, block) for block in range(4)]
                else:
                    pieces = [(begin, target.shape[1] // 2, None)]
                for start, width, block in pieces:
                    low, high = max(start, first), min(start + width, last)
                    if low >= high:
                        continue
                    columns = pl.ds(pl.multiple_of(half * width + (low - start), 128), high - low)
                    row = there * SLAB if block is None else there * (4 * SLAB) + block * SLAB
                    pltpu.make_async_copy(
                        ref.at[leading + (slice(None), pl.ds(low - first, high - low))],
                        target.at[pl.ds(pl.multiple_of(row, SLAB), SLAB), columns],
                        sems[name],
                    ).start()


def start_fetch(sources, refs, targets, sems):
    for source in sources:
        own, refs = refs[: len(source.arrays)], refs[len(source.arrays) :]
        wanted = {name: targets[name] for name in source.starts if name in targets}
        if not source.natural:
            fetch_parts(source.weights, own, source.starts, wanted, sems)
            continue
        for name, target in wanted.items():
            pieces = [(0, slice(None), target.shape[1])]
            if name == "down":
                pieces = [(b * WIDTH, pl.ds(b * WIDTH, WIDTH), WIDTH) for b in range(4)]
            for shift, rows, width in pieces:
                pltpu.make_async_copy(
                    own[0].at[:, pl.ds(source.starts[name] + shift, width)], target.at[rows, :], sems[name]
                ).start()


def arrays_of(sources):
    return [array for source in sources for array in source.arrays]


def arrived(target, sem):
    pltpu.make_async_copy(target, target, sem).wait()


def dot(left, right, contract):
    return lax.dot_general(left, right, ((contract[:1], contract[1:]), ((), ())), preferred_element_type=F32)


def unit_of(hidden):
    average = jnp.mean(hidden, axis=-1, keepdims=True)
    centred = hidden - average
    inverse = lax.rsqrt(jnp.mean(centred * centred, axis=-1, keepdims=True) + EPSILON)
    return centred * inverse, inverse


def back_of_norm(grad_rows, unit_rows, inverse, gain):
    scaled = grad_rows * gain
    first_mean = jnp.mean(scaled, axis=-1, keepdims=True)
    second_mean = jnp.mean(scaled * unit_rows, axis=-1, keepdims=True)
    return inverse * (scaled - first_mean - unit_rows * second_mean)


def gelu_pair(value):
    factor = math.sqrt(2.0 / math.pi)
    square = value * value
    bend = jnp.tanh(factor * value * (1.0 + 0.044715 * square))
    half_up = 0.5 * (1.0 + bend)
    slope = half_up + 0.5 * value * (1.0 - bend * bend) * factor * (1.0 + 3.0 * 0.044715 * square)
    return value * half_up, slope


def softmax_rows(query, keys, same):
    scores = dot(query, keys, (1, 1)) * (1.0 / math.sqrt(HEAD_DIM))
    masked = jnp.where(same, scores, -1e30)
    expo = jnp.exp(masked - jnp.max(masked, axis=-1, keepdims=True))
    return expo * (1.0 / jnp.sum(expo, axis=-1, keepdims=True))


def head_lanes(count):
    return lax.broadcasted_iota(jnp.int32, (count, PAIR), 1) < HEAD_DIM


def pair_slice(pair, block):
    return pl.ds(pl.multiple_of(block * WIDTH + pair * PAIR, PAIR), PAIR)


def attn_steps(hidden, row_ref, docs_refs, packed_ref, mixed_ref, qkv_ref, out_ref, named):
    unit, _ = unit_of(hidden)
    normed = (unit * spot(row_ref, "gain_a") + spot(row_ref, "shift_a")).astype(BF)
    arrived(qkv_ref, named["qkv"])
    for block in range(3):
        columns = slice(block * WIDTH, (block + 1) * WIDTH)
        packed_ref[:, columns] = (
            dot(normed, qkv_ref[:, columns], (1, 0))
            + row_ref[:, BIAS_AT + block * WIDTH : BIAS_AT + (block + 1) * WIDTH]
        ).astype(BF)
    same = docs_refs[0][...] == docs_refs[1][...]
    first_head = head_lanes(hidden.shape[0])
    for pair in range(HEADS // 2):
        query, keys, values = [packed_ref[:, pair_slice(pair, block)] for block in range(3)]
        blank = jnp.zeros_like(query)
        mixes = []
        for own in (jnp.where(first_head, query, blank), jnp.where(first_head, blank, query)):
            mixes.append(dot(softmax_rows(own, keys, same).astype(BF), values, (1, 0)))
        mixed_ref[:, pair_slice(pair, 0)] = jnp.where(first_head, mixes[0], mixes[1]).astype(BF)
    arrived(out_ref, named["out"])
    return hidden + dot(mixed_ref[...], out_ref[...], (1, 0)) + spot(row_ref, "out_b")


def layer_forward(hidden, row, docs, sources):
    arrays = arrays_of(sources)
    tokens = hidden.shape[0]
    names = ("qkv", "out", "up", "down")

    def body(hidden_ref, row_ref, down_docs, across_docs, *rest):
        refs, rest = rest[: len(arrays)], rest[len(arrays) :]
        packed_ref, mixed_ref, middle_ref, top_ref = rest[:4]
        targets, sems = dict(zip(names, rest[4:8])), rest[8]
        named = {name: sems.at[n] for n, name in enumerate(names)}
        start_fetch(sources, refs, targets, named)
        middle = attn_steps(
            hidden_ref[...],
            row_ref,
            (down_docs, across_docs),
            packed_ref,
            mixed_ref,
            targets["qkv"],
            targets["out"],
            named,
        )
        middle_ref[...] = middle
        unit, _ = unit_of(middle)
        normed = (unit * spot(row_ref, "gain_b") + spot(row_ref, "shift_b")).astype(BF)
        total = middle + spot(row_ref, "down_b")
        up_ref, down_ref = targets["up"], targets["down"]
        arrived(up_ref, named["up"])
        arrived(down_ref, named["down"])
        for tile in range(4):
            columns = slice(tile * WIDTH, (tile + 1) * WIDTH)
            lifted = dot(normed, up_ref[:, columns], (1, 0))
            lifted = lifted + row_ref[:, UP_AT + tile * WIDTH : UP_AT + (tile + 1) * WIDTH]
            active, _ = gelu_pair(lifted)
            total = total + dot(active.astype(BF), down_ref[columns, :], (1, 0))
        top_ref[...] = total

    return pl.pallas_call(
        body,
        out_shape=[
            jax.ShapeDtypeStruct((tokens, 3 * WIDTH), BF),
            jax.ShapeDtypeStruct((tokens, WIDTH), BF),
            jax.ShapeDtypeStruct((tokens, WIDTH), F32),
            jax.ShapeDtypeStruct((tokens, WIDTH), F32),
        ],
        in_specs=[WHOLE] * 4 + [ANY] * len(arrays),
        out_specs=[WHOLE] * 4,
        scratch_shapes=[pltpu.VMEM(SHAPES[name], BF) for name in names] + [pltpu.SemaphoreType.DMA((4,))],
        compiler_params=pltpu.CompilerParams(vmem_limit_bytes=50 * 2**20),
        cost_estimate=pl.CostEstimate(flops=1, bytes_accessed=1, transcendentals=1),
        name="layer_forward",
    )(hidden, row, docs.reshape(-1, 1), docs.reshape(1, -1), *arrays)


def send_rows(source, rows, columns, targets, half, first, sem):
    index = lax.axis_index("dp")
    core, chip = index % 2, index // 2
    for side, target in enumerate(targets):

        @pl.when(core == half ^ side)
        def _(target=target):
            for there, row in rows:
                pltpu.make_async_copy(
                    source.at[pl.ds(row, SLAB), columns],
                    target.at[chip ^ there, :, pl.ds(first, columns.size)],
                    sem,
                ).start()


def mlp_backward(hidden, grad_top, row, sources, docs=None):
    natural = any(source.natural and "down" in source.starts for source in sources)
    arrays = arrays_of(sources)
    tokens = hidden.shape[0]
    whole_layer = docs is not None
    names = ("up", "down", "qkv", "out") if whole_layer else ("up", "down")
    doc_operands = [docs.reshape(-1, 1), docs.reshape(1, -1)] if whole_layer else []

    def body(hidden_ref, grad_ref, row_ref, *rest):
        docs_refs, rest = rest[: len(doc_operands)], rest[len(doc_operands) :]
        refs, rest = rest[: len(arrays)], rest[len(arrays) :]
        grads_ref, (mid_ref, small_ref), rest = rest[:2], rest[2:4], rest[4:]
        if whole_layer:
            (packed_ref, mixed_ref, top_ref), rest = rest[:3], rest[3:]
        targets, (up_stage, down_stage, sems) = dict(zip(names, rest[:-3])), rest[-3:]
        named = {name: sems.at[n] for n, name in enumerate(names)}
        up_sem, down_sem = sems.at[4], sems.at[5]
        up_ref, down_ref = targets["up"], targets["down"]
        start_fetch(sources, refs, targets, named)
        middle = hidden_ref[...]
        if whole_layer:
            middle = attn_steps(
                middle, row_ref, docs_refs, packed_ref, mixed_ref, targets["qkv"], targets["out"], named
            )
        unit, inverse = unit_of(middle)
        normed = unit * spot(row_ref, "gain_b") + spot(row_ref, "shift_b")
        normed_turned = normed.T.astype(BF)
        normed = normed.astype(BF)
        grad_top_rows = grad_ref[...].astype(F32)
        grad_down = grad_top_rows.astype(BF)
        small_ref[:, HIDDEN : HIDDEN + WIDTH] = jnp.sum(grad_down.astype(F32), axis=0, keepdims=True)
        grad_nb = jnp.zeros((tokens, WIDTH), F32)
        total = middle + spot(row_ref, "down_b") if whole_layer else None
        arrived(up_ref, named["up"])
        arrived(down_ref, named["down"])
        for tile in range(4):
            columns = slice(tile * WIDTH, (tile + 1) * WIDTH)
            lifted = dot(normed, up_ref[:, columns], (1, 0))
            lifted = lifted + row_ref[:, UP_AT + tile * WIDTH : UP_AT + (tile + 1) * WIDTH]
            active, slope = gelu_pair(lifted)
            active = active.astype(BF)
            if whole_layer:
                total = total + dot(active, down_ref[columns, :], (1, 0))
            grad_act = dot(grad_down, down_ref[columns, :], (1, 1))
            grad_lift = (grad_act * slope).astype(BF)
            small_ref[:, columns] = jnp.sum(grad_lift.astype(F32), axis=0, keepdims=True)
            grad_nb = grad_nb + dot(grad_lift, up_ref[:, columns], (1, 1))
            up_stage[:, columns] = dot(normed_turned, grad_lift, (1, 0)).astype(BF)
            down_stage[columns, :] = dot(active, grad_down, (0, 0)).astype(BF)
            send_rows(
                up_stage,
                [(there, there * SLAB) for there in range(16)],
                pl.ds(tile * WIDTH, WIDTH),
                grads_ref,
                tile // 2,
                tile % 2 * WIDTH,
                up_sem,
            )
            if natural:
                pieces = [(tile, [(there, tile * WIDTH + there * SLAB) for there in range(16)])]
            else:
                chips = range(4 * tile, 4 * tile + 4)
                pieces = [(b, [(there, there * 4 * SLAB + b * SLAB) for there in chips]) for b in range(4)]
            for half in range(2):
                for block, rows in pieces:
                    send_rows(
                        down_stage,
                        rows,
                        pl.ds(half * HALF, HALF),
                        grads_ref,
                        half,
                        4 * HALF + block * HALF,
                        down_sem,
                    )
        if whole_layer:
            top_ref[...] = total.astype(BF)
        small_ref[:, HIDDEN + WIDTH : HIDDEN + 2 * WIDTH] = jnp.sum(grad_nb * unit, axis=0, keepdims=True)
        small_ref[:, HIDDEN + 2 * WIDTH :] = jnp.sum(grad_nb, axis=0, keepdims=True)
        mid_ref[...] = grad_top_rows + back_of_norm(grad_nb, unit, inverse, spot(row_ref, "gain_b"))
        arrived(up_stage, up_sem)
        arrived(down_stage, down_sem)

    outs = [jax.ShapeDtypeStruct((16, SLAB, HIDDEN), BF)] * 2 + [
        jax.ShapeDtypeStruct((tokens, WIDTH), F32),
        jax.ShapeDtypeStruct((1, HIDDEN + 3 * WIDTH), F32),
    ]
    if whole_layer:
        outs += [jax.ShapeDtypeStruct((tokens, count * WIDTH), BF) for count in (3, 1, 1)]
    return pl.pallas_call(
        body,
        out_shape=outs,
        in_specs=[WHOLE] * (3 + len(doc_operands)) + [ANY] * len(arrays),
        out_specs=[ANY] * 2 + [WHOLE] * (len(outs) - 2),
        scratch_shapes=[pltpu.VMEM(SHAPES[name], BF) for name in names + ("up", "down")]
        + [pltpu.SemaphoreType.DMA((6,))],
        compiler_params=pltpu.CompilerParams(vmem_limit_bytes=54 * 2**20),
        cost_estimate=pl.CostEstimate(flops=1, bytes_accessed=1, transcendentals=1),
        name="top_layer" if whole_layer else "mlp_backward",
    )(hidden, grad_top, row, *doc_operands, *arrays)


def attn_backward(hidden, grad_mid, packed, mixed, row, docs, sources, steps):
    arrays = arrays_of(sources)
    tokens = hidden.shape[0]
    scale = 1.0 / math.sqrt(HEAD_DIM)

    def body(hidden_ref, mid_ref, packed_ref, mixed_ref, row_ref, down_docs, across_docs, *rest):
        if steps is not None:
            steps_ref, rest = rest[0], rest[1:]
        refs, rest = rest[: len(arrays)], rest[len(arrays) :]
        grads_ref, rest = rest[:2], rest[2:]
        in_ref, small_ref = rest[:2]
        qkv_ref, out_ref, qkv_stage, out_stage, gm_ref, gp_ref, sems = rest[2:9]
        named = {"qkv": sems.at[0], "out": sems.at[1]}
        start_fetch(sources, refs, {"qkv": qkv_ref, "out": out_ref}, named)
        unit, inverse = unit_of(hidden_ref[...])
        normed = (unit * spot(row_ref, "gain_a") + spot(row_ref, "shift_a")).astype(BF)
        grad_branch = mid_ref[...].astype(BF)
        small_ref[:, 2 * WIDTH : 3 * WIDTH] = jnp.sum(grad_branch.astype(F32), axis=0, keepdims=True)
        out_stage[...] = dot(mixed_ref[...], grad_branch, (0, 0)).astype(BF)
        chips = [(there, there * SLAB) for there in range(16)]
        for half in range(2):
            send_rows(out_stage, chips, pl.ds(half * HALF, HALF), grads_ref, half, 3 * HALF, sems.at[2])
        arrived(out_ref, named["out"])
        gm_ref[...] = dot(grad_branch, out_ref[...], (1, 1)).astype(BF)
        same = down_docs[...] == across_docs[...]
        first_head = head_lanes(tokens)

        def one_pair(pair, carry):
            query = packed_ref[:, pair_slice(pair, 0)]
            keys = packed_ref[:, pair_slice(pair, 1)]
            values = packed_ref[:, pair_slice(pair, 2)]
            grad_mixed = gm_ref[:, pair_slice(pair, 0)]
            blank = jnp.zeros_like(query)
            query_turned = query.astype(F32).T.astype(BF)
            mixed_turned = grad_mixed.astype(F32).T.astype(BF)
            by_query, by_key, by_value = [], [], []
            for head in range(2):
                rows_of = slice(head * HEAD_DIM, (head + 1) * HEAD_DIM)
                lanes = first_head if head == 0 else jnp.logical_not(first_head)
                probs = softmax_rows(jnp.where(lanes, query, blank), keys, same)
                low = probs.astype(BF)
                grad_probs = dot(jnp.where(lanes, grad_mixed, blank), values, (1, 1))
                grad_scores = probs * (grad_probs - jnp.sum(probs * grad_probs, axis=-1, keepdims=True))
                scores_low = grad_scores.astype(BF)
                by_query.append(dot(scores_low, keys, (1, 0)))
                by_key.append(dot(query_turned[rows_of], scores_low, (1, 0)))
                by_value.append(dot(mixed_turned[rows_of], low, (1, 0)))
            gp_ref[:, pair_slice(pair, 0)] = (jnp.where(first_head, *by_query) * scale).astype(BF)
            gp_ref[:, pair_slice(pair, 1)] = (jnp.concatenate(by_key, axis=0).T * scale).astype(BF)
            gp_ref[:, pair_slice(pair, 2)] = jnp.concatenate(by_value, axis=0).T.astype(BF)
            return carry

        lax.fori_loop(0, HEADS // 2, one_pair, 0, unroll=True)
        arrived(qkv_ref, named["qkv"])
        grad_na = jnp.zeros((tokens, WIDTH), F32)
        for block in range(3):
            columns = slice(block * WIDTH, (block + 1) * WIDTH)
            piece = gp_ref[:, columns]
            sums = jnp.sum(piece.astype(F32), axis=0, keepdims=True)
            if block != 1:
                small_ref[:, block // 2 * WIDTH : (block // 2 + 1) * WIDTH] = sums
            qkv_stage[:, columns] = dot(normed, piece, (0, 0)).astype(BF)
            grad_na = grad_na + dot(piece, qkv_ref[:, columns], (1, 1))
        for half in range(2):
            send_rows(qkv_stage, chips, pl.ds(half * 3 * HALF, 3 * HALF), grads_ref, half, 0, sems.at[3])
        small_ref[:, 3 * WIDTH : 4 * WIDTH] = jnp.sum(grad_na * unit, axis=0, keepdims=True)
        small_ref[:, 4 * WIDTH :] = jnp.sum(grad_na, axis=0, keepdims=True)
        grad_in = mid_ref[...] + back_of_norm(grad_na, unit, inverse, spot(row_ref, "gain_a"))
        in_ref[...] = grad_in
        if steps is not None:
            sums_ref, table_stages = rest[9], rest[10:]
            index = lax.axis_index("dp")
            core, chip = index % 2, index // 2
            for doc in range(8):
                sums_ref[doc : doc + 1, :] = (
                    jnp.sum(jnp.where(down_docs[...] == doc, grad_in, 0.0), axis=0, keepdims=True)
                    if doc < steps.shape[1]
                    else jnp.zeros((1, WIDTH), F32)
                )
            spots = [lax.broadcasted_iota(jnp.int32, (16, SLAB, 8), axis) for axis in range(2)]
            for side, half in enumerate((core, 1 - core)):
                sums = sums_ref[:, pl.ds(pl.multiple_of(half * HALF, HALF), HALF)].astype(BF)
                for owner in range(2):
                    line = ((chip ^ spots[0]) * 2 + owner) * 32 + spots[1]
                    line = jnp.where(spots[1] < 32, line, -1)
                    hot = jnp.where(line == steps_ref[...][None], 1.0, 0.0).reshape(16 * SLAB, 8).astype(BF)
                    block = dot(hot, sums, (1, 0)).astype(BF).reshape(16, SLAB, HALF)
                    stage = table_stages[side]
                    stage[:, :, owner * HALF : (owner + 1) * HALF] = block
                pltpu.make_async_copy(
                    table_stages[side], grads_ref[side].at[:, :, pl.ds(1536, 2 * HALF)], sems.at[4 + side]
                ).start()
            for side in range(2):
                arrived(table_stages[side], sems.at[4 + side])
        arrived(out_stage, sems.at[2])
        arrived(qkv_stage, sems.at[3])

    sums = [(16, SLAB, 1536 if steps is None else 2304)] * 2
    outs = [jax.ShapeDtypeStruct(shape, BF) for shape in sums] + [
        jax.ShapeDtypeStruct((tokens, WIDTH), F32),
        jax.ShapeDtypeStruct((1, 5 * WIDTH), F32),
    ]
    operands = [hidden, grad_mid, packed, mixed, row, docs.reshape(-1, 1), docs.reshape(1, -1)]
    scratch = [pltpu.VMEM(SHAPES["qkv"], BF), pltpu.VMEM(SHAPES["out"], BF)] * 2 + [
        pltpu.VMEM((tokens, WIDTH), BF),
        pltpu.VMEM((tokens, 3 * WIDTH), BF),
        pltpu.SemaphoreType.DMA((6,)),
    ]
    if steps is not None:
        operands.append(jnp.pad(steps, ((0, 0), (0, 8 - steps.shape[1])), constant_values=-2))
        scratch += [pltpu.VMEM((8, WIDTH), F32)] + [pltpu.VMEM((16, SLAB, 2 * HALF), BF)] * 2
    return pl.pallas_call(
        body,
        out_shape=outs,
        in_specs=[WHOLE] * len(operands) + [ANY] * len(arrays),
        out_specs=[ANY] * len(sums) + [WHOLE] * (len(outs) - len(sums)),
        scratch_shapes=scratch,
        compiler_params=pltpu.CompilerParams(vmem_limit_bytes=50 * 2**20),
        cost_estimate=pl.CostEstimate(flops=1, bytes_accessed=1, transcendentals=1),
        name="attn_backward",
    )(*operands, *arrays)


def lay_extra(source):
    def body(*rest):
        refs, (extra_ref, sems) = rest[: len(source.arrays)], rest[len(source.arrays) :]
        named = {"extra": sems.at[0]}
        start_fetch([source], refs, {"extra": extra_ref}, named)
        arrived(extra_ref, named["extra"])

    return pl.pallas_call(
        body,
        out_shape=jax.ShapeDtypeStruct(SHAPES["extra"], BF),
        in_specs=[ANY] * len(source.arrays),
        out_specs=WHOLE,
        scratch_shapes=[pltpu.SemaphoreType.DMA((1,))],
        compiler_params=pltpu.CompilerParams(vmem_limit_bytes=16 * 2**20),
        cost_estimate=pl.CostEstimate(flops=1, bytes_accessed=1, transcendentals=1),
        name="lay_extra",
    )(*source.arrays)


def is_middle():
    level = lax.axis_index("dp") // 8
    return (level == 1) | (level == 2)


def cut_of(value):
    return value.shape[-1] // 256 * 128


def chip_share(layer_weights, extra):
    core, _ = place()
    down = layer_weights.get("down")

    def halves(half):
        def columns(value):
            width = value.shape[1] // 2
            return value[:, half * width : half * width + width]

        narrow = [columns(layer_weights[name]) for name in ("qkv", "out", "up") if name in layer_weights]
        wide = []
        if down is not None:
            wide += [columns(down)[:SLAB], columns(down)[SLAB:]]
        if extra is not None:
            wide.append(columns(extra))
        parts = narrow
        if wide:
            wide = jnp.concatenate(wide, axis=1)
            parts = parts + [wide[:24], wide[24:]]
        return jnp.concatenate(parts, axis=1), sum(v.shape[1] for v in narrow)

    (left, count), (right, _) = halves(0), halves(1)
    kept = jnp.where(core == 0, left, right)
    came = swap(jnp.where(core == 0, right, left), CORE)
    lower = jnp.where(core == 0, kept, came)
    upper = jnp.where(core == 0, came, kept)
    columns = [jnp.concatenate([lower[:, :count], upper[:, :count]], axis=0)]
    wide = (lower.shape[1] - count) // 2
    if wide:
        low, high = [
            jnp.concatenate([v[:, count : count + wide], v[:, count + wide :]], axis=0) for v in (lower, upper)
        ]
        if down is not None:
            columns += [low[:, : 2 * HALF], high[:, : 2 * HALF]]
        if extra is not None:
            columns += [low[:, wide - HALF :], high[:, wide - HALF :]]
    return jnp.concatenate(columns, axis=1)


def line_second(first, third_middle):
    return swap_from(first, MIDDLE, (1, 2)), swap_from(third_middle, ALONG_Z, (1, 2))


def line_third(second_middle):
    return swap_from(second_middle, ALONG_Z, (1, 2))


def line_first(own):
    return swap(own, ALONG_Z), swap_from(own, MIDDLE, (1, 2))


def by_place(middle, end):
    return jnp.where(is_middle(), middle, end)


def along_each(to_x, to_y):
    return swap(to_x, ALONG_X), swap(to_y, ALONG_Y)


def diagonal(by_x, by_y):
    cut = cut_of(by_x)
    return swap(by_x[..., :cut], ALONG_Y), swap(by_y[..., cut:], ALONG_X)


def with_other_core(own, by_x, by_y, low, high, distances, first):
    sides = jnp.stack([own, by_x, by_y])
    across = jnp.concatenate([low, high], axis=-1)
    parts = []
    for array, steps in ((sides, (0, 1, 2)), (across, (3,))):
        if len(steps) > 1:
            entries = [((n, k), 4 * d + step) for n, step in enumerate(steps) for k, d in enumerate(distances)]
        else:
            entries = [((k,), 4 * d + 3) for k, d in enumerate(distances)]
        parts.append(Part(array, entries, first, True))
        parts.append(Part(swap(array, CORE), entries, first, False))
    return parts


def direct_line(levels):
    return [swap(levels[k], ALONG_Z * k) for k in (1, 2, 3)]


def half_line(levels):
    return swap(levels[2:], MIDDLE)


def line_end(levels, came):
    return swap(total(levels[1], came[0]).astype(BF), ALONG_Z)


def line_sum(levels, came, last):
    return total(levels[0], came[1], last)


def along_both(low, high):
    return swap(low, ALONG_Y), swap(high, ALONG_X)


def line_ends(levels):
    return [swap_from(levels[k], ALONG_Z, (0, 3)) for k in (3, 2)]


def line_middles(levels, ends):
    return [
        swap_from(total(levels[2], ends[0]).astype(BF), MIDDLE, (1, 2)),
        swap_from(total(levels[3], ends[1]).astype(BF), MIDDLE, (1, 2)),
    ]


def line_last(levels, middles):
    return swap(total(levels[1], middles[0]).astype(BF), ALONG_Z)


def total(*values):
    return sum(v.astype(F32) for v in values)


class PlaneSums:
    def __init__(self, *pairs):
        self.pairs = [[v.reshape(4, 4, SLAB, v.shape[-1]) for v in pair] for pair in pairs]
        self.columns = sum(pair[0].shape[-1] for pair in pairs)
        self.cut = self.columns // 256 * 128

    def pair(self, step, first=0, last=None):
        last = self.columns if last is None else last
        pieces = []
        begin = 0
        for pair in self.pairs:
            end = begin + pair[0].shape[-1]
            low, high = max(first, begin) - begin, min(last, end) - begin
            if low < high:
                pieces.append(total(*[v[:, step, :, low:high] for v in pair]))
            begin = end
        return pieces[0] if len(pieces) == 1 else jnp.concatenate(pieces, axis=-1)

    def diagonals(self):
        return self.pair(3, 0, self.cut).astype(BF), self.pair(3, self.cut).astype(BF)

    def sides(self, low, high):
        room = [(0, 0)] * 2
        low = jnp.pad(low, room + [(0, self.columns - self.cut)])
        high = jnp.pad(high, room + [(self.cut, 0)])
        return (self.pair(1) + low.astype(F32)).astype(BF), (self.pair(2) + high.astype(F32)).astype(BF)

    def levels(self, by_x, by_y):
        return (self.pair(0) + total(by_x, by_y)).astype(BF)


def by_half(core, mine, other, axis):
    return jnp.where(
        core == 0, jnp.concatenate([mine, other], axis=axis), jnp.concatenate([other, mine], axis=axis)
    )


def own_rows(names, share):
    core, _ = place()
    widths = {"qkv": 1152, "out": 384, "up": 1536, "down": 1536, "down_by_core": 1536, "extra": 768}
    pieces = []
    start = 0
    for name in names:
        piece = share[:, start : start + widths[name]]
        start += widths[name]
        if name in ("down", "extra"):
            m = widths[name] // 2
            mine, theirs = [lax.dynamic_slice_in_dim(piece, side * m, m, 1) for side in (core, 1 - core)]
            if name == "down":
                mine, theirs = [jnp.concatenate([v[:, :HALF], v[:, HALF:]], axis=0) for v in (mine, theirs)]
        else:
            mine, theirs = [lax.dynamic_slice_in_dim(piece, side * 24, 24, 0) for side in (core, 1 - core)]
        pieces.append((mine, theirs))
    sizes = [theirs.shape for _, theirs in pieces]
    packed = jnp.concatenate([theirs.astype(BF).reshape(24, -1) for _, theirs in pieces], axis=1)
    came = swap(packed, CORE)
    outs = []
    start = 0
    for (mine, _), (rows, columns) in zip(pieces, sizes):
        count = rows * columns // 24
        other = came[:, start : start + count].reshape(rows, columns).astype(F32)
        start += count
        outs.append((mine, other))
    for n, name in enumerate(names):
        if name == "down_by_core":
            outs[n] = [jnp.concatenate(jnp.split(v, 4, axis=1), axis=0) for v in outs[n]]
    return [by_half(core, mine, other, 1) for mine, other in outs]


def small_maps(layer):
    device = np.full(ROW_LENGTH, -1, np.int32)
    inner = np.full(ROW_LENGTH, -1, np.int32)

    def put(at, count, each, begin):
        spots = np.arange(count)
        device[at : at + count] = spots // each
        inner[at : at + count] = begin + spots % each

    for n, name in enumerate(WIDE_SMALLS):
        put(SPOTS[name], WIDTH, 24, 24 * n)
    put(BIAS_AT, 2 * WIDTH, 48, 144)
    for array in (device, inner):
        array[BIAS_AT + 2 * WIDTH : BIAS_AT + 3 * WIDTH] = array[BIAS_AT + WIDTH : BIAS_AT + 2 * WIDTH]
        array[BIAS_AT + WIDTH : BIAS_AT + 2 * WIDTH] = -1
    put(UP_AT, HIDDEN, 96, 192)
    if layer == 1:
        block, there, at = np.unravel_index(np.arange(HIDDEN), (4, TUNED, 24))
        device[UP_AT:], inner[UP_AT:] = there, 192 + 24 * block + at
    return device, inner


WIDE_SMALLS = ("out_b", "gain_a", "shift_a", "down_b", "gain_b", "shift_b")
GRAD_ORDER = ("up", "down_b", "gain_b", "shift_b", "query", "value", "out_b", "gain_a", "shift_a")


def grad_maps(layer):
    device, inner = small_maps(layer)
    pieces = {"up": (UP_AT, HIDDEN), "query": (BIAS_AT, WIDTH), "value": (BIAS_AT + 2 * WIDTH, WIDTH)}
    pieces.update({name: (at, WIDTH) for name, at in SPOTS.items()})
    order = np.concatenate([np.arange(at, at + count) for at, count in (pieces[name] for name in GRAD_ORDER)])
    return device[order], inner[order]


def spread_smalls(gathered, layer):
    device, inner = small_maps(layer)
    hot = (jnp.arange(HALF, dtype=jnp.int32)[:, None] == inner[None, :]).astype(BF)
    wide = jnp.dot(gathered, hot, preferred_element_type=F32)
    mine = jnp.arange(TUNED, dtype=jnp.int32)[:, None] == device[None, :]
    return jnp.sum(jnp.where(mine, wide, 0.0), axis=0, keepdims=True)


def collect_smalls(row, layer):
    device, inner = grad_maps(layer)
    mine = jnp.arange(TUNED, dtype=jnp.int32)[:, None] == device[None, :]
    masked = jnp.where(mine, row.astype(BF), jnp.zeros((), BF))
    hot = (inner[:, None] == jnp.arange(HALF, dtype=jnp.int32)[None, :]).astype(BF)
    return jnp.dot(masked, hot, preferred_element_type=F32).astype(BF)


gate = lax.optimization_barrier


def tuned(
    embedded,
    doc_ids,
    step_ids,
    step_table,
    qkv_weight,
    qv_bias,
    out_weight,
    out_bias,
    first_gain,
    first_shift,
    up_weight,
    up_bias,
    down_weight,
    down_bias,
    second_gain,
    second_shift,
    cotangent,
):
    core, chip = place()
    docs = doc_ids[0]
    doc_count = step_ids.shape[1]
    steps = step_ids[0]
    smalls = (out_bias, first_gain, first_shift, down_bias, second_gain, second_shift, qv_bias, up_bias)
    small_rows = jnp.pad(jnp.concatenate(smalls, axis=1), ((0, 0), (0, HALF - 288))).reshape(1, 2 * HALF)
    extra = jnp.concatenate([step_table, jnp.pad(small_rows, ((0, 15), (0, 0)))], axis=0)
    down_blocks = [down_weight[1][24 * b : 24 * b + 24] for b in range(4)]
    up_order = up_weight[1].reshape(24, TUNED, 4, 24).transpose(0, 2, 1, 3).reshape(24, HIDDEN)
    upper_share = jnp.concatenate([qkv_weight[1], out_weight[1], up_order] + down_blocks, axis=1)
    lower_share = chip_share(
        {"qkv": qkv_weight[0], "out": out_weight[0], "up": up_weight[0], "down": down_weight[0]}, extra
    )
    starts = {"qkv": 0, "out": 1152, "up": 1536, "down": 3072, "extra": 4608}
    upper_starts = {"qkv": 0, "out": 3 * WIDTH, "up": 4 * WIDTH, "down": 8 * WIDTH}
    upper = lax.all_gather(upper_share, "dp", axis=0, tiled=True)

    block1, block3_middle = line_first(lower_share)
    second_middle, second_end = line_second(block1, block3_middle)
    third_end = line_third(second_middle)
    blocks = [lower_share, block1, by_place(second_middle, second_end), by_place(block3_middle, third_end)]
    parts = []
    for distance, block in enumerate(blocks):
        by_x, by_y = along_each(block, block)
        plane = jnp.stack([block, by_x, by_y, jnp.concatenate(diagonal(by_x, by_y), axis=1)])
        entries = [((step,), 4 * distance + step, 0) for step in range(4)]
        parts += [Part(plane, entries, True), Part(swap(plane, CORE), entries, False)]
    source0, source1 = Source(parts, starts), Source(upper, upper_starts)

    all_extra = lay_extra(source0)
    small_all = all_extra[32::SLAB].reshape(16, 2, 2, HALF).transpose(1, 0, 2, 3).reshape(2, TUNED, HALF)
    rows = [spread_smalls(small_all[layer], layer) for layer in range(2)]
    owner = steps // 32
    row_of = (owner // 2) * SLAB + steps % 32
    row_hot = (row_of[:, None] == jnp.arange(16 * SLAB, dtype=jnp.int32)[None, :]).astype(BF)
    both_rows = jnp.dot(row_hot, all_extra, preferred_element_type=F32).reshape(doc_count, 2, 2, HALF)
    doc_rows = jnp.where((owner % 2 == 0)[:, None, None], both_rows[:, :, 0], both_rows[:, :, 1])
    doc_rows = doc_rows.reshape(doc_count, WIDTH)
    of_doc = [(docs == s)[:, None] for s in range(doc_count)]
    start = embedded.astype(F32) + sum(jnp.where(of_doc[s], doc_rows[s][None], 0.0) for s in range(doc_count))

    start, rows = gate((start, rows))
    packed0, mixed0, middle0, between = layer_forward(start, rows[0], docs, [source0])

    kept_m, sent_m, mid1, small_mlp1, packed1, mixed1, block_output = mlp_backward(
        between, cotangent, rows[1], [source1], docs
    )
    came_m = swap(sent_m, CORE)
    kept_t, sent_t, in1, small_attn1 = attn_backward(
        between, mid1, packed1, mixed1, rows[1], docs, [source1], None
    )
    in1, came_m, sent_t = gate((in1, came_m, sent_t))
    sums_m = PlaneSums((kept_m, came_m))
    in1, to_go, sent_t = gate((in1, sums_m.diagonals(), sent_t))
    low_m = along_both(*to_go)
    came_t = swap(sent_t, CORE)
    kept_b, sent_b, mid0, small_mlp0 = mlp_backward(middle0, in1, rows[0], [source0])
    mid0, low_m, came_t, sent_b = gate((mid0, low_m, came_t, sent_b))
    came_b = swap(sent_b, CORE)
    sums_t = PlaneSums((kept_t, came_t))
    low_t = along_both(*sums_t.diagonals())
    x_m = along_each(*sums_m.sides(*low_m))
    mid0, to_go, small_mlp1, small_attn1 = gate((mid0, sums_t.sides(*low_t), small_mlp1, small_attn1))
    x_t = along_each(*to_go)
    kept_c, sent_c, input_grad, small_attn0 = attn_backward(
        start, mid0, packed0, mixed0, rows[0], docs, [source0], step_ids
    )
    input_grad, came_b, kept_c, sent_c, small_attn0 = gate((input_grad, came_b, kept_c, sent_c, small_attn0))
    sums_b = PlaneSums((kept_b, came_b))
    small_grads = jnp.stack(
        [
            collect_smalls(jnp.concatenate([small_mlp0, small_attn0], axis=1), 0),
            collect_smalls(jnp.concatenate([small_mlp1, small_attn1], axis=1), 1),
        ]
    ).reshape(2, 16, 2 * HALF)
    small_grads = small_grads[:, chip ^ jnp.arange(16, dtype=jnp.int32)][:, :, None]
    small_grads = jnp.pad(small_grads, ((0, 0), (0, 0), (0, 15), (0, 0)))
    kept_c, sent_c = [
        lax.dynamic_update_slice(
            v, lax.dynamic_index_in_dim(small_grads, side, 0, keepdims=False), (0, 32, 1536)
        )
        for v, side in ((kept_c, core), (sent_c, 1 - core))
    ]
    x_m, x_t, to_go, kept_c, sent_c = gate((x_m, x_t, sums_b.diagonals(), kept_c, sent_c))

    low_b = along_both(*to_go)
    came_c = swap(sent_c, CORE)
    x_m, x_t, came_c = gate((x_m, x_t, came_c))
    sums_c = PlaneSums((kept_c, came_c))
    to_go = sums_c.diagonals()
    low_c = along_both(*to_go)
    levels_m = sums_m.levels(*x_m)
    half_m = half_line(levels_m)
    low_b, to_go = gate((low_b, to_go))
    x_b = along_each(*sums_b.sides(*low_b))
    low_c, half_m = gate((low_c, half_m))
    x_c = along_each(*sums_c.sides(*low_c))
    levels_t = sums_t.levels(*x_t)
    half_t = half_line(levels_t)
    levels_a = jnp.concatenate([levels_m, levels_t], axis=-1)
    half_a = jnp.concatenate([half_m, half_t], axis=-1)
    levels_b = sums_b.levels(*x_b)
    half_b = half_line(levels_b)
    levels_b, half_a = gate((levels_b, half_a))
    last_a = line_end(levels_a, half_a)
    half_b, last_a = gate((half_b, last_a))
    last_b = line_end(levels_b, half_b)
    levels_c = sums_c.levels(*x_c)
    back_c = [swap(levels_c[k], ALONG_Z * k) for k in (1, 2, 3)]
    up_1, down_1, qkv_1, out_1 = own_rows(
        ("up", "down_by_core", "qkv", "out"), line_sum(levels_a, half_a, last_a)
    )
    up_1 = up_1.reshape(24, 4, TUNED, 24).transpose(0, 2, 1, 3).reshape(24, HIDDEN)
    up_0, down_0 = own_rows(("up", "down"), line_sum(levels_b, half_b, last_b))
    up, down = jnp.stack([up_0, up_1]), jnp.stack([down_0, down_1])
    up, down, qkv_1, out_1, back_c = gate((up, down, qkv_1, out_1, back_c))
    sum_c = total(levels_c[0], *back_c)
    qkv_0, out_0, extra_0 = own_rows(("qkv", "out", "extra"), sum_c)
    small_out = extra_0[32].reshape(2, HALF)
    out_b, gain_a, shift_a, down_b, gain_b, shift_b = [small_out[:, n * 24 : n * 24 + 24] for n in range(6)]
    return (
        block_output,
        input_grad,
        extra_0[:32],
        jnp.stack([qkv_0, qkv_1]),
        small_out[:, 144:192],
        jnp.stack([out_0, out_1]),
        out_b,
        gain_a,
        shift_a,
        up,
        small_out[:, 192:288],
        down,
        down_b,
        gain_b,
        shift_b,
    )


def shortened(value):
    return jax.tree.map(lambda a: a.astype(jnp.bfloat16) if a.dtype == jnp.float32 else a, value)


def partner(value, axis, stride):
    return lax.ppermute(value, axis, [(i, i ^ 1 << stride) for i in range(lax.axis_size(axis))])


def norm_rows(hidden, gain_vec, shift_vec):
    average = jnp.mean(hidden, axis=-1, keepdims=True)
    centred = hidden - average
    variance = jnp.mean(centred * centred, axis=-1, keepdims=True)
    inverse = lax.rsqrt(variance + EPSILON)
    unit_rows = centred * inverse
    normed = unit_rows * gain_vec.astype(jnp.float32) + shift_vec.astype(jnp.float32)
    return (normed, unit_rows, inverse)


def norm_back(grad_rows, unit_rows, inverse, gain_vec):
    scaled = grad_rows * gain_vec.astype(jnp.float32)
    first_mean = jnp.mean(scaled, axis=-1, keepdims=True)
    second_mean = jnp.mean(scaled * unit_rows, axis=-1, keepdims=True)
    return inverse * (scaled - first_mean - unit_rows * second_mean)


def smooth_gate(lifted):
    return jax.nn.gelu(lifted, approximate=True)


def halving_sum(members, send_fn):
    levels = lax.axis_size("dp").bit_length() - 1
    position = lax.axis_index("dp")
    current = tuple(members)
    for level in range(levels - 1, -1, -1):
        upper_side = position // (1 << level) % 2 == 1
        kept_list = []
        sent_list = []
        for member in current:
            half = member.shape[0] // 2
            lower_part = member[:half]
            upper_part = member[half:]
            kept_list.append(jnp.where(upper_side, upper_part, lower_part))
            sent_list.append(jnp.where(upper_side, lower_part, upper_part))
        received = send_fn(tuple(sent_list), level)
        current = tuple((kept + came for kept, came in zip(kept_list, received)))
    return current


def layer_apply(hidden, params, same_doc):
    qkv_w, qv_b, out_w, out_b, gain_a, shift_a, up_w, up_b, down_w, down_b, gain_b, shift_b = params
    width = out_w.shape[0]
    tok_count = hidden.shape[0]
    scale = 1.0 / math.sqrt(HEAD_DIM)
    normed_a, unit_a, inverse_a = norm_rows(hidden, gain_a, shift_a)
    normed_a = normed_a.astype(jnp.bfloat16)
    qv_float = qv_b.astype(jnp.float32)
    bias_full = jnp.concatenate(
        [qv_float[:width], jnp.zeros((width,), jnp.float32), qv_float[width:]]
    )
    packed = (jnp.dot(normed_a, qkv_w, preferred_element_type=jnp.float32) + bias_full).astype(
        jnp.bfloat16
    )
    queries = packed[:, :width].reshape(tok_count, HEADS, HEAD_DIM)
    key_rows = packed[:, width : 2 * width].reshape(tok_count, HEADS, HEAD_DIM)
    value_rows = packed[:, 2 * width :].reshape(tok_count, HEADS, HEAD_DIM)
    scores = (
        jnp.einsum("qhd,khd->hqk", queries, key_rows, preferred_element_type=jnp.float32) * scale
    )
    masked = jnp.where(same_doc[None], scores, -1e30)
    top_score = jnp.max(masked, axis=-1, keepdims=True)
    expo_rows = jnp.exp(masked - top_score)
    probs = expo_rows / jnp.sum(expo_rows, axis=-1, keepdims=True)
    probs_low = probs.astype(jnp.bfloat16)
    mixed = jnp.einsum("hqk,khd->qhd", probs_low, value_rows, preferred_element_type=jnp.float32)
    mixed = mixed.reshape(tok_count, width).astype(jnp.bfloat16)
    middle = (
        hidden
        + jnp.dot(mixed, out_w, preferred_element_type=jnp.float32)
        + out_b.astype(jnp.float32)
    )
    normed_b, unit_b, inverse_b = norm_rows(middle, gain_b, shift_b)
    normed_b = normed_b.astype(jnp.bfloat16)
    lifted = jnp.dot(normed_b, up_w, preferred_element_type=jnp.float32) + up_b.astype(jnp.float32)
    activated = smooth_gate(lifted).astype(jnp.bfloat16)
    output = (
        middle
        + jnp.dot(activated, down_w, preferred_element_type=jnp.float32)
        + down_b.astype(jnp.float32)
    )
    saved = (
        unit_a,
        inverse_a,
        normed_a,
        queries,
        key_rows,
        value_rows,
        probs,
        probs_low,
        mixed,
        unit_b,
        inverse_b,
        normed_b,
        lifted,
        activated,
    )
    return (output, saved)


def layer_back(hidden, params, same_doc, grad_top):
    qkv_w, qv_b, out_w, out_b, gain_a, shift_a, up_w, up_b, down_w, down_b, gain_b, shift_b = params
    unused_output, saved = layer_apply(hidden, params, same_doc)
    (
        unit_a,
        inverse_a,
        normed_a,
        queries,
        key_rows,
        value_rows,
        probs,
        probs_low,
        mixed,
        unit_b,
        inverse_b,
        normed_b,
        lifted,
        activated,
    ) = saved
    width = out_w.shape[0]
    tok_count = hidden.shape[0]
    scale = 1.0 / math.sqrt(HEAD_DIM)
    grad_down = grad_top.astype(jnp.bfloat16)
    down_b_grad = jnp.sum(grad_down.astype(jnp.float32), axis=0)
    down_w_grad = jnp.einsum("tf,td->fd", activated, grad_down, preferred_element_type=jnp.float32)
    grad_act = jnp.einsum("td,fd->tf", grad_down, down_w, preferred_element_type=jnp.float32)
    unused_gate, gate_pull = jax.vjp(smooth_gate, lifted)
    grad_lift = gate_pull(grad_act)[0].astype(jnp.bfloat16)
    up_b_grad = jnp.sum(grad_lift.astype(jnp.float32), axis=0)
    up_w_grad = jnp.einsum("td,tf->df", normed_b, grad_lift, preferred_element_type=jnp.float32)
    grad_nb = jnp.einsum("tf,df->td", grad_lift, up_w, preferred_element_type=jnp.float32)
    gain_b_grad = jnp.sum(grad_nb * unit_b, axis=0)
    shift_b_grad = jnp.sum(grad_nb, axis=0)
    grad_mid = grad_top + norm_back(grad_nb, unit_b, inverse_b, gain_b)
    grad_branch = grad_mid.astype(jnp.bfloat16)
    out_b_grad = jnp.sum(grad_branch.astype(jnp.float32), axis=0)
    out_w_grad = jnp.einsum("te,td->ed", mixed, grad_branch, preferred_element_type=jnp.float32)
    grad_mixed = jnp.einsum("td,ed->te", grad_branch, out_w, preferred_element_type=jnp.float32)
    grad_mixed = grad_mixed.astype(jnp.bfloat16).reshape(tok_count, HEADS, HEAD_DIM)
    grad_probs = jnp.einsum(
        "qhd,khd->hqk", grad_mixed, value_rows, preferred_element_type=jnp.float32
    )
    grad_values = jnp.einsum(
        "hqk,qhd->khd", probs_low, grad_mixed, preferred_element_type=jnp.float32
    )
    grad_scores = probs * (grad_probs - jnp.sum(probs * grad_probs, axis=-1, keepdims=True))
    scores_low = grad_scores.astype(jnp.bfloat16)
    grad_queries = (
        jnp.einsum("hqk,khd->qhd", scores_low, key_rows, preferred_element_type=jnp.float32) * scale
    )
    grad_keys = (
        jnp.einsum("hqk,qhd->khd", scores_low, queries, preferred_element_type=jnp.float32) * scale
    )
    grad_packed = jnp.concatenate(
        [
            grad_queries.reshape(tok_count, width),
            grad_keys.reshape(tok_count, width),
            grad_values.reshape(tok_count, width),
        ],
        axis=1,
    ).astype(jnp.bfloat16)
    packed_sums = jnp.sum(grad_packed.astype(jnp.float32), axis=0)
    qv_b_grad = jnp.concatenate([packed_sums[:width], packed_sums[2 * width :]])
    qkv_w_grad = jnp.einsum("td,te->de", normed_a, grad_packed, preferred_element_type=jnp.float32)
    grad_na = jnp.einsum("te,de->td", grad_packed, qkv_w, preferred_element_type=jnp.float32)
    gain_a_grad = jnp.sum(grad_na * unit_a, axis=0)
    shift_a_grad = jnp.sum(grad_na, axis=0)
    grad_in = grad_mid + norm_back(grad_na, unit_a, inverse_a, gain_a)
    grads = (
        qkv_w_grad,
        qv_b_grad,
        out_w_grad,
        out_b_grad,
        gain_a_grad,
        shift_a_grad,
        up_w_grad,
        up_b_grad,
        down_w_grad,
        down_b_grad,
        gain_b_grad,
        shift_b_grad,
    )
    return (grad_in, grads)


def plain(
    embedded,
    doc_ids,
    step_ids,
    step_table,
    qkv_weight,
    qv_bias,
    out_weight,
    out_bias,
    first_gain,
    first_shift,
    up_weight,
    up_bias,
    down_weight,
    down_bias,
    second_gain,
    second_shift,
    cotangent,
):
    docs_row = doc_ids[0]
    same_doc = docs_row[:, None] == docs_row[None, :]
    doc_count = step_ids.shape[1]
    doc_hot = (docs_row[:, None] == jnp.arange(doc_count, dtype=jnp.int32)[None, :]).astype(
        jnp.float32
    )
    gathered_first = (
        lax.all_gather(qkv_weight[0], "dp", axis=0, tiled=True),
        lax.all_gather(qv_bias[0], "dp", axis=0, tiled=True),
        lax.all_gather(out_weight[0], "dp", axis=0, tiled=True),
        lax.all_gather(out_bias[0], "dp", axis=0, tiled=True),
        lax.all_gather(first_gain[0], "dp", axis=0, tiled=True),
        lax.all_gather(first_shift[0], "dp", axis=0, tiled=True),
        lax.all_gather(up_weight[0], "dp", axis=0, tiled=True),
        lax.all_gather(up_bias[0], "dp", axis=0, tiled=True),
        lax.all_gather(down_weight[0], "dp", axis=0, tiled=True),
        lax.all_gather(down_bias[0], "dp", axis=0, tiled=True),
        lax.all_gather(second_gain[0], "dp", axis=0, tiled=True),
        lax.all_gather(second_shift[0], "dp", axis=0, tiled=True),
        lax.all_gather(step_table, "dp", axis=0, tiled=True),
    )
    params_lower = gathered_first[:12]
    table_whole = gathered_first[12]
    step_hot = step_ids[0][:, None] == jnp.arange(table_whole.shape[0], dtype=jnp.int32)[None, :]
    doc_rows = jnp.dot(
        step_hot.astype(jnp.bfloat16), table_whole, preferred_element_type=jnp.float32
    )
    start = embedded.astype(jnp.float32) + jnp.dot(
        doc_hot, doc_rows, precision=lax.Precision.HIGHEST
    )
    middle_hidden, unused_lower = layer_apply(start, params_lower, same_doc)
    params_upper = (
        lax.all_gather(qkv_weight[1], "dp", axis=0, tiled=True),
        lax.all_gather(qv_bias[1], "dp", axis=0, tiled=True),
        lax.all_gather(out_weight[1], "dp", axis=0, tiled=True),
        lax.all_gather(out_bias[1], "dp", axis=0, tiled=True),
        lax.all_gather(first_gain[1], "dp", axis=0, tiled=True),
        lax.all_gather(first_shift[1], "dp", axis=0, tiled=True),
        lax.all_gather(up_weight[1], "dp", axis=0, tiled=True),
        lax.all_gather(up_bias[1], "dp", axis=0, tiled=True),
        lax.all_gather(down_weight[1], "dp", axis=0, tiled=True),
        lax.all_gather(down_bias[1], "dp", axis=0, tiled=True),
        lax.all_gather(second_gain[1], "dp", axis=0, tiled=True),
        lax.all_gather(second_shift[1], "dp", axis=0, tiled=True),
    )
    final_hidden, unused_upper = layer_apply(middle_hidden, params_upper, same_doc)
    block_output = final_hidden.astype(jnp.bfloat16)

    def weights_for(layer_index):
        return (
            lax.all_gather(qkv_weight[layer_index], "dp", axis=0, tiled=True),
            lax.all_gather(qv_bias[layer_index], "dp", axis=0, tiled=True),
            lax.all_gather(out_weight[layer_index], "dp", axis=0, tiled=True),
            lax.all_gather(out_bias[layer_index], "dp", axis=0, tiled=True),
            lax.all_gather(first_gain[layer_index], "dp", axis=0, tiled=True),
            lax.all_gather(first_shift[layer_index], "dp", axis=0, tiled=True),
            lax.all_gather(up_weight[layer_index], "dp", axis=0, tiled=True),
            lax.all_gather(up_bias[layer_index], "dp", axis=0, tiled=True),
            lax.all_gather(down_weight[layer_index], "dp", axis=0, tiled=True),
            lax.all_gather(down_bias[layer_index], "dp", axis=0, tiled=True),
            lax.all_gather(second_gain[layer_index], "dp", axis=0, tiled=True),
            lax.all_gather(second_shift[layer_index], "dp", axis=0, tiled=True),
        )

    grad_upper_in, upper_grads = layer_back(
        middle_hidden, weights_for(1), same_doc, cotangent.astype(jnp.float32)
    )

    def send_upper(sent, level):
        return jax.tree.map(
            lambda part, own: part.astype(own.dtype), partner(shortened(sent), "dp", level), sent
        )

    upper_shards = halving_sum(upper_grads, send_upper)
    input_grad, lower_grads = layer_back(start, weights_for(0), same_doc, grad_upper_in)
    doc_grads = jnp.einsum("ts,td->sd", doc_hot, input_grad, precision=lax.Precision.HIGHEST)
    table_full_grad = jnp.einsum(
        "sn,sd->nd", step_hot.astype(jnp.float32), doc_grads, precision=lax.Precision.HIGHEST
    )

    def send_lower(sent, level):
        return jax.tree.map(
            lambda part, own: part.astype(own.dtype), partner(shortened(sent), "dp", level), sent
        )

    lower_all = halving_sum(tuple(lower_grads) + (table_full_grad,), send_lower)
    lower_shards = lower_all[:12]
    table_shard = lower_all[12]
    stacked = [jnp.stack([lower_shards[index], upper_shards[index]], axis=0) for index in range(12)]
    return (
        block_output,
        input_grad,
        table_shard,
        stacked[0],
        stacked[1],
        stacked[2],
        stacked[3],
        stacked[4],
        stacked[5],
        stacked[6],
        stacked[7],
        stacked[8],
        stacked[9],
        stacked[10],
        stacked[11],
    )


def solution(mesh):
    local = tuned if mesh.shape["dp"] == TUNED else plain
    in_specs = (
        P("dp", None),
        P("dp", None),
        P("dp", None),
        P("dp", None),
        P(None, "dp", None),
        P(None, "dp"),
        P(None, "dp", None),
        P(None, "dp"),
        P(None, "dp"),
        P(None, "dp"),
        P(None, "dp", None),
        P(None, "dp"),
        P(None, "dp", None),
        P(None, "dp"),
        P(None, "dp"),
        P(None, "dp"),
        P("dp", None),
    )
    out_specs = (
        P("dp", None),
        P("dp", None),
        P("dp", None),
        P(None, "dp", None),
        P(None, "dp"),
        P(None, "dp", None),
        P(None, "dp"),
        P(None, "dp"),
        P(None, "dp"),
        P(None, "dp", None),
        P(None, "dp"),
        P(None, "dp", None),
        P(None, "dp"),
        P(None, "dp"),
        P(None, "dp"),
    )
    return jax.shard_map(local, mesh=mesh, in_specs=in_specs, out_specs=out_specs, check_vma=False)
```

```python
import math

import jax
import jax.numpy as jnp
import numpy as np
from jax import lax
from jax.experimental import pallas as pl
from jax.experimental.pallas import tpu as pltpu
from jax.sharding import PartitionSpec as P

HEADS = 12
HEAD_DIM = 64
EPSILON = 1e-05
BF = jnp.bfloat16
F32 = jnp.float32

TUNED = 32
CORE, ALONG_X, ALONG_Y, ALONG_Z, MIDDLE = 1, 2, 4, 8, 24
SLAB = 48
HALF = 384


def swap(value, stride):
    return lax.ppermute(value, "dp", [(i, i ^ stride) for i in range(TUNED)])


def swap_from(value, stride, zs):
    return lax.ppermute(value, "dp", [(i, i ^ stride) for i in range(TUNED) if i // 8 in zs])


def after(done, waiting):
    return lax.optimization_barrier((done, waiting))


def place():
    index = lax.axis_index("dp")
    return index % 2, index // 2


WIDTH = HEADS * HEAD_DIM
HIDDEN = 4 * WIDTH
PAIR = 2 * HEAD_DIM
ANY = pl.BlockSpec(memory_space=pl.ANY)
WHOLE = pl.BlockSpec(memory_space=pltpu.VMEM)
ATTN = {"qkv": 1152, "out": 384}
MLP = {"up": 1536, "down": 1536}
SHAPES = {"qkv": (768, 2304), "out": (768, 768), "up": (768, 3072), "down": (3072, 768), "extra": (768, 1536)}


SPOTS = {"gain_a": 0, "shift_a": 768, "out_b": 1536, "gain_b": 2304, "shift_b": 3072, "down_b": 3840}
BIAS_AT, UP_AT, ROW_LENGTH = 4608, 6912, 9984


def spot(ref, name):
    return ref[:, SPOTS[name] : SPOTS[name] + WIDTH]


class Part:
    def __init__(self, array, entries, own):
        self.array, self.entries, self.own = array, entries, own


class Source:
    def __init__(self, weights, starts):
        self.weights, self.starts = weights, starts
        self.natural = not isinstance(weights, list)
        self.arrays = [weights] if self.natural else [part.array for part in weights]


def fetch_parts(parts, refs, starts, targets, sems):
    index = lax.axis_index("dp")
    core, chip = index % 2, index // 2
    for part, ref in zip(parts, refs):
        half = core if part.own else 1 - core
        for leading, code, first in part.entries:
            last = first + part.array.shape[-1]
            there = chip ^ code
            for name, target in targets.items():
                begin = starts[name]
                if name == "down":
                    pieces = [(begin + block * HALF, HALF, block) for block in range(4)]
                else:
                    pieces = [(begin, target.shape[1] // 2, None)]
                for start, width, block in pieces:
                    low, high = max(start, first), min(start + width, last)
                    if low >= high:
                        continue
                    columns = pl.ds(pl.multiple_of(half * width + (low - start), 128), high - low)
                    row = there * SLAB if block is None else there * (4 * SLAB) + block * SLAB
                    pltpu.make_async_copy(
                        ref.at[leading + (slice(None), pl.ds(low - first, high - low))],
                        target.at[pl.ds(pl.multiple_of(row, SLAB), SLAB), columns],
                        sems[name],
                    ).start()


def start_fetch(sources, refs, targets, sems):
    for source in sources:
        own, refs = refs[: len(source.arrays)], refs[len(source.arrays) :]
        wanted = {name: targets[name] for name in source.starts if name in targets}
        if not source.natural:
            fetch_parts(source.weights, own, source.starts, wanted, sems)
            continue
        for name, target in wanted.items():
            pieces = [(0, slice(None), target.shape[1])]
            if name == "down":
                pieces = [(b * WIDTH, pl.ds(b * WIDTH, WIDTH), WIDTH) for b in range(4)]
            for shift, rows, width in pieces:
                pltpu.make_async_copy(
                    own[0].at[:, pl.ds(source.starts[name] + shift, width)], target.at[rows, :], sems[name]
                ).start()


def arrays_of(sources):
    return [array for source in sources for array in source.arrays]


def arrived(target, sem):
    pltpu.make_async_copy(target, target, sem).wait()


def dot(left, right, contract):
    return lax.dot_general(left, right, ((contract[:1], contract[1:]), ((), ())), preferred_element_type=F32)


def unit_of(hidden):
    average = jnp.mean(hidden, axis=-1, keepdims=True)
    centred = hidden - average
    inverse = lax.rsqrt(jnp.mean(centred * centred, axis=-1, keepdims=True) + EPSILON)
    return centred * inverse, inverse


def back_of_norm(grad_rows, unit_rows, inverse, gain):
    scaled = grad_rows * gain
    first_mean = jnp.mean(scaled, axis=-1, keepdims=True)
    second_mean = jnp.mean(scaled * unit_rows, axis=-1, keepdims=True)
    return inverse * (scaled - first_mean - unit_rows * second_mean)


def gelu_pair(value):
    factor = math.sqrt(2.0 / math.pi)
    square = value * value
    bend = jnp.tanh(factor * value * (1.0 + 0.044715 * square))
    half_up = 0.5 * (1.0 + bend)
    slope = half_up + 0.5 * value * (1.0 - bend * bend) * factor * (1.0 + 3.0 * 0.044715 * square)
    return value * half_up, slope


def softmax_rows(query, keys, same):
    scores = dot(query, keys, (1, 1)) * (1.0 / math.sqrt(HEAD_DIM))
    masked = jnp.where(same, scores, -1e30)
    expo = jnp.exp(masked - jnp.max(masked, axis=-1, keepdims=True))
    return expo * (1.0 / jnp.sum(expo, axis=-1, keepdims=True))


def head_lanes(count):
    return lax.broadcasted_iota(jnp.int32, (count, PAIR), 1) < HEAD_DIM


def pair_slice(pair, block):
    return pl.ds(pl.multiple_of(block * WIDTH + pair * PAIR, PAIR), PAIR)


def attn_steps(hidden, row_ref, docs_refs, packed_ref, mixed_ref, qkv_ref, out_ref, named):
    unit, _ = unit_of(hidden)
    normed = (unit * spot(row_ref, "gain_a") + spot(row_ref, "shift_a")).astype(BF)
    arrived(qkv_ref, named["qkv"])
    for block in range(3):
        columns = slice(block * WIDTH, (block + 1) * WIDTH)
        packed_ref[:, columns] = (
            dot(normed, qkv_ref[:, columns], (1, 0))
            + row_ref[:, BIAS_AT + block * WIDTH : BIAS_AT + (block + 1) * WIDTH]
        ).astype(BF)
    same = docs_refs[0][...] == docs_refs[1][...]
    first_head = head_lanes(hidden.shape[0])
    for pair in range(HEADS // 2):
        query, keys, values = [packed_ref[:, pair_slice(pair, block)] for block in range(3)]
        blank = jnp.zeros_like(query)
        mixes = []
        for own in (jnp.where(first_head, query, blank), jnp.where(first_head, blank, query)):
            mixes.append(dot(softmax_rows(own, keys, same).astype(BF), values, (1, 0)))
        mixed_ref[:, pair_slice(pair, 0)] = jnp.where(first_head, mixes[0], mixes[1]).astype(BF)
    arrived(out_ref, named["out"])
    return hidden + dot(mixed_ref[...], out_ref[...], (1, 0)) + spot(row_ref, "out_b")


def layer_forward(hidden, row, docs, sources):
    arrays = arrays_of(sources)
    tokens = hidden.shape[0]
    names = ("qkv", "out", "up", "down")

    def body(hidden_ref, row_ref, down_docs, across_docs, *rest):
        refs, rest = rest[: len(arrays)], rest[len(arrays) :]
        saved_at, top_ref = rest[:3], rest[3]
        targets, sems, saved = dict(zip(names, rest[4:8])), rest[8], rest[9:]
        packed_ref, mixed_ref, middle_ref = saved
        named = {name: sems.at[n] for n, name in enumerate(names)}
        start_fetch(sources, refs, targets, named)
        middle = attn_steps(
            hidden_ref[...],
            row_ref,
            (down_docs, across_docs),
            packed_ref,
            mixed_ref,
            targets["qkv"],
            targets["out"],
            named,
        )
        middle_ref[...] = middle
        writes = [pltpu.make_async_copy(a, b, sems.at[4 + n]) for n, (a, b) in enumerate(zip(saved, saved_at))]
        for write in writes:
            write.start()
        unit, _ = unit_of(middle)
        normed = (unit * spot(row_ref, "gain_b") + spot(row_ref, "shift_b")).astype(BF)
        total = middle + spot(row_ref, "down_b")
        up_ref, down_ref = targets["up"], targets["down"]
        arrived(up_ref, named["up"])
        arrived(down_ref, named["down"])
        for tile in range(4):
            columns = slice(tile * WIDTH, (tile + 1) * WIDTH)
            lifted = dot(normed, up_ref[:, columns], (1, 0))
            lifted = lifted + row_ref[:, UP_AT + tile * WIDTH : UP_AT + (tile + 1) * WIDTH]
            active, _ = gelu_pair(lifted)
            total = total + dot(active.astype(BF), down_ref[columns, :], (1, 0))
        top_ref[...] = total
        for write in writes:
            write.wait()

    return pl.pallas_call(
        body,
        out_shape=[
            jax.ShapeDtypeStruct((tokens, 3 * WIDTH), BF),
            jax.ShapeDtypeStruct((tokens, WIDTH), BF),
            jax.ShapeDtypeStruct((tokens, WIDTH), F32),
            jax.ShapeDtypeStruct((tokens, WIDTH), F32),
        ],
        in_specs=[WHOLE] * 4 + [ANY] * len(arrays),
        out_specs=[ANY] * 3 + [WHOLE],
        scratch_shapes=[pltpu.VMEM(SHAPES[name], BF) for name in names]
        + [pltpu.SemaphoreType.DMA((7,))]
        + [pltpu.VMEM((tokens, 3 * WIDTH), BF), pltpu.VMEM((tokens, WIDTH), BF), pltpu.VMEM((tokens, WIDTH), F32)],
        compiler_params=pltpu.CompilerParams(vmem_limit_bytes=50 * 2**20),
        cost_estimate=pl.CostEstimate(flops=1, bytes_accessed=1, transcendentals=1),
        name="layer_forward",
    )(hidden, row, docs.reshape(-1, 1), docs.reshape(1, -1), *arrays)


def send_rows(source, rows, columns, targets, half, first, sem):
    index = lax.axis_index("dp")
    core, chip = index % 2, index // 2
    for side, target in enumerate(targets):

        @pl.when(core == half ^ side)
        def _(target=target):
            for there, row in rows:
                pltpu.make_async_copy(
                    source.at[pl.ds(row, SLAB), columns],
                    target.at[chip ^ there, :, pl.ds(first, columns.size)],
                    sem,
                ).start()


def mlp_backward(hidden, grad_top, row, sources, docs=None):
    natural = any(source.natural and "down" in source.starts for source in sources)
    arrays = arrays_of(sources)
    tokens = hidden.shape[0]
    whole_layer = docs is not None
    names = ("up", "down", "qkv", "out") if whole_layer else ("up", "down")
    doc_operands = [docs.reshape(-1, 1), docs.reshape(1, -1)] if whole_layer else []

    def body(hidden_ref, grad_ref, row_ref, *rest):
        docs_refs, rest = rest[: len(doc_operands)], rest[len(doc_operands) :]
        refs, rest = rest[: len(arrays)], rest[len(arrays) :]
        grads_ref, (mid_ref, small_ref), rest = rest[:2], rest[2:4], rest[4:]
        if whole_layer:
            (packed_at, mixed_at, top_ref), (packed_ref, mixed_ref), rest = rest[:3], rest[-2:], rest[3:-2]
        targets, (up_stage, down_stage, sems) = dict(zip(names, rest[:-3])), rest[-3:]
        named = {name: sems.at[n] for n, name in enumerate(names)}
        up_sem, down_sem = sems.at[4], sems.at[5]
        up_ref, down_ref = targets["up"], targets["down"]
        start_fetch(sources, refs, targets, named)
        middle = hidden_ref[...]
        if whole_layer:
            middle = attn_steps(
                middle, row_ref, docs_refs, packed_ref, mixed_ref, targets["qkv"], targets["out"], named
            )
            writes = [
                pltpu.make_async_copy(packed_ref, packed_at, sems.at[6]),
                pltpu.make_async_copy(mixed_ref, mixed_at, sems.at[7]),
            ]
            for write in writes:
                write.start()
        unit, inverse = unit_of(middle)
        normed = unit * spot(row_ref, "gain_b") + spot(row_ref, "shift_b")
        normed_turned = normed.T.astype(BF)
        normed = normed.astype(BF)
        grad_top_rows = grad_ref[...].astype(F32)
        grad_down = grad_top_rows.astype(BF)
        small_ref[:, HIDDEN : HIDDEN + WIDTH] = jnp.sum(grad_down.astype(F32), axis=0, keepdims=True)
        grad_nb = jnp.zeros((tokens, WIDTH), F32)
        total = middle + spot(row_ref, "down_b") if whole_layer else None
        arrived(up_ref, named["up"])
        arrived(down_ref, named["down"])
        for tile in range(4):
            columns = slice(tile * WIDTH, (tile + 1) * WIDTH)
            lifted = dot(normed, up_ref[:, columns], (1, 0))
            lifted = lifted + row_ref[:, UP_AT + tile * WIDTH : UP_AT + (tile + 1) * WIDTH]
            active, slope = gelu_pair(lifted)
            active = active.astype(BF)
            if whole_layer:
                total = total + dot(active, down_ref[columns, :], (1, 0))
            grad_act = dot(grad_down, down_ref[columns, :], (1, 1))
            grad_lift = (grad_act * slope).astype(BF)
            small_ref[:, columns] = jnp.sum(grad_lift.astype(F32), axis=0, keepdims=True)
            grad_nb = grad_nb + dot(grad_lift, up_ref[:, columns], (1, 1))
            up_stage[:, columns] = dot(normed_turned, grad_lift, (1, 0)).astype(BF)
            down_stage[columns, :] = dot(active, grad_down, (0, 0)).astype(BF)
            send_rows(
                up_stage,
                [(there, there * SLAB) for there in range(16)],
                pl.ds(tile * WIDTH, WIDTH),
                grads_ref,
                tile // 2,
                tile % 2 * WIDTH,
                up_sem,
            )
            if natural:
                pieces = [(tile, [(there, tile * WIDTH + there * SLAB) for there in range(16)])]
            else:
                chips = range(4 * tile, 4 * tile + 4)
                pieces = [(b, [(there, there * 4 * SLAB + b * SLAB) for there in chips]) for b in range(4)]
            for half in range(2):
                for block, rows in pieces:
                    send_rows(
                        down_stage,
                        rows,
                        pl.ds(half * HALF, HALF),
                        grads_ref,
                        half,
                        4 * HALF + block * HALF,
                        down_sem,
                    )
        if whole_layer:
            top_ref[...] = total.astype(BF)
            for write in writes:
                write.wait()
        small_ref[:, HIDDEN + WIDTH : HIDDEN + 2 * WIDTH] = jnp.sum(grad_nb * unit, axis=0, keepdims=True)
        small_ref[:, HIDDEN + 2 * WIDTH :] = jnp.sum(grad_nb, axis=0, keepdims=True)
        mid_ref[...] = grad_top_rows + back_of_norm(grad_nb, unit, inverse, spot(row_ref, "gain_b"))
        arrived(up_stage, up_sem)
        arrived(down_stage, down_sem)

    outs = [jax.ShapeDtypeStruct((16, SLAB, HIDDEN), BF)] * 2 + [
        jax.ShapeDtypeStruct((tokens, WIDTH), F32),
        jax.ShapeDtypeStruct((1, HIDDEN + 3 * WIDTH), F32),
    ]
    if whole_layer:
        outs += [jax.ShapeDtypeStruct((tokens, count * WIDTH), BF) for count in (3, 1, 1)]
    return pl.pallas_call(
        body,
        out_shape=outs,
        in_specs=[WHOLE] * (3 + len(doc_operands)) + [ANY] * len(arrays),
        out_specs=[ANY] * 2 + [WHOLE] * 2 + ([ANY, ANY, WHOLE] if whole_layer else []),
        scratch_shapes=[pltpu.VMEM(SHAPES[name], BF) for name in names + ("up", "down")]
        + [pltpu.SemaphoreType.DMA((8,))]
        + ([pltpu.VMEM((tokens, 3 * WIDTH), BF), pltpu.VMEM((tokens, WIDTH), BF)] if whole_layer else []),
        compiler_params=pltpu.CompilerParams(vmem_limit_bytes=54 * 2**20),
        cost_estimate=pl.CostEstimate(flops=1, bytes_accessed=1, transcendentals=1),
        name="top_layer" if whole_layer else "mlp_backward",
    )(hidden, grad_top, row, *doc_operands, *arrays)


def attn_backward(hidden, grad_mid, packed, mixed, row, docs, sources, steps):
    arrays = arrays_of(sources)
    tokens = hidden.shape[0]
    scale = 1.0 / math.sqrt(HEAD_DIM)

    def body(hidden_at, packed_at, mixed_at, mid_ref, row_ref, down_docs, across_docs, *rest):
        if steps is not None:
            steps_ref, rest = rest[0], rest[1:]
        refs, rest = rest[: len(arrays)], rest[len(arrays) :]
        grads_ref, rest = rest[:2], rest[2:]
        in_ref, small_ref = rest[:2]
        qkv_ref, out_ref, qkv_stage, out_stage, gm_ref, gp_ref, sems = rest[2:9]
        hidden_ref, packed_ref, mixed_ref, rest = rest[9], rest[10], rest[11], rest[:9] + rest[12:]
        saved = [(hidden_at, hidden_ref), (mixed_at, mixed_ref), (packed_at, packed_ref)]
        saved = [pltpu.make_async_copy(*pair, sems.at[6 + n]) for n, pair in enumerate(saved)]
        for copy in saved:
            copy.start()
        named = {"qkv": sems.at[0], "out": sems.at[1]}
        start_fetch(sources, refs, {"qkv": qkv_ref, "out": out_ref}, named)
        saved[0].wait()
        unit, inverse = unit_of(hidden_ref[...])
        normed = (unit * spot(row_ref, "gain_a") + spot(row_ref, "shift_a")).astype(BF)
        grad_branch = mid_ref[...].astype(BF)
        small_ref[:, 2 * WIDTH : 3 * WIDTH] = jnp.sum(grad_branch.astype(F32), axis=0, keepdims=True)
        saved[1].wait()
        out_stage[...] = dot(mixed_ref[...], grad_branch, (0, 0)).astype(BF)
        chips = [(there, there * SLAB) for there in range(16)]
        for half in range(2):
            send_rows(out_stage, chips, pl.ds(half * HALF, HALF), grads_ref, half, 3 * HALF, sems.at[2])
        arrived(out_ref, named["out"])
        gm_ref[...] = dot(grad_branch, out_ref[...], (1, 1)).astype(BF)
        saved[2].wait()
        same = down_docs[...] == across_docs[...]
        first_head = head_lanes(tokens)

        def one_pair(pair, carry):
            query = packed_ref[:, pair_slice(pair, 0)]
            keys = packed_ref[:, pair_slice(pair, 1)]
            values = packed_ref[:, pair_slice(pair, 2)]
            grad_mixed = gm_ref[:, pair_slice(pair, 0)]
            blank = jnp.zeros_like(query)
            query_turned = query.astype(F32).T.astype(BF)
            mixed_turned = grad_mixed.astype(F32).T.astype(BF)
            by_query, by_key, by_value = [], [], []
            for head in range(2):
                rows_of = slice(head * HEAD_DIM, (head + 1) * HEAD_DIM)
                lanes = first_head if head == 0 else jnp.logical_not(first_head)
                probs = softmax_rows(jnp.where(lanes, query, blank), keys, same)
                low = probs.astype(BF)
                grad_probs = dot(jnp.where(lanes, grad_mixed, blank), values, (1, 1))
                grad_scores = probs * (grad_probs - jnp.sum(probs * grad_probs, axis=-1, keepdims=True))
                scores_low = grad_scores.astype(BF)
                by_query.append(dot(scores_low, keys, (1, 0)))
                by_key.append(dot(query_turned[rows_of], scores_low, (1, 0)))
                by_value.append(dot(mixed_turned[rows_of], low, (1, 0)))
            gp_ref[:, pair_slice(pair, 0)] = (jnp.where(first_head, *by_query) * scale).astype(BF)
            gp_ref[:, pair_slice(pair, 1)] = (jnp.concatenate(by_key, axis=0).T * scale).astype(BF)
            gp_ref[:, pair_slice(pair, 2)] = jnp.concatenate(by_value, axis=0).T.astype(BF)
            return carry

        lax.fori_loop(0, HEADS // 2, one_pair, 0, unroll=True)
        arrived(qkv_ref, named["qkv"])
        grad_na = jnp.zeros((tokens, WIDTH), F32)
        for block in range(3):
            columns = slice(block * WIDTH, (block + 1) * WIDTH)
            piece = gp_ref[:, columns]
            sums = jnp.sum(piece.astype(F32), axis=0, keepdims=True)
            if block != 1:
                small_ref[:, block // 2 * WIDTH : (block // 2 + 1) * WIDTH] = sums
            qkv_stage[:, columns] = dot(normed, piece, (0, 0)).astype(BF)
            grad_na = grad_na + dot(piece, qkv_ref[:, columns], (1, 1))
        for half in range(2):
            send_rows(qkv_stage, chips, pl.ds(half * 3 * HALF, 3 * HALF), grads_ref, half, 0, sems.at[3])
        small_ref[:, 3 * WIDTH : 4 * WIDTH] = jnp.sum(grad_na * unit, axis=0, keepdims=True)
        small_ref[:, 4 * WIDTH :] = jnp.sum(grad_na, axis=0, keepdims=True)
        grad_in = mid_ref[...] + back_of_norm(grad_na, unit, inverse, spot(row_ref, "gain_a"))
        in_ref[...] = grad_in
        if steps is not None:
            sums_ref, table_stages = rest[9], rest[10:]
            index = lax.axis_index("dp")
            core, chip = index % 2, index // 2
            for doc in range(8):
                sums_ref[doc : doc + 1, :] = (
                    jnp.sum(jnp.where(down_docs[...] == doc, grad_in, 0.0), axis=0, keepdims=True)
                    if doc < steps.shape[1]
                    else jnp.zeros((1, WIDTH), F32)
                )
            spots = [lax.broadcasted_iota(jnp.int32, (16, SLAB, 8), axis) for axis in range(2)]
            for side, half in enumerate((core, 1 - core)):
                sums = sums_ref[:, pl.ds(pl.multiple_of(half * HALF, HALF), HALF)].astype(BF)
                for owner in range(2):
                    line = ((chip ^ spots[0]) * 2 + owner) * 32 + spots[1]
                    line = jnp.where(spots[1] < 32, line, -1)
                    hot = jnp.where(line == steps_ref[...][None], 1.0, 0.0).reshape(16 * SLAB, 8).astype(BF)
                    block = dot(hot, sums, (1, 0)).astype(BF).reshape(16, SLAB, HALF)
                    stage = table_stages[side]
                    stage[:, :, owner * HALF : (owner + 1) * HALF] = block
                pltpu.make_async_copy(
                    table_stages[side], grads_ref[side].at[:, :, pl.ds(1536, 2 * HALF)], sems.at[4 + side]
                ).start()
            for side in range(2):
                arrived(table_stages[side], sems.at[4 + side])
        arrived(out_stage, sems.at[2])
        arrived(qkv_stage, sems.at[3])

    sums = [(16, SLAB, 1536 if steps is None else 2304)] * 2
    outs = [jax.ShapeDtypeStruct(shape, BF) for shape in sums] + [
        jax.ShapeDtypeStruct((tokens, WIDTH), F32),
        jax.ShapeDtypeStruct((1, 5 * WIDTH), F32),
    ]
    operands = [hidden, packed, mixed, grad_mid, row, docs.reshape(-1, 1), docs.reshape(1, -1)]
    scratch = [pltpu.VMEM(SHAPES["qkv"], BF), pltpu.VMEM(SHAPES["out"], BF)] * 2 + [
        pltpu.VMEM((tokens, WIDTH), BF),
        pltpu.VMEM((tokens, 3 * WIDTH), BF),
        pltpu.SemaphoreType.DMA((9,)),
        pltpu.VMEM((tokens, WIDTH), F32),
        pltpu.VMEM((tokens, 3 * WIDTH), BF),
        pltpu.VMEM((tokens, WIDTH), BF),
    ]
    if steps is not None:
        operands.append(jnp.pad(steps, ((0, 0), (0, 8 - steps.shape[1])), constant_values=-2))
        scratch += [pltpu.VMEM((8, WIDTH), F32)] + [pltpu.VMEM((16, SLAB, 2 * HALF), BF)] * 2
    return pl.pallas_call(
        body,
        out_shape=outs,
        in_specs=[ANY] * 3 + [WHOLE] * (len(operands) - 3) + [ANY] * len(arrays),
        out_specs=[ANY] * len(sums) + [WHOLE] * (len(outs) - len(sums)),
        scratch_shapes=scratch,
        compiler_params=pltpu.CompilerParams(vmem_limit_bytes=60 * 2**20),
        cost_estimate=pl.CostEstimate(flops=1, bytes_accessed=1, transcendentals=1),
        name="attn_backward",
    )(*operands, *arrays)


def lay_extra(source):
    def body(*rest):
        refs, (extra_ref, sems) = rest[: len(source.arrays)], rest[len(source.arrays) :]
        named = {"extra": sems.at[0]}
        start_fetch([source], refs, {"extra": extra_ref}, named)
        arrived(extra_ref, named["extra"])

    return pl.pallas_call(
        body,
        out_shape=jax.ShapeDtypeStruct(SHAPES["extra"], BF),
        in_specs=[ANY] * len(source.arrays),
        out_specs=WHOLE,
        scratch_shapes=[pltpu.SemaphoreType.DMA((1,))],
        compiler_params=pltpu.CompilerParams(vmem_limit_bytes=16 * 2**20),
        cost_estimate=pl.CostEstimate(flops=1, bytes_accessed=1, transcendentals=1),
        name="lay_extra",
    )(*source.arrays)


def is_middle():
    level = lax.axis_index("dp") // 8
    return (level == 1) | (level == 2)


def cut_of(value):
    return value.shape[-1] // 256 * 128


def chip_share(layer_weights, extra):
    core, _ = place()
    down = layer_weights.get("down")

    def halves(half):
        def columns(value):
            width = value.shape[1] // 2
            return value[:, half * width : half * width + width]

        narrow = [columns(layer_weights[name]) for name in ("qkv", "out", "up") if name in layer_weights]
        wide = []
        if down is not None:
            wide += [columns(down)[:SLAB], columns(down)[SLAB:]]
        if extra is not None:
            wide.append(columns(extra))
        parts = narrow
        if wide:
            wide = jnp.concatenate(wide, axis=1)
            parts = parts + [wide[:24], wide[24:]]
        return jnp.concatenate(parts, axis=1), sum(v.shape[1] for v in narrow)

    (left, count), (right, _) = halves(0), halves(1)
    kept = jnp.where(core == 0, left, right)
    came = swap(jnp.where(core == 0, right, left), CORE)
    lower = jnp.where(core == 0, kept, came)
    upper = jnp.where(core == 0, came, kept)
    columns = [jnp.concatenate([lower[:, :count], upper[:, :count]], axis=0)]
    wide = (lower.shape[1] - count) // 2
    if wide:
        low, high = [
            jnp.concatenate([v[:, count : count + wide], v[:, count + wide :]], axis=0) for v in (lower, upper)
        ]
        if down is not None:
            columns += [low[:, : 2 * HALF], high[:, : 2 * HALF]]
        if extra is not None:
            columns += [low[:, wide - HALF :], high[:, wide - HALF :]]
    return jnp.concatenate(columns, axis=1)


def line_second(first, third_middle):
    return swap_from(first, MIDDLE, (1, 2)), swap_from(third_middle, ALONG_Z, (1, 2))


def line_third(second_middle):
    return swap_from(second_middle, ALONG_Z, (1, 2))


def line_first(own):
    return swap(own, ALONG_Z), swap_from(own, MIDDLE, (1, 2))


def by_place(middle, end):
    return jnp.where(is_middle(), middle, end)


def along_each(to_x, to_y):
    return swap(to_x, ALONG_X), swap(to_y, ALONG_Y)


def diagonal(by_x, by_y):
    cut = cut_of(by_x)
    return swap(by_x[..., :cut], ALONG_Y), swap(by_y[..., cut:], ALONG_X)


def with_other_core(own, by_x, by_y, low, high, distances, first):
    sides = jnp.stack([own, by_x, by_y])
    across = jnp.concatenate([low, high], axis=-1)
    parts = []
    for array, steps in ((sides, (0, 1, 2)), (across, (3,))):
        if len(steps) > 1:
            entries = [((n, k), 4 * d + step) for n, step in enumerate(steps) for k, d in enumerate(distances)]
        else:
            entries = [((k,), 4 * d + 3) for k, d in enumerate(distances)]
        parts.append(Part(array, entries, first, True))
        parts.append(Part(swap(array, CORE), entries, first, False))
    return parts


def direct_line(levels):
    return [swap(levels[k], ALONG_Z * k) for k in (1, 2, 3)]


def half_line(levels):
    return swap(levels[2:], MIDDLE)


def line_end(levels, came):
    return swap(total(levels[1], came[0]).astype(BF), ALONG_Z)


def line_sum(levels, came, last):
    return total(levels[0], came[1], last)


def along_both(low, high):
    return swap(low, ALONG_Y), swap(high, ALONG_X)


def line_ends(levels):
    return [swap_from(levels[k], ALONG_Z, (0, 3)) for k in (3, 2)]


def line_middles(levels, ends):
    return [
        swap_from(total(levels[2], ends[0]).astype(BF), MIDDLE, (1, 2)),
        swap_from(total(levels[3], ends[1]).astype(BF), MIDDLE, (1, 2)),
    ]


def line_last(levels, middles):
    return swap(total(levels[1], middles[0]).astype(BF), ALONG_Z)


def total(*values):
    return sum(v.astype(F32) for v in values)


class PlaneSums:
    def __init__(self, *pairs):
        self.pairs = [[v.reshape(4, 4, SLAB, v.shape[-1]) for v in pair] for pair in pairs]
        self.columns = sum(pair[0].shape[-1] for pair in pairs)
        self.cut = self.columns // 256 * 128

    def pair(self, step, first=0, last=None):
        last = self.columns if last is None else last
        pieces = []
        begin = 0
        for pair in self.pairs:
            end = begin + pair[0].shape[-1]
            low, high = max(first, begin) - begin, min(last, end) - begin
            if low < high:
                pieces.append(total(*[v[:, step, :, low:high] for v in pair]))
            begin = end
        return pieces[0] if len(pieces) == 1 else jnp.concatenate(pieces, axis=-1)

    def diagonals(self):
        return self.pair(3, 0, self.cut).astype(BF), self.pair(3, self.cut).astype(BF)

    def sides(self, low, high):
        room = [(0, 0)] * 2
        low = jnp.pad(low, room + [(0, self.columns - self.cut)])
        high = jnp.pad(high, room + [(self.cut, 0)])
        return (self.pair(1) + low.astype(F32)).astype(BF), (self.pair(2) + high.astype(F32)).astype(BF)

    def levels(self, by_x, by_y):
        return (self.pair(0) + total(by_x, by_y)).astype(BF)


def by_half(core, mine, other, axis):
    return jnp.where(
        core == 0, jnp.concatenate([mine, other], axis=axis), jnp.concatenate([other, mine], axis=axis)
    )


def own_rows(names, share):
    core, _ = place()
    widths = {"qkv": 1152, "out": 384, "up": 1536, "down": 1536, "down_by_core": 1536, "extra": 768}
    pieces = []
    start = 0
    for name in names:
        piece = share[:, start : start + widths[name]]
        start += widths[name]
        if name in ("down", "extra"):
            m = widths[name] // 2
            mine, theirs = [lax.dynamic_slice_in_dim(piece, side * m, m, 1) for side in (core, 1 - core)]
            if name == "down":
                mine, theirs = [jnp.concatenate([v[:, :HALF], v[:, HALF:]], axis=0) for v in (mine, theirs)]
        else:
            mine, theirs = [lax.dynamic_slice_in_dim(piece, side * 24, 24, 0) for side in (core, 1 - core)]
        pieces.append((mine, theirs))
    sizes = [theirs.shape for _, theirs in pieces]
    packed = jnp.concatenate([theirs.astype(BF).reshape(24, -1) for _, theirs in pieces], axis=1)
    came = swap(packed, CORE)
    outs = []
    start = 0
    for (mine, _), (rows, columns) in zip(pieces, sizes):
        count = rows * columns // 24
        other = came[:, start : start + count].reshape(rows, columns).astype(F32)
        start += count
        outs.append((mine, other))
    for n, name in enumerate(names):
        if name == "down_by_core":
            outs[n] = [jnp.concatenate(jnp.split(v, 4, axis=1), axis=0) for v in outs[n]]
    return [by_half(core, mine, other, 1) for mine, other in outs]


def small_maps(layer):
    device = np.full(ROW_LENGTH, -1, np.int32)
    inner = np.full(ROW_LENGTH, -1, np.int32)

    def put(at, count, each, begin):
        spots = np.arange(count)
        device[at : at + count] = spots // each
        inner[at : at + count] = begin + spots % each

    for n, name in enumerate(WIDE_SMALLS):
        put(SPOTS[name], WIDTH, 24, 24 * n)
    put(BIAS_AT, 2 * WIDTH, 48, 144)
    for array in (device, inner):
        array[BIAS_AT + 2 * WIDTH : BIAS_AT + 3 * WIDTH] = array[BIAS_AT + WIDTH : BIAS_AT + 2 * WIDTH]
        array[BIAS_AT + WIDTH : BIAS_AT + 2 * WIDTH] = -1
    put(UP_AT, HIDDEN, 96, 192)
    if layer == 1:
        block, there, at = np.unravel_index(np.arange(HIDDEN), (4, TUNED, 24))
        device[UP_AT:], inner[UP_AT:] = there, 192 + 24 * block + at
    return device, inner


WIDE_SMALLS = ("out_b", "gain_a", "shift_a", "down_b", "gain_b", "shift_b")
GRAD_ORDER = ("up", "down_b", "gain_b", "shift_b", "query", "value", "out_b", "gain_a", "shift_a")


def grad_maps(layer):
    device, inner = small_maps(layer)
    pieces = {"up": (UP_AT, HIDDEN), "query": (BIAS_AT, WIDTH), "value": (BIAS_AT + 2 * WIDTH, WIDTH)}
    pieces.update({name: (at, WIDTH) for name, at in SPOTS.items()})
    order = np.concatenate([np.arange(at, at + count) for at, count in (pieces[name] for name in GRAD_ORDER)])
    return device[order], inner[order]


def spread_smalls(gathered, layer):
    device, inner = small_maps(layer)
    hot = (jnp.arange(HALF, dtype=jnp.int32)[:, None] == inner[None, :]).astype(BF)
    wide = jnp.dot(gathered, hot, preferred_element_type=F32)
    mine = jnp.arange(TUNED, dtype=jnp.int32)[:, None] == device[None, :]
    return jnp.sum(jnp.where(mine, wide, 0.0), axis=0, keepdims=True)


def collect_smalls(row, layer):
    device, inner = grad_maps(layer)
    mine = jnp.arange(TUNED, dtype=jnp.int32)[:, None] == device[None, :]
    masked = jnp.where(mine, row.astype(BF), jnp.zeros((), BF))
    hot = (inner[:, None] == jnp.arange(HALF, dtype=jnp.int32)[None, :]).astype(BF)
    return jnp.dot(masked, hot, preferred_element_type=F32).astype(BF)


gate = lax.optimization_barrier


def tuned(
    embedded,
    doc_ids,
    step_ids,
    step_table,
    qkv_weight,
    qv_bias,
    out_weight,
    out_bias,
    first_gain,
    first_shift,
    up_weight,
    up_bias,
    down_weight,
    down_bias,
    second_gain,
    second_shift,
    cotangent,
):
    core, chip = place()
    docs = doc_ids[0]
    doc_count = step_ids.shape[1]
    steps = step_ids[0]
    smalls = (out_bias, first_gain, first_shift, down_bias, second_gain, second_shift, qv_bias, up_bias)
    small_rows = jnp.pad(jnp.concatenate(smalls, axis=1), ((0, 0), (0, HALF - 288))).reshape(1, 2 * HALF)
    extra = jnp.concatenate([step_table, jnp.pad(small_rows, ((0, 15), (0, 0)))], axis=0)
    down_blocks = [down_weight[1][24 * b : 24 * b + 24] for b in range(4)]
    up_order = up_weight[1].reshape(24, TUNED, 4, 24).transpose(0, 2, 1, 3).reshape(24, HIDDEN)
    upper_share = jnp.concatenate([qkv_weight[1], out_weight[1], up_order] + down_blocks, axis=1)
    lower_share = chip_share(
        {"qkv": qkv_weight[0], "out": out_weight[0], "up": up_weight[0], "down": down_weight[0]}, extra
    )
    starts = {"qkv": 0, "out": 1152, "up": 1536, "down": 3072, "extra": 4608}
    upper_starts = {"qkv": 0, "out": 3 * WIDTH, "up": 4 * WIDTH, "down": 8 * WIDTH}
    upper = lax.all_gather(upper_share, "dp", axis=0, tiled=True)

    block1, block3_middle = line_first(lower_share)
    second_middle, second_end = line_second(block1, block3_middle)
    third_end = line_third(second_middle)
    blocks = [lower_share, block1, by_place(second_middle, second_end), by_place(block3_middle, third_end)]
    parts = []
    for distance, block in enumerate(blocks):
        by_x, by_y = along_each(block, block)
        plane = jnp.stack([block, by_x, by_y, jnp.concatenate(diagonal(by_x, by_y), axis=1)])
        entries = [((step,), 4 * distance + step, 0) for step in range(4)]
        parts += [Part(plane, entries, True), Part(swap(plane, CORE), entries, False)]
    source0, source1 = Source(parts, starts), Source(upper, upper_starts)

    all_extra = lay_extra(source0)
    small_all = all_extra[32::SLAB].reshape(16, 2, 2, HALF).transpose(1, 0, 2, 3).reshape(2, TUNED, HALF)
    rows = [spread_smalls(small_all[0], 0)]
    owner = steps // 32
    row_of = (owner // 2) * SLAB + steps % 32
    row_hot = (row_of[:, None] == jnp.arange(16 * SLAB, dtype=jnp.int32)[None, :]).astype(BF)
    both_rows = jnp.dot(row_hot, all_extra, preferred_element_type=F32).reshape(doc_count, 2, 2, HALF)
    doc_rows = jnp.where((owner % 2 == 0)[:, None, None], both_rows[:, :, 0], both_rows[:, :, 1])
    doc_rows = doc_rows.reshape(doc_count, WIDTH)
    of_doc = [(docs == s)[:, None] for s in range(doc_count)]
    start = embedded.astype(F32) + sum(jnp.where(of_doc[s], doc_rows[s][None], 0.0) for s in range(doc_count))

    packed0, mixed0, middle0, between = layer_forward(start, rows[0], docs, [source0])

    between, small_1 = gate((between, small_all[1]))
    rows.append(spread_smalls(small_1, 1))
    kept_m, sent_m, mid1, small_mlp1, packed1, mixed1, block_output = mlp_backward(
        between, cotangent, rows[1], [source1], docs
    )
    came_m = swap(sent_m, CORE)
    kept_t, sent_t, in1, small_attn1 = attn_backward(
        between, mid1, packed1, mixed1, rows[1], docs, [source1], None
    )
    in1, came_m, sent_t = gate((in1, came_m, sent_t))
    sums_m = PlaneSums((kept_m, came_m))
    in1, to_go, sent_t = gate((in1, sums_m.diagonals(), sent_t))
    low_m = along_both(*to_go)
    came_t = swap(sent_t, CORE)
    kept_b, sent_b, mid0, small_mlp0 = mlp_backward(middle0, in1, rows[0], [source0])
    mid0, low_m, came_t, sent_b = gate((mid0, low_m, came_t, sent_b))
    came_b = swap(sent_b, CORE)
    sums_t = PlaneSums((kept_t, came_t))
    low_t = along_both(*sums_t.diagonals())
    x_m = along_each(*sums_m.sides(*low_m))
    mid0, to_go, small_mlp1, small_attn1 = gate((mid0, sums_t.sides(*low_t), small_mlp1, small_attn1))
    x_t = along_each(*to_go)
    kept_c, sent_c, input_grad, small_attn0 = attn_backward(
        start, mid0, packed0, mixed0, rows[0], docs, [source0], step_ids
    )
    input_grad, came_b, kept_c, sent_c, small_attn0 = gate((input_grad, came_b, kept_c, sent_c, small_attn0))
    sums_b = PlaneSums((kept_b, came_b))
    small_grads = jnp.stack(
        [
            collect_smalls(jnp.concatenate([small_mlp0, small_attn0], axis=1), 0),
            collect_smalls(jnp.concatenate([small_mlp1, small_attn1], axis=1), 1),
        ]
    ).reshape(2, 16, 2 * HALF)
    small_grads = small_grads[:, chip ^ jnp.arange(16, dtype=jnp.int32)][:, :, None]
    small_grads = jnp.pad(small_grads, ((0, 0), (0, 0), (0, 15), (0, 0)))
    kept_c, sent_c = [
        lax.dynamic_update_slice(
            v, lax.dynamic_index_in_dim(small_grads, side, 0, keepdims=False), (0, 32, 1536)
        )
        for v, side in ((kept_c, core), (sent_c, 1 - core))
    ]
    x_m, x_t, to_go, kept_c, sent_c = gate((x_m, x_t, sums_b.diagonals(), kept_c, sent_c))

    low_b = along_both(*to_go)
    came_c = swap(sent_c, CORE)
    x_m, x_t, came_c = gate((x_m, x_t, came_c))
    sums_c = PlaneSums((kept_c, came_c))
    to_go = sums_c.diagonals()
    low_c = along_both(*to_go)
    levels_m = sums_m.levels(*x_m)
    half_m = half_line(levels_m)
    low_b, to_go = gate((low_b, to_go))
    x_b = along_each(*sums_b.sides(*low_b))
    low_c, half_m, x_t = gate((low_c, half_m, x_t))
    x_c = along_each(*sums_c.sides(*low_c))
    levels_t = sums_t.levels(*x_t)
    half_t = half_line(levels_t)
    levels_a = jnp.concatenate([levels_m, levels_t], axis=-1)
    half_a = jnp.concatenate([half_m, half_t], axis=-1)
    levels_b = sums_b.levels(*x_b)
    half_b = half_line(levels_b)
    x_c, levels_b = gate((x_c, levels_b))
    levels_c, half_a = gate((sums_c.levels(*x_c), half_a))
    back_c = [swap(levels_c[k], ALONG_Z * k) for k in (1, 2, 3)]
    last_a = line_end(levels_a, half_a)
    up_1, down_1, qkv_1, out_1 = own_rows(
        ("up", "down_by_core", "qkv", "out"), line_sum(levels_a, half_a, last_a)
    )
    up_1 = up_1.reshape(24, 4, TUNED, 24).transpose(0, 2, 1, 3).reshape(24, HIDDEN)
    half_b, back_c, up_1, down_1, qkv_1, out_1 = gate((half_b, back_c, up_1, down_1, qkv_1, out_1))
    last_b = line_end(levels_b, half_b)
    qkv_0, out_0, extra_0 = own_rows(("qkv", "out", "extra"), total(levels_c[0], *back_c))
    up_0, down_0 = own_rows(("up", "down"), line_sum(levels_b, half_b, last_b))
    up, down = jnp.stack([up_0, up_1]), jnp.stack([down_0, down_1])
    small_out = extra_0[32].reshape(2, HALF)
    out_b, gain_a, shift_a, down_b, gain_b, shift_b = [small_out[:, n * 24 : n * 24 + 24] for n in range(6)]
    return (
        block_output,
        input_grad,
        extra_0[:32],
        jnp.stack([qkv_0, qkv_1]),
        small_out[:, 144:192],
        jnp.stack([out_0, out_1]),
        out_b,
        gain_a,
        shift_a,
        up,
        small_out[:, 192:288],
        down,
        down_b,
        gain_b,
        shift_b,
    )


def shortened(value):
    return jax.tree.map(lambda a: a.astype(jnp.bfloat16) if a.dtype == jnp.float32 else a, value)


def partner(value, axis, stride):
    return lax.ppermute(value, axis, [(i, i ^ 1 << stride) for i in range(lax.axis_size(axis))])


def norm_rows(hidden, gain_vec, shift_vec):
    average = jnp.mean(hidden, axis=-1, keepdims=True)
    centred = hidden - average
    variance = jnp.mean(centred * centred, axis=-1, keepdims=True)
    inverse = lax.rsqrt(variance + EPSILON)
    unit_rows = centred * inverse
    normed = unit_rows * gain_vec.astype(jnp.float32) + shift_vec.astype(jnp.float32)
    return (normed, unit_rows, inverse)


def norm_back(grad_rows, unit_rows, inverse, gain_vec):
    scaled = grad_rows * gain_vec.astype(jnp.float32)
    first_mean = jnp.mean(scaled, axis=-1, keepdims=True)
    second_mean = jnp.mean(scaled * unit_rows, axis=-1, keepdims=True)
    return inverse * (scaled - first_mean - unit_rows * second_mean)


def smooth_gate(lifted):
    return jax.nn.gelu(lifted, approximate=True)


def halving_sum(members, send_fn):
    levels = lax.axis_size("dp").bit_length() - 1
    position = lax.axis_index("dp")
    current = tuple(members)
    for level in range(levels - 1, -1, -1):
        upper_side = position // (1 << level) % 2 == 1
        kept_list = []
        sent_list = []
        for member in current:
            half = member.shape[0] // 2
            lower_part = member[:half]
            upper_part = member[half:]
            kept_list.append(jnp.where(upper_side, upper_part, lower_part))
            sent_list.append(jnp.where(upper_side, lower_part, upper_part))
        received = send_fn(tuple(sent_list), level)
        current = tuple((kept + came for kept, came in zip(kept_list, received)))
    return current


def layer_apply(hidden, params, same_doc):
    qkv_w, qv_b, out_w, out_b, gain_a, shift_a, up_w, up_b, down_w, down_b, gain_b, shift_b = params
    width = out_w.shape[0]
    tok_count = hidden.shape[0]
    scale = 1.0 / math.sqrt(HEAD_DIM)
    normed_a, unit_a, inverse_a = norm_rows(hidden, gain_a, shift_a)
    normed_a = normed_a.astype(jnp.bfloat16)
    qv_float = qv_b.astype(jnp.float32)
    bias_full = jnp.concatenate(
        [qv_float[:width], jnp.zeros((width,), jnp.float32), qv_float[width:]]
    )
    packed = (jnp.dot(normed_a, qkv_w, preferred_element_type=jnp.float32) + bias_full).astype(
        jnp.bfloat16
    )
    queries = packed[:, :width].reshape(tok_count, HEADS, HEAD_DIM)
    key_rows = packed[:, width : 2 * width].reshape(tok_count, HEADS, HEAD_DIM)
    value_rows = packed[:, 2 * width :].reshape(tok_count, HEADS, HEAD_DIM)
    scores = (
        jnp.einsum("qhd,khd->hqk", queries, key_rows, preferred_element_type=jnp.float32) * scale
    )
    masked = jnp.where(same_doc[None], scores, -1e30)
    top_score = jnp.max(masked, axis=-1, keepdims=True)
    expo_rows = jnp.exp(masked - top_score)
    probs = expo_rows / jnp.sum(expo_rows, axis=-1, keepdims=True)
    probs_low = probs.astype(jnp.bfloat16)
    mixed = jnp.einsum("hqk,khd->qhd", probs_low, value_rows, preferred_element_type=jnp.float32)
    mixed = mixed.reshape(tok_count, width).astype(jnp.bfloat16)
    middle = (
        hidden
        + jnp.dot(mixed, out_w, preferred_element_type=jnp.float32)
        + out_b.astype(jnp.float32)
    )
    normed_b, unit_b, inverse_b = norm_rows(middle, gain_b, shift_b)
    normed_b = normed_b.astype(jnp.bfloat16)
    lifted = jnp.dot(normed_b, up_w, preferred_element_type=jnp.float32) + up_b.astype(jnp.float32)
    activated = smooth_gate(lifted).astype(jnp.bfloat16)
    output = (
        middle
        + jnp.dot(activated, down_w, preferred_element_type=jnp.float32)
        + down_b.astype(jnp.float32)
    )
    saved = (
        unit_a,
        inverse_a,
        normed_a,
        queries,
        key_rows,
        value_rows,
        probs,
        probs_low,
        mixed,
        unit_b,
        inverse_b,
        normed_b,
        lifted,
        activated,
    )
    return (output, saved)


def layer_back(hidden, params, same_doc, grad_top):
    qkv_w, qv_b, out_w, out_b, gain_a, shift_a, up_w, up_b, down_w, down_b, gain_b, shift_b = params
    unused_output, saved = layer_apply(hidden, params, same_doc)
    (
        unit_a,
        inverse_a,
        normed_a,
        queries,
        key_rows,
        value_rows,
        probs,
        probs_low,
        mixed,
        unit_b,
        inverse_b,
        normed_b,
        lifted,
        activated,
    ) = saved
    width = out_w.shape[0]
    tok_count = hidden.shape[0]
    scale = 1.0 / math.sqrt(HEAD_DIM)
    grad_down = grad_top.astype(jnp.bfloat16)
    down_b_grad = jnp.sum(grad_down.astype(jnp.float32), axis=0)
    down_w_grad = jnp.einsum("tf,td->fd", activated, grad_down, preferred_element_type=jnp.float32)
    grad_act = jnp.einsum("td,fd->tf", grad_down, down_w, preferred_element_type=jnp.float32)
    unused_gate, gate_pull = jax.vjp(smooth_gate, lifted)
    grad_lift = gate_pull(grad_act)[0].astype(jnp.bfloat16)
    up_b_grad = jnp.sum(grad_lift.astype(jnp.float32), axis=0)
    up_w_grad = jnp.einsum("td,tf->df", normed_b, grad_lift, preferred_element_type=jnp.float32)
    grad_nb = jnp.einsum("tf,df->td", grad_lift, up_w, preferred_element_type=jnp.float32)
    gain_b_grad = jnp.sum(grad_nb * unit_b, axis=0)
    shift_b_grad = jnp.sum(grad_nb, axis=0)
    grad_mid = grad_top + norm_back(grad_nb, unit_b, inverse_b, gain_b)
    grad_branch = grad_mid.astype(jnp.bfloat16)
    out_b_grad = jnp.sum(grad_branch.astype(jnp.float32), axis=0)
    out_w_grad = jnp.einsum("te,td->ed", mixed, grad_branch, preferred_element_type=jnp.float32)
    grad_mixed = jnp.einsum("td,ed->te", grad_branch, out_w, preferred_element_type=jnp.float32)
    grad_mixed = grad_mixed.astype(jnp.bfloat16).reshape(tok_count, HEADS, HEAD_DIM)
    grad_probs = jnp.einsum(
        "qhd,khd->hqk", grad_mixed, value_rows, preferred_element_type=jnp.float32
    )
    grad_values = jnp.einsum(
        "hqk,qhd->khd", probs_low, grad_mixed, preferred_element_type=jnp.float32
    )
    grad_scores = probs * (grad_probs - jnp.sum(probs * grad_probs, axis=-1, keepdims=True))
    scores_low = grad_scores.astype(jnp.bfloat16)
    grad_queries = (
        jnp.einsum("hqk,khd->qhd", scores_low, key_rows, preferred_element_type=jnp.float32) * scale
    )
    grad_keys = (
        jnp.einsum("hqk,qhd->khd", scores_low, queries, preferred_element_type=jnp.float32) * scale
    )
    grad_packed = jnp.concatenate(
        [
            grad_queries.reshape(tok_count, width),
            grad_keys.reshape(tok_count, width),
            grad_values.reshape(tok_count, width),
        ],
        axis=1,
    ).astype(jnp.bfloat16)
    packed_sums = jnp.sum(grad_packed.astype(jnp.float32), axis=0)
    qv_b_grad = jnp.concatenate([packed_sums[:width], packed_sums[2 * width :]])
    qkv_w_grad = jnp.einsum("td,te->de", normed_a, grad_packed, preferred_element_type=jnp.float32)
    grad_na = jnp.einsum("te,de->td", grad_packed, qkv_w, preferred_element_type=jnp.float32)
    gain_a_grad = jnp.sum(grad_na * unit_a, axis=0)
    shift_a_grad = jnp.sum(grad_na, axis=0)
    grad_in = grad_mid + norm_back(grad_na, unit_a, inverse_a, gain_a)
    grads = (
        qkv_w_grad,
        qv_b_grad,
        out_w_grad,
        out_b_grad,
        gain_a_grad,
        shift_a_grad,
        up_w_grad,
        up_b_grad,
        down_w_grad,
        down_b_grad,
        gain_b_grad,
        shift_b_grad,
    )
    return (grad_in, grads)


def plain(
    embedded,
    doc_ids,
    step_ids,
    step_table,
    qkv_weight,
    qv_bias,
    out_weight,
    out_bias,
    first_gain,
    first_shift,
    up_weight,
    up_bias,
    down_weight,
    down_bias,
    second_gain,
    second_shift,
    cotangent,
):
    docs_row = doc_ids[0]
    same_doc = docs_row[:, None] == docs_row[None, :]
    doc_count = step_ids.shape[1]
    doc_hot = (docs_row[:, None] == jnp.arange(doc_count, dtype=jnp.int32)[None, :]).astype(
        jnp.float32
    )
    gathered_first = (
        lax.all_gather(qkv_weight[0], "dp", axis=0, tiled=True),
        lax.all_gather(qv_bias[0], "dp", axis=0, tiled=True),
        lax.all_gather(out_weight[0], "dp", axis=0, tiled=True),
        lax.all_gather(out_bias[0], "dp", axis=0, tiled=True),
        lax.all_gather(first_gain[0], "dp", axis=0, tiled=True),
        lax.all_gather(first_shift[0], "dp", axis=0, tiled=True),
        lax.all_gather(up_weight[0], "dp", axis=0, tiled=True),
        lax.all_gather(up_bias[0], "dp", axis=0, tiled=True),
        lax.all_gather(down_weight[0], "dp", axis=0, tiled=True),
        lax.all_gather(down_bias[0], "dp", axis=0, tiled=True),
        lax.all_gather(second_gain[0], "dp", axis=0, tiled=True),
        lax.all_gather(second_shift[0], "dp", axis=0, tiled=True),
        lax.all_gather(step_table, "dp", axis=0, tiled=True),
    )
    params_lower = gathered_first[:12]
    table_whole = gathered_first[12]
    step_hot = step_ids[0][:, None] == jnp.arange(table_whole.shape[0], dtype=jnp.int32)[None, :]
    doc_rows = jnp.dot(
        step_hot.astype(jnp.bfloat16), table_whole, preferred_element_type=jnp.float32
    )
    start = embedded.astype(jnp.float32) + jnp.dot(
        doc_hot, doc_rows, precision=lax.Precision.HIGHEST
    )
    middle_hidden, unused_lower = layer_apply(start, params_lower, same_doc)
    params_upper = (
        lax.all_gather(qkv_weight[1], "dp", axis=0, tiled=True),
        lax.all_gather(qv_bias[1], "dp", axis=0, tiled=True),
        lax.all_gather(out_weight[1], "dp", axis=0, tiled=True),
        lax.all_gather(out_bias[1], "dp", axis=0, tiled=True),
        lax.all_gather(first_gain[1], "dp", axis=0, tiled=True),
        lax.all_gather(first_shift[1], "dp", axis=0, tiled=True),
        lax.all_gather(up_weight[1], "dp", axis=0, tiled=True),
        lax.all_gather(up_bias[1], "dp", axis=0, tiled=True),
        lax.all_gather(down_weight[1], "dp", axis=0, tiled=True),
        lax.all_gather(down_bias[1], "dp", axis=0, tiled=True),
        lax.all_gather(second_gain[1], "dp", axis=0, tiled=True),
        lax.all_gather(second_shift[1], "dp", axis=0, tiled=True),
    )
    final_hidden, unused_upper = layer_apply(middle_hidden, params_upper, same_doc)
    block_output = final_hidden.astype(jnp.bfloat16)

    def weights_for(layer_index):
        return (
            lax.all_gather(qkv_weight[layer_index], "dp", axis=0, tiled=True),
            lax.all_gather(qv_bias[layer_index], "dp", axis=0, tiled=True),
            lax.all_gather(out_weight[layer_index], "dp", axis=0, tiled=True),
            lax.all_gather(out_bias[layer_index], "dp", axis=0, tiled=True),
            lax.all_gather(first_gain[layer_index], "dp", axis=0, tiled=True),
            lax.all_gather(first_shift[layer_index], "dp", axis=0, tiled=True),
            lax.all_gather(up_weight[layer_index], "dp", axis=0, tiled=True),
            lax.all_gather(up_bias[layer_index], "dp", axis=0, tiled=True),
            lax.all_gather(down_weight[layer_index], "dp", axis=0, tiled=True),
            lax.all_gather(down_bias[layer_index], "dp", axis=0, tiled=True),
            lax.all_gather(second_gain[layer_index], "dp", axis=0, tiled=True),
            lax.all_gather(second_shift[layer_index], "dp", axis=0, tiled=True),
        )

    grad_upper_in, upper_grads = layer_back(
        middle_hidden, weights_for(1), same_doc, cotangent.astype(jnp.float32)
    )

    def send_upper(sent, level):
        return jax.tree.map(
            lambda part, own: part.astype(own.dtype), partner(shortened(sent), "dp", level), sent
        )

    upper_shards = halving_sum(upper_grads, send_upper)
    input_grad, lower_grads = layer_back(start, weights_for(0), same_doc, grad_upper_in)
    doc_grads = jnp.einsum("ts,td->sd", doc_hot, input_grad, precision=lax.Precision.HIGHEST)
    table_full_grad = jnp.einsum(
        "sn,sd->nd", step_hot.astype(jnp.float32), doc_grads, precision=lax.Precision.HIGHEST
    )

    def send_lower(sent, level):
        return jax.tree.map(
            lambda part, own: part.astype(own.dtype), partner(shortened(sent), "dp", level), sent
        )

    lower_all = halving_sum(tuple(lower_grads) + (table_full_grad,), send_lower)
    lower_shards = lower_all[:12]
    table_shard = lower_all[12]
    stacked = [jnp.stack([lower_shards[index], upper_shards[index]], axis=0) for index in range(12)]
    return (
        block_output,
        input_grad,
        table_shard,
        stacked[0],
        stacked[1],
        stacked[2],
        stacked[3],
        stacked[4],
        stacked[5],
        stacked[6],
        stacked[7],
        stacked[8],
        stacked[9],
        stacked[10],
        stacked[11],
    )


def solution(mesh):
    local = tuned if mesh.shape["dp"] == TUNED else plain
    in_specs = (
        P("dp", None),
        P("dp", None),
        P("dp", None),
        P("dp", None),
        P(None, "dp", None),
        P(None, "dp"),
        P(None, "dp", None),
        P(None, "dp"),
        P(None, "dp"),
        P(None, "dp"),
        P(None, "dp", None),
        P(None, "dp"),
        P(None, "dp", None),
        P(None, "dp"),
        P(None, "dp"),
        P(None, "dp"),
        P("dp", None),
    )
    out_specs = (
        P("dp", None),
        P("dp", None),
        P("dp", None),
        P(None, "dp", None),
        P(None, "dp"),
        P(None, "dp", None),
        P(None, "dp"),
        P(None, "dp"),
        P(None, "dp"),
        P(None, "dp", None),
        P(None, "dp"),
        P(None, "dp", None),
        P(None, "dp"),
        P(None, "dp"),
        P(None, "dp"),
    )
    return jax.shard_map(local, mesh=mesh, in_specs=in_specs, out_specs=out_specs, check_vma=False)
```

```python
import math

import jax
import jax.numpy as jnp
import numpy as np
from jax import lax
from jax.experimental import pallas as pl
from jax.experimental.pallas import tpu as pltpu
from jax.sharding import PartitionSpec as P

HEADS = 12
HEAD_DIM = 64
EPSILON = 1e-05
BF = jnp.bfloat16
F32 = jnp.float32

TUNED = 32
CORE, ALONG_X, ALONG_Y, ALONG_Z, MIDDLE = 1, 2, 4, 8, 24
SLAB = 48
HALF = 384


def swap(value, stride):
    return lax.ppermute(value, "dp", [(i, i ^ stride) for i in range(TUNED)])


def swap_from(value, stride, zs):
    return lax.ppermute(value, "dp", [(i, i ^ stride) for i in range(TUNED) if i // 8 in zs])


def after(done, waiting):
    return lax.optimization_barrier((done, waiting))


def place():
    index = lax.axis_index("dp")
    return index % 2, index // 2


WIDTH = HEADS * HEAD_DIM
HIDDEN = 4 * WIDTH
PAIR = 2 * HEAD_DIM
ANY = pl.BlockSpec(memory_space=pl.ANY)
WHOLE = pl.BlockSpec(memory_space=pltpu.VMEM)
ATTN = {"qkv": 1152, "out": 384}
MLP = {"up": 1536, "down": 1536}
SHAPES = {"qkv": (768, 2304), "out": (768, 768), "up": (768, 3072), "down": (3072, 768), "extra": (768, 1536)}


SPOTS = {"gain_a": 0, "shift_a": 768, "out_b": 1536, "gain_b": 2304, "shift_b": 3072, "down_b": 3840}
BIAS_AT, UP_AT, ROW_LENGTH = 4608, 6912, 9984


def spot(ref, name):
    return ref[:, SPOTS[name] : SPOTS[name] + WIDTH]


class Part:
    def __init__(self, array, entries, own):
        self.array, self.entries, self.own = array, entries, own


class Source:
    def __init__(self, weights, starts):
        self.weights, self.starts = weights, starts
        self.natural = not isinstance(weights, list)
        self.arrays = [weights] if self.natural else [part.array for part in weights]


def fetch_parts(parts, refs, starts, targets, sems):
    index = lax.axis_index("dp")
    core, chip = index % 2, index // 2
    for part, ref in zip(parts, refs):
        half = core if part.own else 1 - core
        for leading, code, first in part.entries:
            last = first + part.array.shape[-1]
            there = chip ^ code
            for name, target in targets.items():
                begin = starts[name]
                if name == "down":
                    pieces = [(begin + block * HALF, HALF, block) for block in range(4)]
                else:
                    pieces = [(begin, target.shape[1] // 2, None)]
                for start, width, block in pieces:
                    low, high = max(start, first), min(start + width, last)
                    if low >= high:
                        continue
                    columns = pl.ds(pl.multiple_of(half * width + (low - start), 128), high - low)
                    row = there * SLAB if block is None else there * (4 * SLAB) + block * SLAB
                    pltpu.make_async_copy(
                        ref.at[leading + (slice(None), pl.ds(low - first, high - low))],
                        target.at[pl.ds(pl.multiple_of(row, SLAB), SLAB), columns],
                        sems[name],
                    ).start()


def start_fetch(sources, refs, targets, sems):
    for source in sources:
        own, refs = refs[: len(source.arrays)], refs[len(source.arrays) :]
        wanted = {name: targets[name] for name in source.starts if name in targets}
        if not source.natural:
            fetch_parts(source.weights, own, source.starts, wanted, sems)
            continue
        for name, target in wanted.items():
            pieces = [(0, slice(None), target.shape[1])]
            if name == "down":
                pieces = [(b * WIDTH, pl.ds(b * WIDTH, WIDTH), WIDTH) for b in range(4)]
            for shift, rows, width in pieces:
                pltpu.make_async_copy(
                    own[0].at[:, pl.ds(source.starts[name] + shift, width)], target.at[rows, :], sems[name]
                ).start()


def arrays_of(sources):
    return [array for source in sources for array in source.arrays]


def arrived(target, sem):
    pltpu.make_async_copy(target, target, sem).wait()


def dot(left, right, contract):
    return lax.dot_general(left, right, ((contract[:1], contract[1:]), ((), ())), preferred_element_type=F32)


def unit_of(hidden):
    average = jnp.mean(hidden, axis=-1, keepdims=True)
    centred = hidden - average
    inverse = lax.rsqrt(jnp.mean(centred * centred, axis=-1, keepdims=True) + EPSILON)
    return centred * inverse, inverse


def back_of_norm(grad_rows, unit_rows, inverse, gain):
    scaled = grad_rows * gain
    first_mean = jnp.mean(scaled, axis=-1, keepdims=True)
    second_mean = jnp.mean(scaled * unit_rows, axis=-1, keepdims=True)
    return inverse * (scaled - first_mean - unit_rows * second_mean)


def gelu_pair(value):
    factor = math.sqrt(2.0 / math.pi)
    square = value * value
    bend = jnp.tanh(factor * value * (1.0 + 0.044715 * square))
    half_up = 0.5 * (1.0 + bend)
    slope = half_up + 0.5 * value * (1.0 - bend * bend) * factor * (1.0 + 3.0 * 0.044715 * square)
    return value * half_up, slope


def softmax_rows(query, keys, same):
    scores = dot(query, keys, (1, 1)) * (1.0 / math.sqrt(HEAD_DIM))
    masked = jnp.where(same, scores, -1e30)
    expo = jnp.exp(masked - jnp.max(masked, axis=-1, keepdims=True))
    return expo * (1.0 / jnp.sum(expo, axis=-1, keepdims=True))


def head_lanes(count):
    return lax.broadcasted_iota(jnp.int32, (count, PAIR), 1) < HEAD_DIM


def pair_slice(pair, block):
    return pl.ds(pl.multiple_of(block * WIDTH + pair * PAIR, PAIR), PAIR)


def attn_steps(hidden, row_ref, docs_refs, packed_ref, mixed_ref, qkv_ref, out_ref, named):
    unit, _ = unit_of(hidden)
    normed = (unit * spot(row_ref, "gain_a") + spot(row_ref, "shift_a")).astype(BF)
    arrived(qkv_ref, named["qkv"])
    for block in range(3):
        columns = slice(block * WIDTH, (block + 1) * WIDTH)
        packed_ref[:, columns] = (
            dot(normed, qkv_ref[:, columns], (1, 0))
            + row_ref[:, BIAS_AT + block * WIDTH : BIAS_AT + (block + 1) * WIDTH]
        ).astype(BF)
    same = docs_refs[0][...] == docs_refs[1][...]
    first_head = head_lanes(hidden.shape[0])
    for pair in range(HEADS // 2):
        query, keys, values = [packed_ref[:, pair_slice(pair, block)] for block in range(3)]
        blank = jnp.zeros_like(query)
        mixes = []
        for own in (jnp.where(first_head, query, blank), jnp.where(first_head, blank, query)):
            mixes.append(dot(softmax_rows(own, keys, same).astype(BF), values, (1, 0)))
        mixed_ref[:, pair_slice(pair, 0)] = jnp.where(first_head, mixes[0], mixes[1]).astype(BF)
    arrived(out_ref, named["out"])
    return hidden + dot(mixed_ref[...], out_ref[...], (1, 0)) + spot(row_ref, "out_b")


def layer_forward(hidden, row, docs, sources):
    arrays = arrays_of(sources)
    tokens = hidden.shape[0]
    names = ("qkv", "out", "up", "down")

    def body(hidden_ref, row_ref, down_docs, across_docs, *rest):
        refs, rest = rest[: len(arrays)], rest[len(arrays) :]
        saved_at, top_ref = rest[:3], rest[3]
        targets, sems, saved = dict(zip(names, rest[4:8])), rest[8], rest[9:]
        packed_ref, mixed_ref, middle_ref = saved
        named = {name: sems.at[n] for n, name in enumerate(names)}
        start_fetch(sources, refs, targets, named)
        middle = attn_steps(
            hidden_ref[...],
            row_ref,
            (down_docs, across_docs),
            packed_ref,
            mixed_ref,
            targets["qkv"],
            targets["out"],
            named,
        )
        middle_ref[...] = middle
        writes = [pltpu.make_async_copy(a, b, sems.at[4 + n]) for n, (a, b) in enumerate(zip(saved, saved_at))]
        for write in writes:
            write.start()
        unit, _ = unit_of(middle)
        normed = (unit * spot(row_ref, "gain_b") + spot(row_ref, "shift_b")).astype(BF)
        total = middle + spot(row_ref, "down_b")
        up_ref, down_ref = targets["up"], targets["down"]
        arrived(up_ref, named["up"])
        arrived(down_ref, named["down"])
        for tile in range(4):
            columns = slice(tile * WIDTH, (tile + 1) * WIDTH)
            lifted = dot(normed, up_ref[:, columns], (1, 0))
            lifted = lifted + row_ref[:, UP_AT + tile * WIDTH : UP_AT + (tile + 1) * WIDTH]
            active, _ = gelu_pair(lifted)
            total = total + dot(active.astype(BF), down_ref[columns, :], (1, 0))
        top_ref[...] = total
        for write in writes:
            write.wait()

    return pl.pallas_call(
        body,
        out_shape=[
            jax.ShapeDtypeStruct((tokens, 3 * WIDTH), BF),
            jax.ShapeDtypeStruct((tokens, WIDTH), BF),
            jax.ShapeDtypeStruct((tokens, WIDTH), F32),
            jax.ShapeDtypeStruct((tokens, WIDTH), F32),
        ],
        in_specs=[WHOLE] * 4 + [ANY] * len(arrays),
        out_specs=[ANY] * 3 + [WHOLE],
        scratch_shapes=[pltpu.VMEM(SHAPES[name], BF) for name in names]
        + [pltpu.SemaphoreType.DMA((7,))]
        + [pltpu.VMEM((tokens, 3 * WIDTH), BF), pltpu.VMEM((tokens, WIDTH), BF), pltpu.VMEM((tokens, WIDTH), F32)],
        compiler_params=pltpu.CompilerParams(vmem_limit_bytes=50 * 2**20),
        cost_estimate=pl.CostEstimate(flops=1, bytes_accessed=1, transcendentals=1),
        name="layer_forward",
    )(hidden, row, docs.reshape(-1, 1), docs.reshape(1, -1), *arrays)


def send_rows(source, rows, columns, targets, half, first, sem):
    index = lax.axis_index("dp")
    core, chip = index % 2, index // 2
    for side, target in enumerate(targets):

        @pl.when(core == half ^ side)
        def _(target=target):
            for there, row in rows:
                pltpu.make_async_copy(
                    source.at[pl.ds(row, SLAB), columns],
                    target.at[chip ^ there, :, pl.ds(first, columns.size)],
                    sem,
                ).start()


def mlp_backward(hidden, grad_top, row, sources, docs=None):
    natural = any(source.natural and "down" in source.starts for source in sources)
    arrays = arrays_of(sources)
    tokens = hidden.shape[0]
    whole_layer = docs is not None
    names = ("up", "down", "qkv", "out") if whole_layer else ("up", "down")
    doc_operands = [docs.reshape(-1, 1), docs.reshape(1, -1)] if whole_layer else []

    def body(hidden_ref, grad_ref, row_ref, *rest):
        docs_refs, rest = rest[: len(doc_operands)], rest[len(doc_operands) :]
        refs, rest = rest[: len(arrays)], rest[len(arrays) :]
        grads_ref, (mid_ref, small_ref), rest = rest[:2], rest[2:4], rest[4:]
        if whole_layer:
            (packed_at, mixed_at, top_ref), (packed_ref, mixed_ref), rest = rest[:3], rest[-2:], rest[3:-2]
        targets, (up_stage, down_stage, sems) = dict(zip(names, rest[:-3])), rest[-3:]
        named = {name: sems.at[n] for n, name in enumerate(names)}
        up_sem, down_sem = sems.at[4], sems.at[5]
        up_ref, down_ref = targets["up"], targets["down"]
        start_fetch(sources, refs, targets, named)
        middle = hidden_ref[...]
        if whole_layer:
            middle = attn_steps(
                middle, row_ref, docs_refs, packed_ref, mixed_ref, targets["qkv"], targets["out"], named
            )
            writes = [
                pltpu.make_async_copy(packed_ref, packed_at, sems.at[6]),
                pltpu.make_async_copy(mixed_ref, mixed_at, sems.at[7]),
            ]
            for write in writes:
                write.start()
        unit, inverse = unit_of(middle)
        normed = unit * spot(row_ref, "gain_b") + spot(row_ref, "shift_b")
        normed_turned = normed.T.astype(BF)
        normed = normed.astype(BF)
        grad_top_rows = grad_ref[...].astype(F32)
        grad_down = grad_top_rows.astype(BF)
        small_ref[:, HIDDEN : HIDDEN + WIDTH] = jnp.sum(grad_down.astype(F32), axis=0, keepdims=True)
        grad_nb = jnp.zeros((tokens, WIDTH), F32)
        total = middle + spot(row_ref, "down_b") if whole_layer else None
        arrived(up_ref, named["up"])
        arrived(down_ref, named["down"])
        for tile in range(4):
            columns = slice(tile * WIDTH, (tile + 1) * WIDTH)
            lifted = dot(normed, up_ref[:, columns], (1, 0))
            lifted = lifted + row_ref[:, UP_AT + tile * WIDTH : UP_AT + (tile + 1) * WIDTH]
            active, slope = gelu_pair(lifted)
            active = active.astype(BF)
            if whole_layer:
                total = total + dot(active, down_ref[columns, :], (1, 0))
            grad_act = dot(grad_down, down_ref[columns, :], (1, 1))
            grad_lift = (grad_act * slope).astype(BF)
            small_ref[:, columns] = jnp.sum(grad_lift.astype(F32), axis=0, keepdims=True)
            grad_nb = grad_nb + dot(grad_lift, up_ref[:, columns], (1, 1))
            up_stage[:, columns] = dot(normed_turned, grad_lift, (1, 0)).astype(BF)
            down_stage[columns, :] = dot(active, grad_down, (0, 0)).astype(BF)
            send_rows(
                up_stage,
                [(there, there * SLAB) for there in range(16)],
                pl.ds(tile * WIDTH, WIDTH),
                grads_ref,
                tile // 2,
                tile % 2 * WIDTH,
                up_sem,
            )
            if natural:
                pieces = [(tile, [(there, tile * WIDTH + there * SLAB) for there in range(16)])]
            else:
                chips = range(4 * tile, 4 * tile + 4)
                pieces = [(b, [(there, there * 4 * SLAB + b * SLAB) for there in chips]) for b in range(4)]
            for half in range(2):
                for block, rows in pieces:
                    send_rows(
                        down_stage,
                        rows,
                        pl.ds(half * HALF, HALF),
                        grads_ref,
                        half,
                        4 * HALF + block * HALF,
                        down_sem,
                    )
        if whole_layer:
            top_ref[...] = total.astype(BF)
            for write in writes:
                write.wait()
        small_ref[:, HIDDEN + WIDTH : HIDDEN + 2 * WIDTH] = jnp.sum(grad_nb * unit, axis=0, keepdims=True)
        small_ref[:, HIDDEN + 2 * WIDTH :] = jnp.sum(grad_nb, axis=0, keepdims=True)
        mid_ref[...] = grad_top_rows + back_of_norm(grad_nb, unit, inverse, spot(row_ref, "gain_b"))
        arrived(up_stage, up_sem)
        arrived(down_stage, down_sem)

    outs = [jax.ShapeDtypeStruct((16, SLAB, HIDDEN), BF)] * 2 + [
        jax.ShapeDtypeStruct((tokens, WIDTH), F32),
        jax.ShapeDtypeStruct((1, HIDDEN + 3 * WIDTH), F32),
    ]
    if whole_layer:
        outs += [jax.ShapeDtypeStruct((tokens, count * WIDTH), BF) for count in (3, 1, 1)]
    return pl.pallas_call(
        body,
        out_shape=outs,
        in_specs=[WHOLE] * (3 + len(doc_operands)) + [ANY] * len(arrays),
        out_specs=[ANY] * 2 + [WHOLE] * 2 + ([ANY, ANY, WHOLE] if whole_layer else []),
        scratch_shapes=[pltpu.VMEM(SHAPES[name], BF) for name in names + ("up", "down")]
        + [pltpu.SemaphoreType.DMA((8,))]
        + ([pltpu.VMEM((tokens, 3 * WIDTH), BF), pltpu.VMEM((tokens, WIDTH), BF)] if whole_layer else []),
        compiler_params=pltpu.CompilerParams(vmem_limit_bytes=54 * 2**20),
        cost_estimate=pl.CostEstimate(flops=1, bytes_accessed=1, transcendentals=1),
        name="top_layer" if whole_layer else "mlp_backward",
    )(hidden, grad_top, row, *doc_operands, *arrays)


def attn_backward(hidden, grad_mid, packed, mixed, row, docs, sources, steps):
    arrays = arrays_of(sources)
    tokens = hidden.shape[0]
    scale = 1.0 / math.sqrt(HEAD_DIM)

    def body(hidden_at, packed_at, mixed_at, mid_ref, row_ref, down_docs, across_docs, *rest):
        if steps is not None:
            steps_ref, rest = rest[0], rest[1:]
        refs, rest = rest[: len(arrays)], rest[len(arrays) :]
        grads_ref, rest = rest[:2], rest[2:]
        in_ref, small_ref = rest[:2]
        qkv_ref, out_ref, qkv_stage, out_stage, gm_ref, gp_ref, sems = rest[2:9]
        hidden_ref, packed_ref, mixed_ref, rest = rest[9], rest[10], rest[11], rest[:9] + rest[12:]
        saved = [(hidden_at, hidden_ref), (mixed_at, mixed_ref), (packed_at, packed_ref)]
        saved = [pltpu.make_async_copy(*pair, sems.at[6 + n]) for n, pair in enumerate(saved)]
        for copy in saved:
            copy.start()
        named = {"qkv": sems.at[0], "out": sems.at[1]}
        start_fetch(sources, refs, {"qkv": qkv_ref, "out": out_ref}, named)
        grad_branch = mid_ref[...].astype(BF)
        small_ref[:, 2 * WIDTH : 3 * WIDTH] = jnp.sum(grad_branch.astype(F32), axis=0, keepdims=True)
        saved[1].wait()
        out_stage[...] = dot(mixed_ref[...], grad_branch, (0, 0)).astype(BF)
        chips = [(there, there * SLAB) for there in range(16)]
        for half in range(2):
            send_rows(out_stage, chips, pl.ds(half * HALF, HALF), grads_ref, half, 3 * HALF, sems.at[2])
        arrived(out_ref, named["out"])
        gm_ref[...] = dot(grad_branch, out_ref[...], (1, 1)).astype(BF)
        saved[0].wait()
        unit, inverse = unit_of(hidden_ref[...])
        normed = (unit * spot(row_ref, "gain_a") + spot(row_ref, "shift_a")).astype(BF)
        saved[2].wait()
        same = down_docs[...] == across_docs[...]
        first_head = head_lanes(tokens)

        def one_pair(pair, carry):
            query = packed_ref[:, pair_slice(pair, 0)]
            keys = packed_ref[:, pair_slice(pair, 1)]
            values = packed_ref[:, pair_slice(pair, 2)]
            grad_mixed = gm_ref[:, pair_slice(pair, 0)]
            blank = jnp.zeros_like(query)
            query_turned = query.astype(F32).T.astype(BF)
            mixed_turned = grad_mixed.astype(F32).T.astype(BF)
            by_query, by_key, by_value = [], [], []
            for head in range(2):
                rows_of = slice(head * HEAD_DIM, (head + 1) * HEAD_DIM)
                lanes = first_head if head == 0 else jnp.logical_not(first_head)
                probs = softmax_rows(jnp.where(lanes, query, blank), keys, same)
                low = probs.astype(BF)
                grad_probs = dot(jnp.where(lanes, grad_mixed, blank), values, (1, 1))
                grad_scores = probs * (grad_probs - jnp.sum(probs * grad_probs, axis=-1, keepdims=True))
                scores_low = grad_scores.astype(BF)
                by_query.append(dot(scores_low, keys, (1, 0)))
                by_key.append(dot(query_turned[rows_of], scores_low, (1, 0)))
                by_value.append(dot(mixed_turned[rows_of], low, (1, 0)))
            gp_ref[:, pair_slice(pair, 0)] = (jnp.where(first_head, *by_query) * scale).astype(BF)
            gp_ref[:, pair_slice(pair, 1)] = (jnp.concatenate(by_key, axis=0).T * scale).astype(BF)
            gp_ref[:, pair_slice(pair, 2)] = jnp.concatenate(by_value, axis=0).T.astype(BF)
            return carry

        lax.fori_loop(0, HEADS // 2, one_pair, 0, unroll=True)
        arrived(qkv_ref, named["qkv"])
        grad_na = jnp.zeros((tokens, WIDTH), F32)
        for block in range(3):
            columns = slice(block * WIDTH, (block + 1) * WIDTH)
            piece = gp_ref[:, columns]
            sums = jnp.sum(piece.astype(F32), axis=0, keepdims=True)
            if block != 1:
                small_ref[:, block // 2 * WIDTH : (block // 2 + 1) * WIDTH] = sums
            qkv_stage[:, columns] = dot(normed, piece, (0, 0)).astype(BF)
            grad_na = grad_na + dot(piece, qkv_ref[:, columns], (1, 1))
        for half in range(2):
            send_rows(qkv_stage, chips, pl.ds(half * 3 * HALF, 3 * HALF), grads_ref, half, 0, sems.at[3])
        small_ref[:, 3 * WIDTH : 4 * WIDTH] = jnp.sum(grad_na * unit, axis=0, keepdims=True)
        small_ref[:, 4 * WIDTH :] = jnp.sum(grad_na, axis=0, keepdims=True)
        grad_in = mid_ref[...] + back_of_norm(grad_na, unit, inverse, spot(row_ref, "gain_a"))
        in_ref[...] = grad_in
        if steps is not None:
            sums_ref, table_stages = rest[9], rest[10:]
            index = lax.axis_index("dp")
            core, chip = index % 2, index // 2
            for doc in range(8):
                sums_ref[doc : doc + 1, :] = (
                    jnp.sum(jnp.where(down_docs[...] == doc, grad_in, 0.0), axis=0, keepdims=True)
                    if doc < steps.shape[1]
                    else jnp.zeros((1, WIDTH), F32)
                )
            spots = [lax.broadcasted_iota(jnp.int32, (16, SLAB, 8), axis) for axis in range(2)]
            for side, half in enumerate((core, 1 - core)):
                sums = sums_ref[:, pl.ds(pl.multiple_of(half * HALF, HALF), HALF)].astype(BF)
                for owner in range(2):
                    line = ((chip ^ spots[0]) * 2 + owner) * 32 + spots[1]
                    line = jnp.where(spots[1] < 32, line, -1)
                    hot = jnp.where(line == steps_ref[...][None], 1.0, 0.0).reshape(16 * SLAB, 8).astype(BF)
                    block = dot(hot, sums, (1, 0)).astype(BF).reshape(16, SLAB, HALF)
                    stage = table_stages[side]
                    stage[:, :, owner * HALF : (owner + 1) * HALF] = block
                pltpu.make_async_copy(
                    table_stages[side], grads_ref[side].at[:, :, pl.ds(1536, 2 * HALF)], sems.at[4 + side]
                ).start()
            for side in range(2):
                arrived(table_stages[side], sems.at[4 + side])
        arrived(out_stage, sems.at[2])
        arrived(qkv_stage, sems.at[3])

    sums = [(16, SLAB, 1536 if steps is None else 2304)] * 2
    outs = [jax.ShapeDtypeStruct(shape, BF) for shape in sums] + [
        jax.ShapeDtypeStruct((tokens, WIDTH), F32),
        jax.ShapeDtypeStruct((1, 5 * WIDTH), F32),
    ]
    operands = [hidden, packed, mixed, grad_mid, row, docs.reshape(-1, 1), docs.reshape(1, -1)]
    scratch = [pltpu.VMEM(SHAPES["qkv"], BF), pltpu.VMEM(SHAPES["out"], BF)] * 2 + [
        pltpu.VMEM((tokens, WIDTH), BF),
        pltpu.VMEM((tokens, 3 * WIDTH), BF),
        pltpu.SemaphoreType.DMA((9,)),
        pltpu.VMEM((tokens, WIDTH), F32),
        pltpu.VMEM((tokens, 3 * WIDTH), BF),
        pltpu.VMEM((tokens, WIDTH), BF),
    ]
    if steps is not None:
        operands.append(jnp.pad(steps, ((0, 0), (0, 8 - steps.shape[1])), constant_values=-2))
        scratch += [pltpu.VMEM((8, WIDTH), F32)] + [pltpu.VMEM((16, SLAB, 2 * HALF), BF)] * 2
    return pl.pallas_call(
        body,
        out_shape=outs,
        in_specs=[ANY] * 3 + [WHOLE] * (len(operands) - 3) + [ANY] * len(arrays),
        out_specs=[ANY] * len(sums) + [WHOLE] * (len(outs) - len(sums)),
        scratch_shapes=scratch,
        compiler_params=pltpu.CompilerParams(vmem_limit_bytes=60 * 2**20),
        cost_estimate=pl.CostEstimate(flops=1, bytes_accessed=1, transcendentals=1),
        name="attn_backward",
    )(*operands, *arrays)


def lay_extra(source):
    def body(*rest):
        refs, (extra_ref, sems) = rest[: len(source.arrays)], rest[len(source.arrays) :]
        named = {"extra": sems.at[0]}
        start_fetch([source], refs, {"extra": extra_ref}, named)
        arrived(extra_ref, named["extra"])

    return pl.pallas_call(
        body,
        out_shape=jax.ShapeDtypeStruct(SHAPES["extra"], BF),
        in_specs=[ANY] * len(source.arrays),
        out_specs=WHOLE,
        scratch_shapes=[pltpu.SemaphoreType.DMA((1,))],
        compiler_params=pltpu.CompilerParams(vmem_limit_bytes=16 * 2**20),
        cost_estimate=pl.CostEstimate(flops=1, bytes_accessed=1, transcendentals=1),
        name="lay_extra",
    )(*source.arrays)


def is_middle():
    level = lax.axis_index("dp") // 8
    return (level == 1) | (level == 2)


def cut_of(value):
    return value.shape[-1] // 256 * 128


def chip_share(layer_weights, extra):
    core, _ = place()
    down = layer_weights.get("down")

    def halves(half):
        def columns(value):
            width = value.shape[1] // 2
            return value[:, half * width : half * width + width]

        narrow = [columns(layer_weights[name]) for name in ("qkv", "out", "up") if name in layer_weights]
        wide = []
        if down is not None:
            wide += [columns(down)[:SLAB], columns(down)[SLAB:]]
        if extra is not None:
            wide.append(columns(extra))
        parts = narrow
        if wide:
            wide = jnp.concatenate(wide, axis=1)
            parts = parts + [wide[:24], wide[24:]]
        return jnp.concatenate(parts, axis=1), sum(v.shape[1] for v in narrow)

    (left, count), (right, _) = halves(0), halves(1)
    kept = jnp.where(core == 0, left, right)
    came = swap(jnp.where(core == 0, right, left), CORE)
    lower = jnp.where(core == 0, kept, came)
    upper = jnp.where(core == 0, came, kept)
    columns = [jnp.concatenate([lower[:, :count], upper[:, :count]], axis=0)]
    wide = (lower.shape[1] - count) // 2
    if wide:
        low, high = [
            jnp.concatenate([v[:, count : count + wide], v[:, count + wide :]], axis=0) for v in (lower, upper)
        ]
        if down is not None:
            columns += [low[:, : 2 * HALF], high[:, : 2 * HALF]]
        if extra is not None:
            columns += [low[:, wide - HALF :], high[:, wide - HALF :]]
    return jnp.concatenate(columns, axis=1)


def line_second(first, third_middle):
    return swap_from(first, MIDDLE, (1, 2)), swap_from(third_middle, ALONG_Z, (1, 2))


def line_third(second_middle):
    return swap_from(second_middle, ALONG_Z, (1, 2))


def line_first(own):
    return swap(own, ALONG_Z), swap_from(own, MIDDLE, (1, 2))


def by_place(middle, end):
    return jnp.where(is_middle(), middle, end)


def along_each(to_x, to_y):
    return swap(to_x, ALONG_X), swap(to_y, ALONG_Y)


def diagonal(by_x, by_y):
    cut = cut_of(by_x)
    return swap(by_x[..., :cut], ALONG_Y), swap(by_y[..., cut:], ALONG_X)


def with_other_core(own, by_x, by_y, low, high, distances, first):
    sides = jnp.stack([own, by_x, by_y])
    across = jnp.concatenate([low, high], axis=-1)
    parts = []
    for array, steps in ((sides, (0, 1, 2)), (across, (3,))):
        if len(steps) > 1:
            entries = [((n, k), 4 * d + step) for n, step in enumerate(steps) for k, d in enumerate(distances)]
        else:
            entries = [((k,), 4 * d + 3) for k, d in enumerate(distances)]
        parts.append(Part(array, entries, first, True))
        parts.append(Part(swap(array, CORE), entries, first, False))
    return parts


def direct_line(levels):
    return [swap(levels[k], ALONG_Z * k) for k in (1, 2, 3)]


def half_line(levels):
    return swap(levels[2:], MIDDLE)


def line_end(levels, came):
    return swap(total(levels[1], came[0]).astype(BF), ALONG_Z)


def line_sum(levels, came, last):
    return total(levels[0], came[1], last)


def along_both(low, high):
    return swap(low, ALONG_Y), swap(high, ALONG_X)


def line_ends(levels):
    return [swap_from(levels[k], ALONG_Z, (0, 3)) for k in (3, 2)]


def line_middles(levels, ends):
    return [
        swap_from(total(levels[2], ends[0]).astype(BF), MIDDLE, (1, 2)),
        swap_from(total(levels[3], ends[1]).astype(BF), MIDDLE, (1, 2)),
    ]


def line_last(levels, middles):
    return swap(total(levels[1], middles[0]).astype(BF), ALONG_Z)


def total(*values):
    return sum(v.astype(F32) for v in values)


class PlaneSums:
    def __init__(self, *pairs):
        self.pairs = [[v.reshape(4, 4, SLAB, v.shape[-1]) for v in pair] for pair in pairs]
        self.columns = sum(pair[0].shape[-1] for pair in pairs)
        self.cut = self.columns // 256 * 128

    def pair(self, step, first=0, last=None):
        last = self.columns if last is None else last
        pieces = []
        begin = 0
        for pair in self.pairs:
            end = begin + pair[0].shape[-1]
            low, high = max(first, begin) - begin, min(last, end) - begin
            if low < high:
                pieces.append(total(*[v[:, step, :, low:high] for v in pair]))
            begin = end
        return pieces[0] if len(pieces) == 1 else jnp.concatenate(pieces, axis=-1)

    def diagonals(self):
        return self.pair(3, 0, self.cut).astype(BF), self.pair(3, self.cut).astype(BF)

    def sides(self, low, high):
        room = [(0, 0)] * 2
        low = jnp.pad(low, room + [(0, self.columns - self.cut)])
        high = jnp.pad(high, room + [(self.cut, 0)])
        return (self.pair(1) + low.astype(F32)).astype(BF), (self.pair(2) + high.astype(F32)).astype(BF)

    def levels(self, by_x, by_y):
        return (self.pair(0) + total(by_x, by_y)).astype(BF)


def by_half(core, mine, other, axis):
    return jnp.where(
        core == 0, jnp.concatenate([mine, other], axis=axis), jnp.concatenate([other, mine], axis=axis)
    )


def own_rows(names, share):
    core, _ = place()
    widths = {"qkv": 1152, "out": 384, "up": 1536, "down": 1536, "down_by_core": 1536, "extra": 768}
    pieces = []
    start = 0
    for name in names:
        piece = share[:, start : start + widths[name]]
        start += widths[name]
        if name in ("down", "extra"):
            m = widths[name] // 2
            mine, theirs = [lax.dynamic_slice_in_dim(piece, side * m, m, 1) for side in (core, 1 - core)]
            if name == "down":
                mine, theirs = [jnp.concatenate([v[:, :HALF], v[:, HALF:]], axis=0) for v in (mine, theirs)]
        else:
            mine, theirs = [lax.dynamic_slice_in_dim(piece, side * 24, 24, 0) for side in (core, 1 - core)]
        pieces.append((mine, theirs))
    sizes = [theirs.shape for _, theirs in pieces]
    packed = jnp.concatenate([theirs.astype(BF).reshape(24, -1) for _, theirs in pieces], axis=1)
    came = swap(packed, CORE)
    outs = []
    start = 0
    for (mine, _), (rows, columns) in zip(pieces, sizes):
        count = rows * columns // 24
        other = came[:, start : start + count].reshape(rows, columns).astype(F32)
        start += count
        outs.append((mine, other))
    for n, name in enumerate(names):
        if name == "down_by_core":
            outs[n] = [jnp.concatenate(jnp.split(v, 4, axis=1), axis=0) for v in outs[n]]
    return [by_half(core, mine, other, 1) for mine, other in outs]


def small_maps(layer):
    device = np.full(ROW_LENGTH, -1, np.int32)
    inner = np.full(ROW_LENGTH, -1, np.int32)

    def put(at, count, each, begin):
        spots = np.arange(count)
        device[at : at + count] = spots // each
        inner[at : at + count] = begin + spots % each

    for n, name in enumerate(WIDE_SMALLS):
        put(SPOTS[name], WIDTH, 24, 24 * n)
    put(BIAS_AT, 2 * WIDTH, 48, 144)
    for array in (device, inner):
        array[BIAS_AT + 2 * WIDTH : BIAS_AT + 3 * WIDTH] = array[BIAS_AT + WIDTH : BIAS_AT + 2 * WIDTH]
        array[BIAS_AT + WIDTH : BIAS_AT + 2 * WIDTH] = -1
    put(UP_AT, HIDDEN, 96, 192)
    if layer == 1:
        block, there, at = np.unravel_index(np.arange(HIDDEN), (4, TUNED, 24))
        device[UP_AT:], inner[UP_AT:] = there, 192 + 24 * block + at
    return device, inner


WIDE_SMALLS = ("out_b", "gain_a", "shift_a", "down_b", "gain_b", "shift_b")
GRAD_ORDER = ("up", "down_b", "gain_b", "shift_b", "query", "value", "out_b", "gain_a", "shift_a")


def grad_maps(layer):
    device, inner = small_maps(layer)
    pieces = {"up": (UP_AT, HIDDEN), "query": (BIAS_AT, WIDTH), "value": (BIAS_AT + 2 * WIDTH, WIDTH)}
    pieces.update({name: (at, WIDTH) for name, at in SPOTS.items()})
    order = np.concatenate([np.arange(at, at + count) for at, count in (pieces[name] for name in GRAD_ORDER)])
    return device[order], inner[order]


def spread_smalls(gathered, layer):
    device, inner = small_maps(layer)
    hot = (jnp.arange(HALF, dtype=jnp.int32)[:, None] == inner[None, :]).astype(BF)
    wide = jnp.dot(gathered, hot, preferred_element_type=F32)
    mine = jnp.arange(TUNED, dtype=jnp.int32)[:, None] == device[None, :]
    return jnp.sum(jnp.where(mine, wide, 0.0), axis=0, keepdims=True)


def collect_smalls(row, layer):
    device, inner = grad_maps(layer)
    mine = jnp.arange(TUNED, dtype=jnp.int32)[:, None] == device[None, :]
    masked = jnp.where(mine, row.astype(BF), jnp.zeros((), BF))
    hot = (inner[:, None] == jnp.arange(HALF, dtype=jnp.int32)[None, :]).astype(BF)
    return jnp.dot(masked, hot, preferred_element_type=F32).astype(BF)


gate = lax.optimization_barrier


def tuned(
    embedded,
    doc_ids,
    step_ids,
    step_table,
    qkv_weight,
    qv_bias,
    out_weight,
    out_bias,
    first_gain,
    first_shift,
    up_weight,
    up_bias,
    down_weight,
    down_bias,
    second_gain,
    second_shift,
    cotangent,
):
    core, chip = place()
    docs = doc_ids[0]
    doc_count = step_ids.shape[1]
    steps = step_ids[0]
    smalls = (out_bias, first_gain, first_shift, down_bias, second_gain, second_shift, qv_bias, up_bias)
    small_rows = jnp.pad(jnp.concatenate(smalls, axis=1), ((0, 0), (0, HALF - 288))).reshape(1, 2 * HALF)
    extra = jnp.concatenate([step_table, jnp.pad(small_rows, ((0, 15), (0, 0)))], axis=0)
    down_blocks = [down_weight[1][24 * b : 24 * b + 24] for b in range(4)]
    up_order = up_weight[1].reshape(24, TUNED, 4, 24).transpose(0, 2, 1, 3).reshape(24, HIDDEN)
    upper_share = jnp.concatenate([qkv_weight[1], out_weight[1], up_order] + down_blocks, axis=1)
    lower_share = chip_share(
        {"qkv": qkv_weight[0], "out": out_weight[0], "up": up_weight[0], "down": down_weight[0]}, extra
    )
    starts = {"qkv": 0, "out": 1152, "up": 1536, "down": 3072, "extra": 4608}
    upper_starts = {"qkv": 0, "out": 3 * WIDTH, "up": 4 * WIDTH, "down": 8 * WIDTH}
    upper = lax.all_gather(upper_share, "dp", axis=0, tiled=True)

    block1, block3_middle = line_first(lower_share)
    second_middle, second_end = line_second(block1, block3_middle)
    third_end = line_third(second_middle)
    blocks = [lower_share, block1, by_place(second_middle, second_end), by_place(block3_middle, third_end)]
    parts = []
    for distance, block in enumerate(blocks):
        by_x, by_y = along_each(block, block)
        plane = jnp.stack([block, by_x, by_y, jnp.concatenate(diagonal(by_x, by_y), axis=1)])
        entries = [((step,), 4 * distance + step, 0) for step in range(4)]
        parts += [Part(plane, entries, True), Part(swap(plane, CORE), entries, False)]
    source0, source1 = Source(parts, starts), Source(upper, upper_starts)

    all_extra = lay_extra(source0)
    small_all = all_extra[32::SLAB].reshape(16, 2, 2, HALF).transpose(1, 0, 2, 3).reshape(2, TUNED, HALF)
    rows = [spread_smalls(small_all[0], 0)]
    owner = steps // 32
    row_of = (owner // 2) * SLAB + steps % 32
    row_hot = (row_of[:, None] == jnp.arange(16 * SLAB, dtype=jnp.int32)[None, :]).astype(BF)
    both_rows = jnp.dot(row_hot, all_extra, preferred_element_type=F32).reshape(doc_count, 2, 2, HALF)
    doc_rows = jnp.where((owner % 2 == 0)[:, None, None], both_rows[:, :, 0], both_rows[:, :, 1])
    doc_rows = doc_rows.reshape(doc_count, WIDTH)
    of_doc = [(docs == s)[:, None] for s in range(doc_count)]
    start = embedded.astype(F32) + sum(jnp.where(of_doc[s], doc_rows[s][None], 0.0) for s in range(doc_count))

    packed0, mixed0, middle0, between = layer_forward(start, rows[0], docs, [source0])

    between, small_1 = gate((between, small_all[1]))
    rows.append(spread_smalls(small_1, 1))
    kept_m, sent_m, mid1, small_mlp1, packed1, mixed1, block_output = mlp_backward(
        between, cotangent, rows[1], [source1], docs
    )
    came_m = swap(sent_m, CORE)
    kept_t, sent_t, in1, small_attn1 = attn_backward(
        between, mid1, packed1, mixed1, rows[1], docs, [source1], None
    )
    in1, came_m, sent_t = gate((in1, came_m, sent_t))
    sums_m = PlaneSums((kept_m, came_m))
    in1, to_go, sent_t = gate((in1, sums_m.diagonals(), sent_t))
    low_m = along_both(*to_go)
    came_t = swap(sent_t, CORE)
    kept_b, sent_b, mid0, small_mlp0 = mlp_backward(middle0, in1, rows[0], [source0])
    mid0, low_m, came_t, sent_b = gate((mid0, low_m, came_t, sent_b))
    came_b = swap(sent_b, CORE)
    sums_t = PlaneSums((kept_t, came_t))
    low_t = along_both(*sums_t.diagonals())
    x_m = along_each(*sums_m.sides(*low_m))
    mid0, to_go, small_mlp1, small_attn1 = gate((mid0, sums_t.sides(*low_t), small_mlp1, small_attn1))
    x_t = along_each(*to_go)
    kept_c, sent_c, input_grad, small_attn0 = attn_backward(
        start, mid0, packed0, mixed0, rows[0], docs, [source0], step_ids
    )
    input_grad, came_b, kept_c, sent_c, small_attn0 = gate((input_grad, came_b, kept_c, sent_c, small_attn0))
    sums_b = PlaneSums((kept_b, came_b))
    small_grads = jnp.stack(
        [
            collect_smalls(jnp.concatenate([small_mlp0, small_attn0], axis=1), 0),
            collect_smalls(jnp.concatenate([small_mlp1, small_attn1], axis=1), 1),
        ]
    ).reshape(2, 16, 2 * HALF)
    small_grads = small_grads[:, chip ^ jnp.arange(16, dtype=jnp.int32)][:, :, None]
    small_grads = jnp.pad(small_grads, ((0, 0), (0, 0), (0, 15), (0, 0)))
    kept_c, sent_c = [
        lax.dynamic_update_slice(
            v, lax.dynamic_index_in_dim(small_grads, side, 0, keepdims=False), (0, 32, 1536)
        )
        for v, side in ((kept_c, core), (sent_c, 1 - core))
    ]
    x_m, x_t, to_go, kept_c, sent_c = gate((x_m, x_t, sums_b.diagonals(), kept_c, sent_c))

    low_b = along_both(*to_go)
    came_c = swap(sent_c, CORE)
    x_m, x_t, came_c = gate((x_m, x_t, came_c))
    sums_c = PlaneSums((kept_c, came_c))
    to_go = sums_c.diagonals()
    low_c = along_both(*to_go)
    levels_m = sums_m.levels(*x_m)
    half_m = half_line(levels_m)
    low_b, to_go = gate((low_b, to_go))
    x_b = along_each(*sums_b.sides(*low_b))
    low_c, half_m, x_t = gate((low_c, half_m, x_t))
    x_c = along_each(*sums_c.sides(*low_c))
    levels_t = sums_t.levels(*x_t)
    half_t = half_line(levels_t)
    levels_a = jnp.concatenate([levels_m, levels_t], axis=-1)
    half_a = jnp.concatenate([half_m, half_t], axis=-1)
    levels_b = sums_b.levels(*x_b)
    half_b = half_line(levels_b)
    x_c, levels_b = gate((x_c, levels_b))
    levels_c, half_a = gate((sums_c.levels(*x_c), half_a))
    back_c = [swap(levels_c[k], ALONG_Z * k) for k in (1, 2, 3)]
    last_a = line_end(levels_a, half_a)
    up_1, down_1, qkv_1, out_1 = own_rows(
        ("up", "down_by_core", "qkv", "out"), line_sum(levels_a, half_a, last_a)
    )
    up_1 = up_1.reshape(24, 4, TUNED, 24).transpose(0, 2, 1, 3).reshape(24, HIDDEN)
    half_b, back_c, up_1, down_1, qkv_1, out_1 = gate((half_b, back_c, up_1, down_1, qkv_1, out_1))
    last_b = line_end(levels_b, half_b)
    qkv_0, out_0, extra_0 = own_rows(("qkv", "out", "extra"), total(levels_c[0], *back_c))
    up_0, down_0 = own_rows(("up", "down"), line_sum(levels_b, half_b, last_b))
    up, down = jnp.stack([up_0, up_1]), jnp.stack([down_0, down_1])
    small_out = extra_0[32].reshape(2, HALF)
    out_b, gain_a, shift_a, down_b, gain_b, shift_b = [small_out[:, n * 24 : n * 24 + 24] for n in range(6)]
    return (
        block_output,
        input_grad,
        extra_0[:32],
        jnp.stack([qkv_0, qkv_1]),
        small_out[:, 144:192],
        jnp.stack([out_0, out_1]),
        out_b,
        gain_a,
        shift_a,
        up,
        small_out[:, 192:288],
        down,
        down_b,
        gain_b,
        shift_b,
    )


def shortened(value):
    return jax.tree.map(lambda a: a.astype(jnp.bfloat16) if a.dtype == jnp.float32 else a, value)


def partner(value, axis, stride):
    return lax.ppermute(value, axis, [(i, i ^ 1 << stride) for i in range(lax.axis_size(axis))])


def norm_rows(hidden, gain_vec, shift_vec):
    average = jnp.mean(hidden, axis=-1, keepdims=True)
    centred = hidden - average
    variance = jnp.mean(centred * centred, axis=-1, keepdims=True)
    inverse = lax.rsqrt(variance + EPSILON)
    unit_rows = centred * inverse
    normed = unit_rows * gain_vec.astype(jnp.float32) + shift_vec.astype(jnp.float32)
    return (normed, unit_rows, inverse)


def norm_back(grad_rows, unit_rows, inverse, gain_vec):
    scaled = grad_rows * gain_vec.astype(jnp.float32)
    first_mean = jnp.mean(scaled, axis=-1, keepdims=True)
    second_mean = jnp.mean(scaled * unit_rows, axis=-1, keepdims=True)
    return inverse * (scaled - first_mean - unit_rows * second_mean)


def smooth_gate(lifted):
    return jax.nn.gelu(lifted, approximate=True)


def halving_sum(members, send_fn):
    levels = lax.axis_size("dp").bit_length() - 1
    position = lax.axis_index("dp")
    current = tuple(members)
    for level in range(levels - 1, -1, -1):
        upper_side = position // (1 << level) % 2 == 1
        kept_list = []
        sent_list = []
        for member in current:
            half = member.shape[0] // 2
            lower_part = member[:half]
            upper_part = member[half:]
            kept_list.append(jnp.where(upper_side, upper_part, lower_part))
            sent_list.append(jnp.where(upper_side, lower_part, upper_part))
        received = send_fn(tuple(sent_list), level)
        current = tuple((kept + came for kept, came in zip(kept_list, received)))
    return current


def layer_apply(hidden, params, same_doc):
    qkv_w, qv_b, out_w, out_b, gain_a, shift_a, up_w, up_b, down_w, down_b, gain_b, shift_b = params
    width = out_w.shape[0]
    tok_count = hidden.shape[0]
    scale = 1.0 / math.sqrt(HEAD_DIM)
    normed_a, unit_a, inverse_a = norm_rows(hidden, gain_a, shift_a)
    normed_a = normed_a.astype(jnp.bfloat16)
    qv_float = qv_b.astype(jnp.float32)
    bias_full = jnp.concatenate(
        [qv_float[:width], jnp.zeros((width,), jnp.float32), qv_float[width:]]
    )
    packed = (jnp.dot(normed_a, qkv_w, preferred_element_type=jnp.float32) + bias_full).astype(
        jnp.bfloat16
    )
    queries = packed[:, :width].reshape(tok_count, HEADS, HEAD_DIM)
    key_rows = packed[:, width : 2 * width].reshape(tok_count, HEADS, HEAD_DIM)
    value_rows = packed[:, 2 * width :].reshape(tok_count, HEADS, HEAD_DIM)
    scores = (
        jnp.einsum("qhd,khd->hqk", queries, key_rows, preferred_element_type=jnp.float32) * scale
    )
    masked = jnp.where(same_doc[None], scores, -1e30)
    top_score = jnp.max(masked, axis=-1, keepdims=True)
    expo_rows = jnp.exp(masked - top_score)
    probs = expo_rows / jnp.sum(expo_rows, axis=-1, keepdims=True)
    probs_low = probs.astype(jnp.bfloat16)
    mixed = jnp.einsum("hqk,khd->qhd", probs_low, value_rows, preferred_element_type=jnp.float32)
    mixed = mixed.reshape(tok_count, width).astype(jnp.bfloat16)
    middle = (
        hidden
        + jnp.dot(mixed, out_w, preferred_element_type=jnp.float32)
        + out_b.astype(jnp.float32)
    )
    normed_b, unit_b, inverse_b = norm_rows(middle, gain_b, shift_b)
    normed_b = normed_b.astype(jnp.bfloat16)
    lifted = jnp.dot(normed_b, up_w, preferred_element_type=jnp.float32) + up_b.astype(jnp.float32)
    activated = smooth_gate(lifted).astype(jnp.bfloat16)
    output = (
        middle
        + jnp.dot(activated, down_w, preferred_element_type=jnp.float32)
        + down_b.astype(jnp.float32)
    )
    saved = (
        unit_a,
        inverse_a,
        normed_a,
        queries,
        key_rows,
        value_rows,
        probs,
        probs_low,
        mixed,
        unit_b,
        inverse_b,
        normed_b,
        lifted,
        activated,
    )
    return (output, saved)


def layer_back(hidden, params, same_doc, grad_top):
    qkv_w, qv_b, out_w, out_b, gain_a, shift_a, up_w, up_b, down_w, down_b, gain_b, shift_b = params
    unused_output, saved = layer_apply(hidden, params, same_doc)
    (
        unit_a,
        inverse_a,
        normed_a,
        queries,
        key_rows,
        value_rows,
        probs,
        probs_low,
        mixed,
        unit_b,
        inverse_b,
        normed_b,
        lifted,
        activated,
    ) = saved
    width = out_w.shape[0]
    tok_count = hidden.shape[0]
    scale = 1.0 / math.sqrt(HEAD_DIM)
    grad_down = grad_top.astype(jnp.bfloat16)
    down_b_grad = jnp.sum(grad_down.astype(jnp.float32), axis=0)
    down_w_grad = jnp.einsum("tf,td->fd", activated, grad_down, preferred_element_type=jnp.float32)
    grad_act = jnp.einsum("td,fd->tf", grad_down, down_w, preferred_element_type=jnp.float32)
    unused_gate, gate_pull = jax.vjp(smooth_gate, lifted)
    grad_lift = gate_pull(grad_act)[0].astype(jnp.bfloat16)
    up_b_grad = jnp.sum(grad_lift.astype(jnp.float32), axis=0)
    up_w_grad = jnp.einsum("td,tf->df", normed_b, grad_lift, preferred_element_type=jnp.float32)
    grad_nb = jnp.einsum("tf,df->td", grad_lift, up_w, preferred_element_type=jnp.float32)
    gain_b_grad = jnp.sum(grad_nb * unit_b, axis=0)
    shift_b_grad = jnp.sum(grad_nb, axis=0)
    grad_mid = grad_top + norm_back(grad_nb, unit_b, inverse_b, gain_b)
    grad_branch = grad_mid.astype(jnp.bfloat16)
    out_b_grad = jnp.sum(grad_branch.astype(jnp.float32), axis=0)
    out_w_grad = jnp.einsum("te,td->ed", mixed, grad_branch, preferred_element_type=jnp.float32)
    grad_mixed = jnp.einsum("td,ed->te", grad_branch, out_w, preferred_element_type=jnp.float32)
    grad_mixed = grad_mixed.astype(jnp.bfloat16).reshape(tok_count, HEADS, HEAD_DIM)
    grad_probs = jnp.einsum(
        "qhd,khd->hqk", grad_mixed, value_rows, preferred_element_type=jnp.float32
    )
    grad_values = jnp.einsum(
        "hqk,qhd->khd", probs_low, grad_mixed, preferred_element_type=jnp.float32
    )
    grad_scores = probs * (grad_probs - jnp.sum(probs * grad_probs, axis=-1, keepdims=True))
    scores_low = grad_scores.astype(jnp.bfloat16)
    grad_queries = (
        jnp.einsum("hqk,khd->qhd", scores_low, key_rows, preferred_element_type=jnp.float32) * scale
    )
    grad_keys = (
        jnp.einsum("hqk,qhd->khd", scores_low, queries, preferred_element_type=jnp.float32) * scale
    )
    grad_packed = jnp.concatenate(
        [
            grad_queries.reshape(tok_count, width),
            grad_keys.reshape(tok_count, width),
            grad_values.reshape(tok_count, width),
        ],
        axis=1,
    ).astype(jnp.bfloat16)
    packed_sums = jnp.sum(grad_packed.astype(jnp.float32), axis=0)
    qv_b_grad = jnp.concatenate([packed_sums[:width], packed_sums[2 * width :]])
    qkv_w_grad = jnp.einsum("td,te->de", normed_a, grad_packed, preferred_element_type=jnp.float32)
    grad_na = jnp.einsum("te,de->td", grad_packed, qkv_w, preferred_element_type=jnp.float32)
    gain_a_grad = jnp.sum(grad_na * unit_a, axis=0)
    shift_a_grad = jnp.sum(grad_na, axis=0)
    grad_in = grad_mid + norm_back(grad_na, unit_a, inverse_a, gain_a)
    grads = (
        qkv_w_grad,
        qv_b_grad,
        out_w_grad,
        out_b_grad,
        gain_a_grad,
        shift_a_grad,
        up_w_grad,
        up_b_grad,
        down_w_grad,
        down_b_grad,
        gain_b_grad,
        shift_b_grad,
    )
    return (grad_in, grads)


def plain(
    embedded,
    doc_ids,
    step_ids,
    step_table,
    qkv_weight,
    qv_bias,
    out_weight,
    out_bias,
    first_gain,
    first_shift,
    up_weight,
    up_bias,
    down_weight,
    down_bias,
    second_gain,
    second_shift,
    cotangent,
):
    docs_row = doc_ids[0]
    same_doc = docs_row[:, None] == docs_row[None, :]
    doc_count = step_ids.shape[1]
    doc_hot = (docs_row[:, None] == jnp.arange(doc_count, dtype=jnp.int32)[None, :]).astype(
        jnp.float32
    )
    gathered_first = (
        lax.all_gather(qkv_weight[0], "dp", axis=0, tiled=True),
        lax.all_gather(qv_bias[0], "dp", axis=0, tiled=True),
        lax.all_gather(out_weight[0], "dp", axis=0, tiled=True),
        lax.all_gather(out_bias[0], "dp", axis=0, tiled=True),
        lax.all_gather(first_gain[0], "dp", axis=0, tiled=True),
        lax.all_gather(first_shift[0], "dp", axis=0, tiled=True),
        lax.all_gather(up_weight[0], "dp", axis=0, tiled=True),
        lax.all_gather(up_bias[0], "dp", axis=0, tiled=True),
        lax.all_gather(down_weight[0], "dp", axis=0, tiled=True),
        lax.all_gather(down_bias[0], "dp", axis=0, tiled=True),
        lax.all_gather(second_gain[0], "dp", axis=0, tiled=True),
        lax.all_gather(second_shift[0], "dp", axis=0, tiled=True),
        lax.all_gather(step_table, "dp", axis=0, tiled=True),
    )
    params_lower = gathered_first[:12]
    table_whole = gathered_first[12]
    step_hot = step_ids[0][:, None] == jnp.arange(table_whole.shape[0], dtype=jnp.int32)[None, :]
    doc_rows = jnp.dot(
        step_hot.astype(jnp.bfloat16), table_whole, preferred_element_type=jnp.float32
    )
    start = embedded.astype(jnp.float32) + jnp.dot(
        doc_hot, doc_rows, precision=lax.Precision.HIGHEST
    )
    middle_hidden, unused_lower = layer_apply(start, params_lower, same_doc)
    params_upper = (
        lax.all_gather(qkv_weight[1], "dp", axis=0, tiled=True),
        lax.all_gather(qv_bias[1], "dp", axis=0, tiled=True),
        lax.all_gather(out_weight[1], "dp", axis=0, tiled=True),
        lax.all_gather(out_bias[1], "dp", axis=0, tiled=True),
        lax.all_gather(first_gain[1], "dp", axis=0, tiled=True),
        lax.all_gather(first_shift[1], "dp", axis=0, tiled=True),
        lax.all_gather(up_weight[1], "dp", axis=0, tiled=True),
        lax.all_gather(up_bias[1], "dp", axis=0, tiled=True),
        lax.all_gather(down_weight[1], "dp", axis=0, tiled=True),
        lax.all_gather(down_bias[1], "dp", axis=0, tiled=True),
        lax.all_gather(second_gain[1], "dp", axis=0, tiled=True),
        lax.all_gather(second_shift[1], "dp", axis=0, tiled=True),
    )
    final_hidden, unused_upper = layer_apply(middle_hidden, params_upper, same_doc)
    block_output = final_hidden.astype(jnp.bfloat16)

    def weights_for(layer_index):
        return (
            lax.all_gather(qkv_weight[layer_index], "dp", axis=0, tiled=True),
            lax.all_gather(qv_bias[layer_index], "dp", axis=0, tiled=True),
            lax.all_gather(out_weight[layer_index], "dp", axis=0, tiled=True),
            lax.all_gather(out_bias[layer_index], "dp", axis=0, tiled=True),
            lax.all_gather(first_gain[layer_index], "dp", axis=0, tiled=True),
            lax.all_gather(first_shift[layer_index], "dp", axis=0, tiled=True),
            lax.all_gather(up_weight[layer_index], "dp", axis=0, tiled=True),
            lax.all_gather(up_bias[layer_index], "dp", axis=0, tiled=True),
            lax.all_gather(down_weight[layer_index], "dp", axis=0, tiled=True),
            lax.all_gather(down_bias[layer_index], "dp", axis=0, tiled=True),
            lax.all_gather(second_gain[layer_index], "dp", axis=0, tiled=True),
            lax.all_gather(second_shift[layer_index], "dp", axis=0, tiled=True),
        )

    grad_upper_in, upper_grads = layer_back(
        middle_hidden, weights_for(1), same_doc, cotangent.astype(jnp.float32)
    )

    def send_upper(sent, level):
        return jax.tree.map(
            lambda part, own: part.astype(own.dtype), partner(shortened(sent), "dp", level), sent
        )

    upper_shards = halving_sum(upper_grads, send_upper)
    input_grad, lower_grads = layer_back(start, weights_for(0), same_doc, grad_upper_in)
    doc_grads = jnp.einsum("ts,td->sd", doc_hot, input_grad, precision=lax.Precision.HIGHEST)
    table_full_grad = jnp.einsum(
        "sn,sd->nd", step_hot.astype(jnp.float32), doc_grads, precision=lax.Precision.HIGHEST
    )

    def send_lower(sent, level):
        return jax.tree.map(
            lambda part, own: part.astype(own.dtype), partner(shortened(sent), "dp", level), sent
        )

    lower_all = halving_sum(tuple(lower_grads) + (table_full_grad,), send_lower)
    lower_shards = lower_all[:12]
    table_shard = lower_all[12]
    stacked = [jnp.stack([lower_shards[index], upper_shards[index]], axis=0) for index in range(12)]
    return (
        block_output,
        input_grad,
        table_shard,
        stacked[0],
        stacked[1],
        stacked[2],
        stacked[3],
        stacked[4],
        stacked[5],
        stacked[6],
        stacked[7],
        stacked[8],
        stacked[9],
        stacked[10],
        stacked[11],
    )


def solution(mesh):
    local = tuned if mesh.shape["dp"] == TUNED else plain
    in_specs = (
        P("dp", None),
        P("dp", None),
        P("dp", None),
        P("dp", None),
        P(None, "dp", None),
        P(None, "dp"),
        P(None, "dp", None),
        P(None, "dp"),
        P(None, "dp"),
        P(None, "dp"),
        P(None, "dp", None),
        P(None, "dp"),
        P(None, "dp", None),
        P(None, "dp"),
        P(None, "dp"),
        P(None, "dp"),
        P("dp", None),
    )
    out_specs = (
        P("dp", None),
        P("dp", None),
        P("dp", None),
        P(None, "dp", None),
        P(None, "dp"),
        P(None, "dp", None),
        P(None, "dp"),
        P(None, "dp"),
        P(None, "dp"),
        P(None, "dp", None),
        P(None, "dp"),
        P(None, "dp", None),
        P(None, "dp"),
        P(None, "dp"),
        P(None, "dp"),
    )
    return jax.shard_map(local, mesh=mesh, in_specs=in_specs, out_specs=out_specs, check_vma=False)
```
